1024 devices in a mesh: tm: 8 (over z), gy: 16 (over x_hi, y), gz: 8 (over x_lo, core).
Axes of the slice: x: 8 (x_hi: 2, x_lo: 4; x = x_hi * 4 + x_lo), y: 8, z: 8, core: 2. Of those that a mesh axis runs over, the one named last changes fastest.
Arguments:
- iterate: float32 [8, 2, 4, 1024, 1024], P('tm', None, None, 'gy', 'gz'), may hold values from 0 to 1, as said below
- rates: float32 [2, 4, 1024, 1024], P(None, None, 'gy', 'gz'), may hold values from 0.02 to 0.3
Outputs:
- end_states: float32 [8, 2, 4, 1024, 1024], P('tm', None, None, 'gy', 'gz')
The draws below stay inside these ranges and needn't reach their ends.
Inputs may be any that keep to these rules, and one draw needn't show every extreme that they name: `iterate`: species 0 lies within 0.4 to 1 and species 1 within 0 to 0.5.
All inputs are finite; a program needn't handle non-finite values.
Results may differ from the reference program's by a relative error of at most 0.00002.
Values sent between devices are 32-bit elements; how exact they have to be, the bound alone decides.
No kernel may reach another device: no remote copies, remote signals or barrier semaphores. Data moves between devices by JAX's collectives and lax.ppermute only.
A program may use at most 32 MiB of HBM per device.

```python
import math
import jax
import jax.numpy as jnp
from jax import lax

CX = 4
ITERS = 2
FINE = 4
SLICES = 8
NY = 1024
NZ = 1024


def draw_iterate(key, part):
    key = jax.random.fold_in(key, 11)
    first_key, second_key = jax.random.split(key)
    shape = (SLICES, 1, CX, NY, NZ)
    first_unit = jax.random.uniform(first_key, shape, jnp.float32)
    second_unit = jax.random.uniform(second_key, shape, jnp.float32)
    substrate = 0.4 + 0.6 * first_unit
    catalyst = 0.5 * second_unit
    return jnp.concatenate([substrate, catalyst], axis=1)


def level_of(stream_key, extent, cuts, low, top_value):
    loudness, own = 1.0, jax.random.fold_in(stream_key, 6)
    for position, blocks in cuts:
        heights = jnp.exp(jax.random.uniform(jax.random.fold_in(own, position), (blocks,), jnp.float32, low / len(cuts), top_value / len(cuts)))
        loudness = loudness * jnp.repeat(heights, extent[position] // blocks).reshape([-1 if axis == position else 1 for axis in range(len(extent))])
    return loudness


def setup_inputs(seed: int = 0) -> dict:
    key_of = jax.random.split(jax.random.key(seed), 3)
    iterate = draw_iterate(jax.random.fold_in(key_of[2], 71), 0)
    rates = jnp.clip(jnp.exp(math.log(0.3) - 2.7080503 * jax.random.uniform(key_of[1], (2, CX, NY, NZ), jnp.float32) ** level_of(key_of[1], (2, CX, NY, NZ), ((2, 16), (3, 8)), -0.2, 0.2)), 0.02, 0.3)
    return {"iterate": iterate, "rates": rates}


spread_fast = 0.2
spread_slow = 0.1
fine_step = 0.125
coarse_step = 0.5


def laplace(state):
    walled = jnp.pad(state, ((0, 0), (1, 1), (0, 0), (0, 0)), mode="edge")
    along_x = walled[:, :-2] + walled[:, 2:]
    along_y = jnp.roll(state, 1, 2) + jnp.roll(state, -1, 2)
    along_z = jnp.roll(state, 1, 3) + jnp.roll(state, -1, 3)
    return (along_x + along_y) + along_z - 6.0 * state


def react(state, spread, rates, length):
    substrate = state[0]
    catalyst = state[1]
    feed = rates[0]
    kill = rates[1]
    product = substrate * catalyst * catalyst
    change_a = spread_fast * spread[0] - product + feed * (1.0 - substrate)
    change_b = spread_slow * spread[1] + product - (feed + kill) * catalyst
    return jnp.stack([substrate + length * change_a, catalyst + length * change_b])


def advance(state, rates, length):
    return react(state, laplace(state), rates, length)


def reference(iterate, rates):
    starts = iterate
    end_states = iterate
    for iteration in range(ITERS):
        def fine_run(state):
            for substep in range(FINE):
                state = advance(state, rates, fine_step)
            return state

        fine_ends = lax.map(fine_run, starts)
        coarse_old = lax.map(lambda state: advance(state, rates, coarse_step), starts)
        difference = fine_ends - coarse_old

        def turn(start, term):
            end_state = advance(start, rates, coarse_step) + term
            return end_state, end_state

        last_state, end_states = lax.scan(turn, starts[0], difference)
        starts = jnp.concatenate([starts[:1], end_states[:-1]], axis=0)
    return end_states
```

```python
import jax
import jax.numpy as jnp
from jax import lax
from jax.experimental import pallas as pl
from jax.experimental.pallas import tpu as pltpu
from jax.sharding import PartitionSpec as P

FINE = 4
SLICES = 8
HALO = 16
SUB = 32
WIN = SUB + 2 * HALO
ROWS = 64
LANES = 128
EXT = ROWS + 2 * HALO
TILES = EXT // 8

spread_fast = 0.2
spread_slow = 0.1
fine_step = 0.125
coarse_step = 0.5

PAIRS = ((0, 3), (1, 2))


def lane_index():
    return lax.broadcasted_iota(jnp.int32, (8, LANES), 1)


def roll(block, shift, axis):
    shift = shift % block.shape[axis]
    return block if shift == 0 else pltpu.roll(block, shift, axis)


def ext_tile(low, own, high, index):
    if index < 2:
        return low[8 * index : 8 * index + 8, :]
    if index < 10:
        return own[8 * (index - 2) : 8 * (index - 2) + 8, :]
    return high[8 * (index - 10) : 8 * (index - 10) + 8, :]


def strips_kernel(state, rates, low, high, to_low, to_high):
    lane = lane_index()
    for which, source in enumerate((state, rates)):
        for tile in range(TILES):
            first = jnp.zeros((8, LANES), jnp.float32)
            last = jnp.zeros((8, LANES), jnp.float32)
            for k in range(8):
                c, x = k // 4, k % 4
                rows = ext_tile(low.at[which, c, x], source.at[c, x], high.at[which, c, x], tile)
                here = (lane >= 16 * k) & (lane < 16 * k + 16)
                first = jnp.where(here, roll(rows, 16 * k, 1), first)
                last = jnp.where(here, roll(rows, 16 * k + 16, 1), last)
            to_low[which, 8 * tile : 8 * tile + 8, :] = first
            to_high[which, 8 * tile : 8 * tile + 8, :] = last


def windows_of(low, own, high, left, right, tile, c, pair, tz, lane):
    parts = []
    for half, x in enumerate(PAIRS[pair]):
        rows = ext_tile(low.at[c, x], own.at[c, x], high.at[c, x], tile)
        parts.append(roll(rows, 64 * half - (SUB * tz - HALO), 1))
    block = jnp.where(lane < 64, parts[0], parts[1])
    if tz in (0, 3):
        edge = left if tz == 0 else right
        at = 0 if tz == 0 else 48
        strip = edge[8 * tile : 8 * tile + 8, :]
        for half, x in enumerate(PAIRS[pair]):
            k = 4 * c + x
            begin = 64 * half + at
            here = (lane >= begin) & (lane < begin + 16)
            block = jnp.where(here, roll(strip, begin - 16 * k, 1), block)
    return block


def windows_kernel(me, state, rates, low, high, left, right, windows, rates_here):
    lane = lane_index()
    my_y = me[0] // 4
    my_z = me[0] % 4
    for tz in range(4):
        for c in range(2):
            for pair in range(2):
                for tile in range(TILES):
                    block = windows_of(
                        low.at[0], state, high.at[0], left.at[0], right.at[0], tile, c, pair, tz, lane
                    )
                    for ty in range(2):
                        at = tile - 4 * ty
                        if 0 <= at < 8:
                            windows[4 * ty + tz, c, pair, 8 * at : 8 * at + 8, :] = block

    for mine in range(4):

        @pl.when(my_z == mine)
        def _():
            for c in range(2):
                for pair in range(2):
                    blocks = [
                        windows_of(
                            low.at[1], rates, high.at[1], left.at[1], right.at[1], tile, c, pair, mine, lane
                        )
                        for tile in range(TILES)
                    ]
                    for at in range(8):
                        block = jnp.where(my_y == 0, blocks[at], blocks[at + 4])
                        rates_here[c, pair, 8 * at : 8 * at + 8, :] = block


def load_state(ref):
    return [[[ref[c, p, j] for j in range(8)] for p in range(2)] for c in range(2)]


def save_state(ref, state):
    for c in range(2):
        for p in range(2):
            for j in range(8):
                ref[c, p, j] = state[c][p][j]


def neighbours(s, p, j, other):
    here = s[j]
    if p == 0:
        along_x = here + other[j]
    else:
        along_x = other[j] + roll(here, 64, 1)
    before = s[j - 1] if j > 0 else roll(s[7], 1, 0)
    after = s[j + 1] if j < 7 else roll(s[0], -1, 0)
    along_z = roll(here, 1, 1) + roll(here, -1, 1)
    return (along_x + (before + after)) + along_z


def step(state, coefs, which, length):
    a, b = state
    new_a = [[None] * 8, [None] * 8]
    new_b = [[None] * 8, [None] * 8]
    for p in range(2):
        for j in range(8):
            here_a, here_b = a[p][j], b[p][j]
            product = length * (here_a * here_b * here_b)
            near_a = neighbours(a[p], p, j, a[1 - p])
            near_b = neighbours(b[p], p, j, b[1 - p])
            keep_a = coefs[which, 0, p, j]
            gain = coefs[which, 1, p, j]
            keep_b = coefs[which, 2, p, j]
            new_a[p][j] = here_a * keep_a + (length * spread_fast) * near_a + (gain - product)
            new_b[p][j] = here_b * keep_b + (length * spread_slow) * near_b + product
    return [new_a, new_b]


def combine(op, left, right):
    return [[[op(left[c][p][j], right[c][p][j]) for j in range(8)] for p in range(2)] for c in range(2)]


def add(left, right):
    return combine(lambda l, r: l + r, left, right)


def subtract(left, right):
    return combine(lambda l, r: l - r, left, right)


def sweep_kernel(windows, rates, out, coefs, starts, terms, coarse_ends, rows):
    lane = lane_index()
    for which, length in enumerate((fine_step, coarse_step)):
        for p in range(2):
            for j in range(8):
                feed = rates[0, p, pl.ds(j, 8, stride=8), :]
                kill = rates[1, p, pl.ds(j, 8, stride=8), :]
                coefs[which, 0, p, j] = (1.0 - 6.0 * spread_fast * length) - length * feed
                coefs[which, 1, p, j] = length * feed
                coefs[which, 2, p, j] = (1.0 - 6.0 * spread_slow * length) - length * (feed + kill)

    def fine(state):
        for _ in range(FINE):
            state = step(state, coefs, 0, fine_step)
        return state

    def coarse(state):
        return step(state, coefs, 1, coarse_step)

    def first(n, carry):
        state = [
            [[windows[n, c, p, pl.ds(j, 8, stride=8), :] for j in range(8)] for p in range(2)]
            for c in range(2)
        ]
        save_state(starts.at[n], state)
        save_state(coarse_ends.at[n], coarse(state))
        end = fine(load_state(starts.at[n]))
        save_state(terms.at[n], subtract(end, load_state(coarse_ends.at[n])))
        return carry

    lax.fori_loop(0, SLICES - 1, first, 0)

    save_state(starts.at[1], add(load_state(coarse_ends.at[0]), load_state(terms.at[0])))

    def first_sweep(n, carry):
        end = coarse(load_state(starts.at[n]))
        save_state(coarse_ends.at[n], end)
        save_state(starts.at[n + 1], add(end, load_state(terms.at[n])))
        return carry

    lax.fori_loop(1, SLICES - 1, first_sweep, 0)
    save_state(coarse_ends.at[SLICES - 1], coarse(load_state(starts.at[SLICES - 1])))

    def second(n, carry):
        end = fine(load_state(starts.at[n]))
        save_state(terms.at[n], subtract(end, load_state(coarse_ends.at[n])))
        return carry

    lax.fori_loop(1, SLICES, second, 0)

    def put(n, state):
        for c in range(2):
            for j in range(8):
                outer, inner = state[c][0][j], state[c][1][j]
                low = jnp.where(lane < 32, roll(outer, -16, 1), roll(inner, 16, 1))
                high = jnp.where(lane < 96, roll(inner, -16, 1), roll(outer, 16, 1))
                rows[c, pl.ds(j, 8, stride=8), :] = jnp.where(lane < 64, low, high)
            out[n, c] = rows[c, HALO : HALO + SUB, :]

    put(0, load_state(starts.at[1]))
    state = add(load_state(coarse_ends.at[1]), load_state(terms.at[1]))
    put(1, state)
    save_state(starts.at[1], state)

    def second_sweep(n, carry):
        state = add(coarse(load_state(starts.at[n - 1])), load_state(terms.at[n]))
        put(n, state)
        save_state(starts.at[n], state)
        return carry

    lax.fori_loop(2, SLICES, second_sweep, 0)


def merge_kernel(parts, out):
    lane = lane_index()
    for c in range(2):
        for x in range(4):
            for ty in range(2):
                for r in range(4):
                    blocks = [
                        roll(parts[4 * ty + tz, c, 8 * r : 8 * r + 8, :], SUB * (tz - x), 1) for tz in range(4)
                    ]
                    low = jnp.where(lane < 32, blocks[0], blocks[1])
                    high = jnp.where(lane < 96, blocks[2], blocks[3])
                    at = SUB * ty + 8 * r
                    out[c, x, at : at + 8, :] = jnp.where(lane < 64, low, high)


def call(kernel, shapes, scratch=(), scalars=0):
    vmem = pl.BlockSpec(memory_space=pltpu.VMEM)
    smem = pl.BlockSpec(memory_space=pltpu.SMEM)

    def run(*args):
        out_shape = [jax.ShapeDtypeStruct(s, jnp.float32) for s in shapes]
        return pl.pallas_call(
            kernel,
            out_shape=out_shape,
            in_specs=[smem] * scalars + [vmem] * (len(args) - scalars),
            out_specs=[vmem] * len(shapes),
            scratch_shapes=list(scratch),
            compiler_params=pltpu.CompilerParams(vmem_limit_bytes=32 * 1024 * 1024),
        )(*args)

    return run


def shift(block, axis, distance):
    count = lax.axis_size(axis)
    return lax.ppermute(block, axis, [(i, (i + distance) % count) for i in range(count)])


def per_device(iterate, rates):
    state = iterate[0]
    both = jnp.stack([state, rates])
    low = shift(both[:, :, :, ROWS - HALO :, :], "gy", 1)
    high = shift(both[:, :, :, :HALO, :], "gy", -1)
    strip = (2, EXT, LANES)
    to_low, to_high = call(strips_kernel, [strip, strip])(state, rates, low, high)
    left = shift(to_high, "gz", 1)
    right = shift(to_low, "gz", -1)

    me = lax.axis_index("tm").astype(jnp.int32).reshape(1)
    windows, rates_here = call(
        windows_kernel, [(SLICES, 2, 2, WIN, LANES), (2, 2, WIN, LANES)], scalars=1
    )(me, state, rates, low, high, left, right)
    windows = lax.all_to_all(windows, "tm", 0, 0)

    kept = pltpu.VMEM((SLICES, 2, 2, 8, 8, LANES), jnp.float32)
    (ends,) = call(
        sweep_kernel,
        [(SLICES, 2, SUB, LANES)],
        scratch=[
            pltpu.VMEM((2, 3, 2, 8, 8, LANES), jnp.float32),
            kept,
            kept,
            kept,
            pltpu.VMEM((2, WIN, LANES), jnp.float32),
        ],
    )(windows, rates_here)
    ends = lax.all_to_all(ends, "tm", 0, 0)
    (out,) = call(merge_kernel, [(2, 4, ROWS, LANES)])(ends)
    return out[None]


def solution(mesh):
    return jax.shard_map(
        per_device,
        mesh=mesh,
        in_specs=(P("tm", None, None, "gy", "gz"), P(None, None, "gy", "gz")),
        out_specs=P("tm", None, None, "gy", "gz"),
        check_vma=False,
    )
```

```python
import jax
import jax.numpy as jnp
from jax import lax
from jax.experimental import pallas as pl
from jax.experimental.pallas import tpu as pltpu
from jax.sharding import PartitionSpec as P

FINE = 4
SLICES = 8
HALO = 16
SUB = 32
WIN = SUB + 2 * HALO
ROWS = 64
LANES = 128
EXT = ROWS + 2 * HALO
TILES = EXT // 8

spread_fast = 0.2
spread_slow = 0.1
fine_step = 0.125
coarse_step = 0.5

PAIRS = ((0, 3), (1, 2))


def lane_index():
    return lax.broadcasted_iota(jnp.int32, (8, LANES), 1)


def roll(block, shift, axis):
    shift = shift % block.shape[axis]
    return block if shift == 0 else pltpu.roll(block, shift, axis)


def pick(even, if_even, if_odd):
    return jnp.where(even, if_even, if_odd)


def ext_tile(one, two, own, even, index):
    if index < 2:
        rows = slice(8 * index, 8 * index + 8)
        return pick(even, two[rows, :], one[rows, :])
    if index < 10:
        return own[8 * (index - 2) : 8 * (index - 2) + 8, :]
    rows = slice(8 * (index - 10), 8 * (index - 10) + 8)
    return pick(even, one[rows, :], two[rows, :])


def edges_kernel(me, state, rates, two, one):
    even = me[1] % 2 == 0
    for which, source in enumerate((state, rates)):
        for c in range(2):
            for x in range(4):
                for r in range(2):
                    first = source[c, x, 8 * r : 8 * r + 8, :]
                    last = source[c, x, ROWS - HALO + 8 * r : ROWS - HALO + 8 * r + 8, :]
                    one[which, c, x, 8 * r : 8 * r + 8, :] = pick(even, last, first)
                    two[which, c, x, 8 * r : 8 * r + 8, :] = pick(even, first, last)


def strips_kernel(me, state, rates, y_two, y_one, two, one):
    lane = lane_index()
    even_y = me[1] % 2 == 0
    even_z = me[2] % 2 == 0
    for which, source in enumerate((state, rates)):
        for tile in range(TILES):
            first = jnp.zeros((8, LANES), jnp.float32)
            last = jnp.zeros((8, LANES), jnp.float32)
            for k in range(8):
                c, x = k // 4, k % 4
                rows = ext_tile(y_one.at[which, c, x], y_two.at[which, c, x], source.at[c, x], even_y, tile)
                here = (lane >= 16 * k) & (lane < 16 * k + 16)
                first = jnp.where(here, roll(rows, 16 * k, 1), first)
                last = jnp.where(here, roll(rows, 16 * k + 16, 1), last)
            one[which, 8 * tile : 8 * tile + 8, :] = pick(even_z, last, first)
            two[which, 8 * tile : 8 * tile + 8, :] = pick(even_z, first, last)


def windows_of(own, y_one, y_two, z_one, z_two, even_y, even_z, tile, c, pair, tz, lane):
    parts = []
    for half, x in enumerate(PAIRS[pair]):
        rows = ext_tile(y_one.at[c, x], y_two.at[c, x], own.at[c, x], even_y, tile)
        parts.append(roll(rows, 64 * half - (SUB * tz - HALO), 1))
    block = jnp.where(lane < 64, parts[0], parts[1])
    if tz in (0, 3):
        left = tz == 0
        at = 0 if left else 48
        rows = slice(8 * tile, 8 * tile + 8)
        near, far = z_one[rows, :], z_two[rows, :]
        strip = pick(even_z, far, near) if left else pick(even_z, near, far)
        for half, x in enumerate(PAIRS[pair]):
            k = 4 * c + x
            begin = 64 * half + at
            here = (lane >= begin) & (lane < begin + 16)
            block = jnp.where(here, roll(strip, begin - 16 * k, 1), block)
    return block


def windows_kernel(me, state, rates, y_two, y_one, z_two, z_one, windows, rates_here):
    lane = lane_index()
    even_y = me[1] % 2 == 0
    even_z = me[2] % 2 == 0

    def halos(which):
        return y_one.at[which], y_two.at[which], z_one.at[which], z_two.at[which], even_y, even_z

    my_y = me[0] // 4
    my_z = me[0] % 4
    for tz in range(4):
        for c in range(2):
            for pair in range(2):
                for tile in range(TILES):
                    block = windows_of(state, *halos(0), tile, c, pair, tz, lane)
                    for ty in range(2):
                        at = tile - 4 * ty
                        if 0 <= at < 8:
                            windows[4 * ty + tz, c, pair, 8 * at : 8 * at + 8, :] = block

    for mine in range(4):

        @pl.when(my_z == mine)
        def _():
            for c in range(2):
                for pair in range(2):
                    blocks = [
                        windows_of(rates, *halos(1), tile, c, pair, mine, lane) for tile in range(TILES)
                    ]
                    for at in range(8):
                        block = jnp.where(my_y == 0, blocks[at], blocks[at + 4])
                        rates_here[c, pair, 8 * at : 8 * at + 8, :] = block


def load_state(ref):
    return [[[ref[c, p, j] for j in range(8)] for p in range(2)] for c in range(2)]


def save_state(ref, state):
    for c in range(2):
        for p in range(2):
            for j in range(8):
                ref[c, p, j] = state[c][p][j]


def neighbours(s, p, j, other):
    here = s[j]
    if p == 0:
        along_x = here + other[j]
    else:
        along_x = other[j] + roll(here, 64, 1)
    before = s[j - 1] if j > 0 else roll(s[7], 1, 0)
    after = s[j + 1] if j < 7 else roll(s[0], -1, 0)
    along_z = roll(here, 1, 1) + roll(here, -1, 1)
    return (along_x + (before + after)) + along_z


def step(state, coefs, which, length):
    a, b = state
    new_a = [[None] * 8, [None] * 8]
    new_b = [[None] * 8, [None] * 8]
    for p in range(2):
        for j in range(8):
            here_a, here_b = a[p][j], b[p][j]
            product = length * (here_a * here_b * here_b)
            near_a = neighbours(a[p], p, j, a[1 - p])
            near_b = neighbours(b[p], p, j, b[1 - p])
            keep_a = coefs[which, 0, p, j]
            gain = coefs[which, 1, p, j]
            keep_b = coefs[which, 2, p, j]
            new_a[p][j] = here_a * keep_a + (length * spread_fast) * near_a + (gain - product)
            new_b[p][j] = here_b * keep_b + (length * spread_slow) * near_b + product
    return [new_a, new_b]


def combine(op, left, right):
    return [[[op(left[c][p][j], right[c][p][j]) for j in range(8)] for p in range(2)] for c in range(2)]


def add(left, right):
    return combine(lambda l, r: l + r, left, right)


def subtract(left, right):
    return combine(lambda l, r: l - r, left, right)


def sweep_kernel(windows, rates, out, coefs, starts, terms, coarse_ends, rows):
    lane = lane_index()
    for which, length in enumerate((fine_step, coarse_step)):
        for p in range(2):
            for j in range(8):
                feed = rates[0, p, pl.ds(j, 8, stride=8), :]
                kill = rates[1, p, pl.ds(j, 8, stride=8), :]
                coefs[which, 0, p, j] = (1.0 - 6.0 * spread_fast * length) - length * feed
                coefs[which, 1, p, j] = length * feed
                coefs[which, 2, p, j] = (1.0 - 6.0 * spread_slow * length) - length * (feed + kill)

    def fine(state):
        for _ in range(FINE):
            state = step(state, coefs, 0, fine_step)
        return state

    def coarse(state):
        return step(state, coefs, 1, coarse_step)

    def first(n, carry):
        state = [
            [[windows[n, c, p, pl.ds(j, 8, stride=8), :] for j in range(8)] for p in range(2)]
            for c in range(2)
        ]
        save_state(starts.at[n], state)
        save_state(coarse_ends.at[n], coarse(state))
        end = fine(load_state(starts.at[n]))
        save_state(terms.at[n], subtract(end, load_state(coarse_ends.at[n])))
        return carry

    lax.fori_loop(0, SLICES - 1, first, 0)

    save_state(starts.at[1], add(load_state(coarse_ends.at[0]), load_state(terms.at[0])))

    def first_sweep(n, carry):
        end = coarse(load_state(starts.at[n]))
        save_state(coarse_ends.at[n], end)
        save_state(starts.at[n + 1], add(end, load_state(terms.at[n])))
        return carry

    lax.fori_loop(1, SLICES - 1, first_sweep, 0)
    save_state(coarse_ends.at[SLICES - 1], coarse(load_state(starts.at[SLICES - 1])))

    def second(n, carry):
        end = fine(load_state(starts.at[n]))
        save_state(terms.at[n], subtract(end, load_state(coarse_ends.at[n])))
        return carry

    lax.fori_loop(1, SLICES, second, 0)

    def put(n, state):
        for c in range(2):
            for j in range(8):
                outer, inner = state[c][0][j], state[c][1][j]
                low = jnp.where(lane < 32, roll(outer, -16, 1), roll(inner, 16, 1))
                high = jnp.where(lane < 96, roll(inner, -16, 1), roll(outer, 16, 1))
                rows[c, pl.ds(j, 8, stride=8), :] = jnp.where(lane < 64, low, high)
            out[n, c] = rows[c, HALO : HALO + SUB, :]

    put(0, load_state(starts.at[1]))
    state = add(load_state(coarse_ends.at[1]), load_state(terms.at[1]))
    put(1, state)
    save_state(starts.at[1], state)

    def second_sweep(n, carry):
        state = add(coarse(load_state(starts.at[n - 1])), load_state(terms.at[n]))
        put(n, state)
        save_state(starts.at[n], state)
        return carry

    lax.fori_loop(2, SLICES, second_sweep, 0)


def merge_kernel(parts, out):
    lane = lane_index()
    for c in range(2):
        for x in range(4):
            for ty in range(2):
                for r in range(4):
                    blocks = [
                        roll(parts[4 * ty + tz, c, 8 * r : 8 * r + 8, :], SUB * (tz - x), 1) for tz in range(4)
                    ]
                    low = jnp.where(lane < 32, blocks[0], blocks[1])
                    high = jnp.where(lane < 96, blocks[2], blocks[3])
                    at = SUB * ty + 8 * r
                    out[c, x, at : at + 8, :] = jnp.where(lane < 64, low, high)


def call(kernel, shapes, scratch=(), scalars=0):
    vmem = pl.BlockSpec(memory_space=pltpu.VMEM)
    smem = pl.BlockSpec(memory_space=pltpu.SMEM)

    def run(*args):
        out_shape = [jax.ShapeDtypeStruct(s, jnp.float32) for s in shapes]
        return pl.pallas_call(
            kernel,
            out_shape=out_shape,
            in_specs=[smem] * scalars + [vmem] * (len(args) - scalars),
            out_specs=[vmem] * len(shapes),
            scratch_shapes=list(scratch),
            compiler_params=pltpu.CompilerParams(vmem_limit_bytes=32 * 1024 * 1024),
        )(*args)

    return run


def swap(block, axis, begin):
    count = lax.axis_size(axis)
    route = []
    for i in range(begin, begin + count, 2):
        a, b = i % count, (i + 1) % count
        route += [(a, b), (b, a)]
    return lax.ppermute(block, axis, route)


def per_device(iterate, rates):
    state = iterate[0]
    me = jnp.stack([lax.axis_index(axis).astype(jnp.int32) for axis in ("tm", "gy", "gz")])
    strip = (2, 2, 4, HALO, LANES)
    two, one = call(edges_kernel, [strip, strip], scalars=1)(me, state, rates)
    y_one = swap(one, "gy", 0)
    y_two = swap(two, "gy", 1)
    strip = (2, EXT, LANES)
    two, one = call(strips_kernel, [strip, strip], scalars=1)(me, state, rates, y_two, y_one)
    z_one = swap(one, "gz", 0)
    z_two = swap(two, "gz", 1)
    windows, rates_here = call(
        windows_kernel, [(SLICES, 2, 2, WIN, LANES), (2, 2, WIN, LANES)], scalars=1
    )(me, state, rates, y_two, y_one, z_two, z_one)
    windows = lax.all_to_all(windows, "tm", 0, 0)

    kept = pltpu.VMEM((SLICES, 2, 2, 8, 8, LANES), jnp.float32)
    (ends,) = call(
        sweep_kernel,
        [(SLICES, 2, SUB, LANES)],
        scratch=[
            pltpu.VMEM((2, 3, 2, 8, 8, LANES), jnp.float32),
            kept,
            kept,
            kept,
            pltpu.VMEM((2, WIN, LANES), jnp.float32),
        ],
    )(windows, rates_here)
    ends = lax.all_to_all(ends, "tm", 0, 0)
    (out,) = call(merge_kernel, [(2, 4, ROWS, LANES)])(ends)
    return out[None]


def solution(mesh):
    return jax.shard_map(
        per_device,
        mesh=mesh,
        in_specs=(P("tm", None, None, "gy", "gz"), P(None, None, "gy", "gz")),
        out_specs=P("tm", None, None, "gy", "gz"),
        check_vma=False,
    )
```

```python
import jax
import jax.numpy as jnp
from jax import lax
from jax.experimental import pallas as pl
from jax.experimental.pallas import tpu as pltpu
from jax.sharding import PartitionSpec as P

FINE = 4
SLICES = 8
HALO = 16
SUB = 32
MARGIN = 12
WIN = SUB + 2 * MARGIN
ROWS = 64
LANES = 128
EXT = ROWS + 2 * HALO
TILES = EXT // 8
BLOCK = WIN // 8

spread_fast = 0.2
spread_slow = 0.1
fine_step = 0.125
coarse_step = 0.5

PAIRS = ((0, 3), (1, 2))


def lane_index():
    return lax.broadcasted_iota(jnp.int32, (8, LANES), 1)


def roll(block, shift, axis):
    shift = shift % block.shape[axis]
    return block if shift == 0 else pltpu.roll(block, shift, axis)


def pick(even, if_even, if_odd):
    return jnp.where(even, if_even, if_odd)


def ext_tile(one, two, own, even, index):
    if index < 2:
        rows = slice(8 * index, 8 * index + 8)
        return pick(even, two[rows, :], one[rows, :])
    if index < 10:
        return own[8 * (index - 2) : 8 * (index - 2) + 8, :]
    rows = slice(8 * (index - 10), 8 * (index - 10) + 8)
    return pick(even, one[rows, :], two[rows, :])


def edges_kernel(me, state, rates, two, one, sems):
    odd = me[1] % 2
    copies = []
    for which, source in enumerate((state, rates)):
        for k, (target, at) in enumerate(((two, odd), (one, 1 - odd))):
            begin = pl.multiple_of(at * (ROWS - HALO), HALO)
            copies.append(
                pltpu.make_async_copy(
                    source.at[:, :, pl.ds(begin, HALO), :], target.at[which], sems.at[2 * which + k]
                )
            )
    for copy in copies:
        copy.start()
    for copy in copies:
        copy.wait()


def strips_kernel(me, state, rates, y_two, y_one, two, one):
    lane = lane_index()
    even_y = me[1] % 2 == 0
    even_z = me[2] % 2 == 0
    for which, source in enumerate((state, rates)):
        for tile in range(TILES):
            first = jnp.zeros((8, LANES), jnp.float32)
            last = jnp.zeros((8, LANES), jnp.float32)
            for k in range(8):
                c, x = k // 4, k % 4
                rows = ext_tile(y_one.at[which, c, x], y_two.at[which, c, x], source.at[c, x], even_y, tile)
                here = (lane >= 16 * k) & (lane < 16 * k + 16)
                first = jnp.where(here, roll(rows, 16 * k, 1), first)
                last = jnp.where(here, roll(rows, 16 * k + 16, 1), last)
            one[which, 8 * tile : 8 * tile + 8, :] = pick(even_z, last, first)
            two[which, 8 * tile : 8 * tile + 8, :] = pick(even_z, first, last)


def lay_out(own, y_one, y_two, z_one, z_two, even_y, even_z, wide, lane):
    for tile in range(TILES):
        rows = slice(8 * tile, 8 * tile + 8)
        near, far = z_one[rows, :], z_two[rows, :]
        left = pick(even_z, far, near)
        right = pick(even_z, near, far)
        for k in range(8):
            c, x = k // 4, k % 4
            here = ext_tile(y_one.at[c, x], y_two.at[c, x], own.at[c, x], even_y, tile)
            wide[0, c, x, rows, :] = jnp.where(lane < 16, roll(left, -16 * k, 1), roll(here, 16, 1))
            wide[1, c, x, rows, :] = jnp.where(lane >= 112, roll(right, 112 - 16 * k, 1), roll(here, -16, 1))


def window_tile(wide, c, pair, ty, tz, r, lane):
    block, moved = ((0, 0), (1, 0), (0, 1), (1, 1))[tz]
    begin = SUB * ty + HALO - MARGIN + 8 * r
    parts = [wide[block, c, x, begin : begin + 8, :] for x in PAIRS[pair]]
    parts[1 - moved] = roll(parts[1 - moved], 64, 1)
    return jnp.where(lane < 64, parts[0], parts[1])


def tile_step(source, target, coefs_of, length):
    for x in range(4):
        for j in range(TILES):
            keep_a, gain, keep_b = coefs_of(x, j)
            here = [source[c, x, j] for c in range(2)]
            near = []
            for c in range(2):
                below = source[c, max(x - 1, 0), j]
                above = source[c, min(x + 1, 3), j]
                before = source[c, x, j - 1] if j > 0 else roll(source[c, x, TILES - 1], 1, 0)
                after = source[c, x, j + 1] if j < TILES - 1 else roll(source[c, x, 0], -1, 0)
                along_z = roll(here[c], 1, 1) + roll(here[c], -1, 1)
                near.append(((below + above) + (before + after)) + along_z)
            a, b = here
            product = length * (a * b * b)
            target[0, x, j] = a * keep_a + (length * spread_fast) * near[0] + (gain - product)
            target[1, x, j] = b * keep_b + (length * spread_slow) * near[1] + product


def coefs_from(feed, kill, length):
    gain = length * feed
    keep_a = (1.0 - 6.0 * spread_fast * length) - gain
    keep_b = (1.0 - 6.0 * spread_slow * length) - length * (feed + kill)
    return keep_a, gain, keep_b


def first_kernel(
    me, state, rates, y_two, y_one, z_two, z_one, windows, rates_here, wide, wide_rates, coefs, even, odd, slow
):
    lane = lane_index()
    even_y = me[1] % 2 == 0
    even_z = me[2] % 2 == 0
    for which, source, target in ((0, state, wide), (1, rates, wide_rates)):
        lay_out(
            source,
            y_one.at[which],
            y_two.at[which],
            z_one.at[which],
            z_two.at[which],
            even_y,
            even_z,
            target,
            lane,
        )

    def rows_of(j):
        return pl.ds(j, 8, stride=TILES)

    def block(w, carry):
        for x in range(4):
            for j in range(TILES):
                feed = wide_rates[w, 0, x, rows_of(j), :]
                kill = wide_rates[w, 1, x, rows_of(j), :]
                for i, value in enumerate(coefs_from(feed, kill, fine_step)):
                    coefs[i, x, j] = value
                for c in range(2):
                    even[c, x, j] = wide[w, c, x, rows_of(j), :]

        def coarse_coefs(x, j):
            feed = wide_rates[w, 0, x, rows_of(j), :]
            kill = wide_rates[w, 1, x, rows_of(j), :]
            return coefs_from(feed, kill, coarse_step)

        def fine_coefs(x, j):
            return [coefs[i, x, j] for i in range(3)]

        tile_step(even, slow, coarse_coefs, coarse_step)

        def two_steps(_, inner):
            tile_step(even, odd, fine_coefs, fine_step)
            tile_step(odd, even, fine_coefs, fine_step)
            return inner

        lax.fori_loop(0, FINE // 2, two_steps, 0)
        leading = me[0] == 0
        for c in range(2):
            for x in range(4):
                for j in range(TILES):
                    coarse_end = slow[c, x, j]
                    difference = even[c, x, j] - coarse_end
                    wide[w, c, x, rows_of(j), :] = jnp.where(leading, coarse_end + difference, difference)
        return carry

    lax.fori_loop(0, 2, block, 0)

    my_y = me[0] // 4
    my_z = me[0] % 4
    for c in range(2):
        for pair in range(2):
            for r in range(BLOCK):
                for tz in range(4):
                    for ty in range(2):
                        windows[4 * ty + tz, c, pair, 8 * r : 8 * r + 8, :] = window_tile(
                            wide, c, pair, ty, tz, r, lane
                        )

    for tz in range(4):

        @pl.when(my_z == tz)
        def _():
            for c in range(2):
                for pair in range(2):
                    for r in range(BLOCK):
                        tiles = [window_tile(wide_rates, c, pair, ty, tz, r, lane) for ty in range(2)]
                        rates_here[c, pair, 8 * r : 8 * r + 8, :] = jnp.where(my_y == 0, tiles[0], tiles[1])


def load_state(ref):
    return [[[ref[c, p, j] for j in range(BLOCK)] for p in range(2)] for c in range(2)]


def save_state(ref, state):
    for c in range(2):
        for p in range(2):
            for j in range(BLOCK):
                ref[c, p, j] = state[c][p][j]


def neighbours(s, p, j, other):
    here = s[j]
    if p == 0:
        along_x = here + other[j]
    else:
        along_x = other[j] + roll(here, 64, 1)
    before = s[j - 1] if j > 0 else roll(s[BLOCK - 1], 1, 0)
    after = s[j + 1] if j < BLOCK - 1 else roll(s[0], -1, 0)
    along_z = roll(here, 1, 1) + roll(here, -1, 1)
    return (along_x + (before + after)) + along_z


def step(state, coefs, which, length):
    a, b = state
    new_a = [[None] * BLOCK, [None] * BLOCK]
    new_b = [[None] * BLOCK, [None] * BLOCK]
    for p in range(2):
        for j in range(BLOCK):
            here_a, here_b = a[p][j], b[p][j]
            product = length * (here_a * here_b * here_b)
            near_a = neighbours(a[p], p, j, a[1 - p])
            near_b = neighbours(b[p], p, j, b[1 - p])
            keep_a = coefs[which, 0, p, j]
            gain = coefs[which, 1, p, j]
            keep_b = coefs[which, 2, p, j]
            new_a[p][j] = here_a * keep_a + (length * spread_fast) * near_a + (gain - product)
            new_b[p][j] = here_b * keep_b + (length * spread_slow) * near_b + product
    return [new_a, new_b]


def combine(op, left, right):
    return [[[op(left[c][p][j], right[c][p][j]) for j in range(BLOCK)] for p in range(2)] for c in range(2)]


def add(left, right):
    return combine(lambda l, r: l + r, left, right)


def subtract(left, right):
    return combine(lambda l, r: l - r, left, right)


def sweep_kernel(windows, rates, out, coefs, starts, terms, coarse_ends, rows):
    lane = lane_index()

    def rows_of(j):
        return pl.ds(j, 8, stride=BLOCK)

    for p in range(2):
        for j in range(BLOCK):
            feed = rates[0, p, rows_of(j), :]
            kill = rates[1, p, rows_of(j), :]
            for which, length in enumerate((fine_step, coarse_step)):
                for i, value in enumerate(coefs_from(feed, kill, length)):
                    coefs[which, i, p, j] = value

    def fine(state):
        for _ in range(FINE):
            state = step(state, coefs, 0, fine_step)
        return state

    def coarse(state):
        return step(state, coefs, 1, coarse_step)

    def received(n):
        return [
            [[windows[n, c, p, rows_of(j), :] for j in range(BLOCK)] for p in range(2)] for c in range(2)
        ]

    save_state(starts.at[1], received(0))

    def first_sweep(n, carry):
        end = coarse(load_state(starts.at[n]))
        save_state(coarse_ends.at[n], end)
        save_state(starts.at[n + 1], add(end, received(n)))
        return carry

    lax.fori_loop(1, SLICES - 1, first_sweep, 0)
    save_state(coarse_ends.at[SLICES - 1], coarse(load_state(starts.at[SLICES - 1])))

    def second(n, carry):
        end = fine(load_state(starts.at[n]))
        save_state(terms.at[n], subtract(end, load_state(coarse_ends.at[n])))
        return carry

    lax.fori_loop(1, SLICES, second, 0)

    def put(n, state):
        for c in range(2):
            for j in range(BLOCK):
                outer, inner = state[c][0][j], state[c][1][j]
                low = jnp.where(lane < 32, roll(outer, -16, 1), roll(inner, 16, 1))
                high = jnp.where(lane < 96, roll(inner, -16, 1), roll(outer, 16, 1))
                rows[c, rows_of(j), :] = jnp.where(lane < 64, low, high)
            out[n, c] = rows[c, MARGIN : MARGIN + SUB, :]

    put(0, load_state(starts.at[1]))
    state = add(load_state(coarse_ends.at[1]), load_state(terms.at[1]))
    put(1, state)
    save_state(starts.at[1], state)

    def second_sweep(n, carry):
        state = add(coarse(load_state(starts.at[n - 1])), load_state(terms.at[n]))
        put(n, state)
        save_state(starts.at[n], state)
        return carry

    lax.fori_loop(2, SLICES, second_sweep, 0)


def merge_kernel(parts, out):
    lane = lane_index()
    for c in range(2):
        for x in range(4):
            for ty in range(2):
                for r in range(4):
                    blocks = [
                        roll(parts[4 * ty + tz, c, 8 * r : 8 * r + 8, :], SUB * (tz - x), 1) for tz in range(4)
                    ]
                    low = jnp.where(lane < 32, blocks[0], blocks[1])
                    high = jnp.where(lane < 96, blocks[2], blocks[3])
                    at = SUB * ty + 8 * r
                    out[c, x, at : at + 8, :] = jnp.where(lane < 64, low, high)


def call(kernel, shapes, scratch=(), scalars=0, inputs=pltpu.VMEM):
    vmem = pl.BlockSpec(memory_space=pltpu.VMEM)
    given = pl.BlockSpec(memory_space=inputs)
    smem = pl.BlockSpec(memory_space=pltpu.SMEM)

    def run(*args):
        out_shape = [jax.ShapeDtypeStruct(s, jnp.float32) for s in shapes]
        return pl.pallas_call(
            kernel,
            out_shape=out_shape,
            in_specs=[smem] * scalars + [given] * (len(args) - scalars),
            out_specs=[vmem] * len(shapes),
            scratch_shapes=list(scratch),
            compiler_params=pltpu.CompilerParams(vmem_limit_bytes=32 * 1024 * 1024),
        )(*args)

    return run


def swap(block, axis, begin):
    count = lax.axis_size(axis)
    route = []
    for i in range(begin, begin + count, 2):
        a, b = i % count, (i + 1) % count
        route += [(a, b), (b, a)]
    return lax.ppermute(block, axis, route)


def per_device(iterate, rates):
    state = iterate[0]
    me = jnp.stack([lax.axis_index(axis).astype(jnp.int32) for axis in ("tm", "gy", "gz")])
    strip = (2, 2, 4, HALO, LANES)
    two, one = call(
        edges_kernel, [strip, strip], scratch=[pltpu.SemaphoreType.DMA((4,))], scalars=1, inputs=pltpu.HBM
    )(me, state, rates)
    y_one = swap(one, "gy", 0)
    y_two = swap(two, "gy", 1)
    strip = (2, EXT, LANES)
    two, one = call(strips_kernel, [strip, strip], scalars=1)(me, state, rates, y_two, y_one)
    z_one = swap(one, "gz", 0)
    z_two = swap(two, "gz", 1)
    tile_state = pltpu.VMEM((2, 4, TILES, 8, LANES), jnp.float32)
    windows, rates_here = call(
        first_kernel,
        [(SLICES, 2, 2, WIN, LANES), (2, 2, WIN, LANES)],
        scratch=[
            pltpu.VMEM((2, 2, 4, EXT, LANES), jnp.float32),
            pltpu.VMEM((2, 2, 4, EXT, LANES), jnp.float32),
            pltpu.VMEM((3, 4, TILES, 8, LANES), jnp.float32),
            tile_state,
            tile_state,
            tile_state,
        ],
        scalars=1,
    )(me, state, rates, y_two, y_one, z_two, z_one)
    windows = lax.all_to_all(windows, "tm", 0, 0)

    kept = pltpu.VMEM((SLICES, 2, 2, BLOCK, 8, LANES), jnp.float32)
    (ends,) = call(
        sweep_kernel,
        [(SLICES, 2, SUB, LANES)],
        scratch=[
            pltpu.VMEM((2, 3, 2, BLOCK, 8, LANES), jnp.float32),
            kept,
            kept,
            kept,
            pltpu.VMEM((2, WIN, LANES), jnp.float32),
        ],
    )(windows, rates_here)
    ends = lax.all_to_all(ends, "tm", 0, 0)
    (out,) = call(merge_kernel, [(2, 4, ROWS, LANES)])(ends)
    return out[None]


def solution(mesh):
    return jax.shard_map(
        per_device,
        mesh=mesh,
        in_specs=(P("tm", None, None, "gy", "gz"), P(None, None, "gy", "gz")),
        out_specs=P("tm", None, None, "gy", "gz"),
        check_vma=False,
    )
```

```python
import jax
import jax.numpy as jnp
from jax import lax
from jax.experimental import pallas as pl
from jax.experimental.pallas import tpu as pltpu
from jax.sharding import Mesh
from jax.sharding import PartitionSpec as P

FINE = 4
GROUP = 4
HALO = 16
SUB = 32
ROWS = 64
MARGIN = 12
WIN = ROWS + 2 * MARGIN
SENT = 80
LANES = 128
EXT = ROWS + 2 * HALO
TILES = EXT // 8
BLOCK = WIN // 8

spread_fast = 0.2
spread_slow = 0.1
fine_step = 0.125
coarse_step = 0.5

PAIRS = ((0, 3), (1, 2))


def lane_index():
    return lax.broadcasted_iota(jnp.int32, (8, LANES), 1)


def roll(block, shift, axis):
    shift = shift % block.shape[axis]
    return block if shift == 0 else pltpu.roll(block, shift, axis)


def pick(even, if_even, if_odd):
    return jnp.where(even, if_even, if_odd)


def ext_tile(one, two, own, even, index):
    if index < 2:
        rows = slice(8 * index, 8 * index + 8)
        return pick(even, two[rows, :], one[rows, :])
    if index < 10:
        return own[8 * (index - 2) : 8 * (index - 2) + 8, :]
    rows = slice(8 * (index - 10), 8 * (index - 10) + 8)
    return pick(even, one[rows, :], two[rows, :])


def strips_kernel(me, state, rates, y_two, y_one, two, one):
    lane = lane_index()
    even_y = me[1] % 2 == 0
    even_z = me[2] % 2 == 0
    for which, source in enumerate((state, rates)):
        for tile in range(TILES):
            first = jnp.zeros((8, LANES), jnp.float32)
            last = jnp.zeros((8, LANES), jnp.float32)
            for k in range(8):
                c, x = k // 4, k % 4
                rows = ext_tile(y_one.at[which, c, x], y_two.at[which, c, x], source.at[c, x], even_y, tile)
                here = (lane >= 16 * k) & (lane < 16 * k + 16)
                first = jnp.where(here, roll(rows, 16 * k, 1), first)
                last = jnp.where(here, roll(rows, 16 * k + 16, 1), last)
            one[which, 8 * tile : 8 * tile + 8, :] = pick(even_z, last, first)
            two[which, 8 * tile : 8 * tile + 8, :] = pick(even_z, first, last)


def lay_out(own, y_one, y_two, z_one, z_two, even_y, even_z, wide, lane):
    for tile in range(TILES):
        rows = slice(8 * tile, 8 * tile + 8)
        near, far = z_one[rows, :], z_two[rows, :]
        left = pick(even_z, far, near)
        right = pick(even_z, near, far)
        for k in range(8):
            c, x = k // 4, k % 4
            here = ext_tile(y_one.at[c, x], y_two.at[c, x], own.at[c, x], even_y, tile)
            wide[0, c, x, rows, :] = jnp.where(lane < 16, roll(left, -16 * k, 1), roll(here, 16, 1))
            wide[1, c, x, rows, :] = jnp.where(lane >= 112, roll(right, 112 - 16 * k, 1), roll(here, -16, 1))


def window_tile(wide, c, pair, sub, r, lane):
    block, moved = ((0, 0), (1, 0), (0, 1), (1, 1))[sub]
    begin = HALO - MARGIN + 8 * r
    parts = [wide[block, c, x, begin : begin + 8, :] for x in PAIRS[pair]]
    parts[1 - moved] = roll(parts[1 - moved], 64, 1)
    return jnp.where(lane < 64, parts[0], parts[1])


def tile_step(source, target, coefs_of, length):
    for x in range(4):
        for j in range(TILES):
            keep_a, gain, keep_b = coefs_of(x, j)
            here = [source[c, x, j] for c in range(2)]
            near = []
            for c in range(2):
                below = source[c, max(x - 1, 0), j]
                above = source[c, min(x + 1, 3), j]
                before = source[c, x, j - 1] if j > 0 else roll(source[c, x, TILES - 1], 1, 0)
                after = source[c, x, j + 1] if j < TILES - 1 else roll(source[c, x, 0], -1, 0)
                along_z = roll(here[c], 1, 1) + roll(here[c], -1, 1)
                near.append(((below + above) + (before + after)) + along_z)
            a, b = here
            product = length * (a * b * b)
            target[0, x, j] = a * keep_a + (length * spread_fast) * near[0] + (gain - product)
            target[1, x, j] = b * keep_b + (length * spread_slow) * near[1] + product


def coefs_from(feed, kill, length):
    gain = length * feed
    keep_a = (1.0 - 6.0 * spread_fast * length) - gain
    keep_b = (1.0 - 6.0 * spread_slow * length) - length * (feed + kill)
    return keep_a, gain, keep_b


def first_kernel(
    me, state, rates, y_two, y_one, z_two, z_one, windows, rates_here, wide, wide_rates, coefs, even, odd, slow
):
    lane = lane_index()
    even_y = me[1] % 2 == 0
    even_z = me[2] % 2 == 0
    for which, source, target in ((0, state, wide), (1, rates, wide_rates)):
        lay_out(
            source,
            y_one.at[which],
            y_two.at[which],
            z_one.at[which],
            z_two.at[which],
            even_y,
            even_z,
            target,
            lane,
        )

    def rows_of(j):
        return pl.ds(j, 8, stride=TILES)

    def block(w, carry):
        for x in range(4):
            for j in range(TILES):
                feed = wide_rates[w, 0, x, rows_of(j), :]
                kill = wide_rates[w, 1, x, rows_of(j), :]
                for i, value in enumerate(coefs_from(feed, kill, fine_step)):
                    coefs[i, x, j] = value
                for c in range(2):
                    even[c, x, j] = wide[w, c, x, rows_of(j), :]

        def coarse_coefs(x, j):
            feed = wide_rates[w, 0, x, rows_of(j), :]
            kill = wide_rates[w, 1, x, rows_of(j), :]
            return coefs_from(feed, kill, coarse_step)

        def fine_coefs(x, j):
            return [coefs[i, x, j] for i in range(3)]

        tile_step(even, slow, coarse_coefs, coarse_step)

        def two_steps(_, inner):
            tile_step(even, odd, fine_coefs, fine_step)
            tile_step(odd, even, fine_coefs, fine_step)
            return inner

        lax.fori_loop(0, FINE // 2, two_steps, 0)
        leading = me[0] == 0
        for c in range(2):
            for x in range(4):
                for j in range(TILES):
                    coarse_end = slow[c, x, j]
                    difference = even[c, x, j] - coarse_end
                    wide[w, c, x, rows_of(j), :] = jnp.where(leading, coarse_end + difference, difference)
        return carry

    lax.fori_loop(0, 2, block, 0)

    early = me[0] < GROUP
    for sub in range(GROUP):
        worker = jnp.where(early, sub, GROUP - 1 - sub)
        for c in range(2):
            for pair in range(2):
                for r in range(BLOCK):
                    windows[worker, c, pair, 8 * r : 8 * r + 8, :] = window_tile(wide, c, pair, sub, r, lane)

        @pl.when(worker == me[0] % GROUP)
        def _():
            for c in range(2):
                for pair in range(2):
                    for r in range(BLOCK):
                        rates_here[c, pair, 8 * r : 8 * r + 8, :] = window_tile(
                            wide_rates, c, pair, sub, r, lane
                        )


def load_state(ref):
    return [[[ref[c, p, j] for j in range(BLOCK)] for p in range(2)] for c in range(2)]


def save_state(ref, state):
    for c in range(2):
        for p in range(2):
            for j in range(BLOCK):
                ref[c, p, j] = state[c][p][j]


def neighbours(s, p, j, other):
    here = s[j]
    if p == 0:
        along_x = here + other[j]
    else:
        along_x = other[j] + roll(here, 64, 1)
    before = s[j - 1] if j > 0 else roll(s[BLOCK - 1], 1, 0)
    after = s[j + 1] if j < BLOCK - 1 else roll(s[0], -1, 0)
    along_z = roll(here, 1, 1) + roll(here, -1, 1)
    return (along_x + (before + after)) + along_z


def step(state, coefs, which, length):
    a, b = state
    new_a = [[None] * BLOCK, [None] * BLOCK]
    new_b = [[None] * BLOCK, [None] * BLOCK]
    for p in range(2):
        for j in range(BLOCK):
            here_a, here_b = a[p][j], b[p][j]
            product = length * (here_a * here_b * here_b)
            near_a = neighbours(a[p], p, j, a[1 - p])
            near_b = neighbours(b[p], p, j, b[1 - p])
            keep_a = coefs[which, 0, p, j]
            gain = coefs[which, 1, p, j]
            keep_b = coefs[which, 2, p, j]
            new_a[p][j] = here_a * keep_a + (length * spread_fast) * near_a + (gain - product)
            new_b[p][j] = here_b * keep_b + (length * spread_slow) * near_b + product
    return [new_a, new_b]


def combine(op, left, right):
    return [[[op(left[c][p][j], right[c][p][j]) for j in range(BLOCK)] for p in range(2)] for c in range(2)]


def add(left, right):
    return combine(lambda l, r: l + r, left, right)


def subtract(left, right):
    return combine(lambda l, r: l - r, left, right)


def rows_of(j):
    return pl.ds(j, 8, stride=BLOCK)


def load_window(ref):
    return [[[ref[c, p, rows_of(j), :] for j in range(BLOCK)] for p in range(2)] for c in range(2)]


def save_coefs(coefs, rates):
    for p in range(2):
        for j in range(BLOCK):
            feed = rates[0, p, rows_of(j), :]
            kill = rates[1, p, rows_of(j), :]
            for which, length in enumerate((fine_step, coarse_step)):
                for i, value in enumerate(coefs_from(feed, kill, length)):
                    coefs[which, i, p, j] = value


def fine(state, coefs):
    for _ in range(FINE):
        state = step(state, coefs, 0, fine_step)
    return state


def coarse(state, coefs):
    return step(state, coefs, 1, coarse_step)


def put(out, rows, m, state):
    lane = lane_index()
    for c in range(2):
        for j in range(BLOCK):
            outer, inner = state[c][0][j], state[c][1][j]
            low = jnp.where(lane < 32, roll(outer, -16, 1), roll(inner, 16, 1))
            high = jnp.where(lane < 96, roll(inner, -16, 1), roll(outer, 16, 1))
            rows[c, rows_of(j), :] = jnp.where(lane < 64, low, high)
        out[m, c] = rows[c, MARGIN : MARGIN + ROWS, :]


def sweep(first, windows, coefs, starts, coarse_ends):
    def turn(m, carry):
        end = coarse(load_state(starts.at[m]), coefs)
        save_state(coarse_ends.at[m], end)
        save_state(starts.at[m + 1], add(end, load_window(windows.at[m])))
        return carry

    lax.fori_loop(first, GROUP, turn, 0)


def second_terms(first, coefs, starts, coarse_ends):
    def turn(m, carry):
        end = fine(load_state(starts.at[m]), coefs)
        save_state(starts.at[m], subtract(end, load_state(coarse_ends.at[m])))
        return carry

    lax.fori_loop(first, GROUP, turn, 0)


def second_sweep(first, coefs, current, terms, rows, out):
    def turn(m, carry):
        state = add(coarse(load_state(current), coefs), load_state(terms.at[m]))
        put(out, rows, m, state)
        save_state(current, state)
        return carry

    lax.fori_loop(first, GROUP, turn, 0)


def early_kernel(me, windows, rates, ends, sent, coefs, starts, coarse_ends, current, rows, kept):
    @pl.when(me[0] < GROUP)
    def _():
        save_coefs(coefs, rates)
        save_state(starts.at[1], load_window(windows.at[0]))
        sweep(1, windows, coefs, starts, coarse_ends)
        put(ends, rows, 0, load_state(starts.at[1]))
        pack(sent, 0, kept, load_state(starts.at[GROUP]))
        second_terms(1, coefs, starts, coarse_ends)
        state = add(load_state(coarse_ends.at[1]), load_state(starts.at[1]))
        put(ends, rows, 1, state)
        save_state(current, state)
        second_sweep(2, coefs, current, starts, rows, ends)
        pack(sent, 1, kept, load_state(current))


def pack(sent, which, kept, state):
    for c in range(2):
        for p in range(2):
            for j in range(BLOCK):
                kept[c, p, rows_of(j), :] = state[c][p][j]
            begin = MARGIN + (ROWS - SENT) // 2
            sent[which, c, p] = kept[c, p, begin : begin + SENT, :]


def unpack(sent, which, kept, target):
    for c in range(2):
        for p in range(2):
            begin = MARGIN + (ROWS - SENT) // 2
            kept[c, p, begin : begin + SENT, :] = sent[which, c, p]
    save_state(target, load_window(kept))


def late_kernel(me, windows, rates, received, early_ends, ends, coefs, starts, coarse_ends, current, rows, kept):
    @pl.when(me[0] < GROUP)
    def _():
        for m in range(GROUP):
            ends[m] = early_ends[m]

    @pl.when(me[0] >= GROUP)
    def _():
        save_coefs(coefs, rates)
        kept[...] = jnp.zeros_like(kept)
        unpack(received, 0, kept, starts.at[0])
        unpack(received, 1, kept, current)
        sweep(0, windows, coefs, starts, coarse_ends)
        second_terms(0, coefs, starts, coarse_ends)
        second_sweep(0, coefs, current, starts, rows, ends)


def merge_kernel(me, parts, out):
    lane = lane_index()
    early = me[0] < GROUP
    workers = [jnp.where(early, sub, GROUP - 1 - sub) for sub in range(GROUP)]
    for c in range(2):
        for r in range(ROWS // 8):
            rows = slice(8 * r, 8 * r + 8)
            strips = [parts[workers[sub], c, rows, :] for sub in range(GROUP)]
            for x in range(4):
                blocks = [roll(strips[sub], SUB * (sub - x), 1) for sub in range(GROUP)]
                low = jnp.where(lane < 32, blocks[0], blocks[1])
                high = jnp.where(lane < 96, blocks[2], blocks[3])
                out[c, x, rows, :] = jnp.where(lane < 64, low, high)


def call(kernel, shapes, scratch=(), scalars=0, inputs=pltpu.VMEM):
    vmem = pl.BlockSpec(memory_space=pltpu.VMEM)
    given = pl.BlockSpec(memory_space=inputs)
    smem = pl.BlockSpec(memory_space=pltpu.SMEM)

    def run(*args):
        out_shape = [jax.ShapeDtypeStruct(s, jnp.float32) for s in shapes]
        return pl.pallas_call(
            kernel,
            out_shape=out_shape,
            in_specs=[smem] * scalars + [given] * (len(args) - scalars),
            out_specs=[vmem] * len(shapes),
            scratch_shapes=list(scratch),
            compiler_params=pltpu.CompilerParams(vmem_limit_bytes=32 * 1024 * 1024),
        )(*args)

    return run


def swap(block, axis, begin):
    count = lax.axis_size(axis)
    route = []
    for i in range(begin, begin + count, 2):
        a, b = i % count, (i + 1) % count
        route += [(a, b), (b, a)]
    return lax.ppermute(block, axis, route)


def edge(blocks, begin):
    return jnp.stack([lax.dynamic_slice_in_dim(block, begin, HALO, 2) for block in blocks])


def per_device(iterate, rates):
    state = iterate[0]
    slice_index = GROUP * lax.axis_index("th") + lax.axis_index("tl")
    gy, gz = lax.axis_index("gy"), lax.axis_index("gz")
    me = jnp.stack([slice_index, gy, gz]).astype(jnp.int32)
    odd = gy % 2
    two = edge((state, rates), odd * (ROWS - HALO))
    one = edge((state, rates), (1 - odd) * (ROWS - HALO))
    y_two = swap(two, "gy", 1)
    y_one = swap(one, "gy", 0)
    strip = (2, EXT, LANES)
    two, one = call(strips_kernel, [strip, strip], scalars=1)(me, state, rates, y_two, y_one)
    z_two = swap(two, "gz", 1)
    z_one = swap(one, "gz", 0)
    tile_state = pltpu.VMEM((2, 4, TILES, 8, LANES), jnp.float32)
    windows, rates_here = call(
        first_kernel,
        [(GROUP, 2, 2, WIN, LANES), (2, 2, WIN, LANES)],
        scratch=[
            pltpu.VMEM((2, 2, 4, EXT, LANES), jnp.float32),
            pltpu.VMEM((2, 2, 4, EXT, LANES), jnp.float32),
            pltpu.VMEM((3, 4, TILES, 8, LANES), jnp.float32),
            tile_state,
            tile_state,
            tile_state,
        ],
        scalars=1,
    )(me, state, rates, y_two, y_one, z_two, z_one)
    windows = lax.all_to_all(windows, "tl", 0, 0)

    scratch = [
        pltpu.VMEM((2, 3, 2, BLOCK, 8, LANES), jnp.float32),
        pltpu.VMEM((GROUP + 1, 2, 2, BLOCK, 8, LANES), jnp.float32),
        pltpu.VMEM((GROUP, 2, 2, BLOCK, 8, LANES), jnp.float32),
        pltpu.VMEM((2, 2, BLOCK, 8, LANES), jnp.float32),
        pltpu.VMEM((2, WIN, LANES), jnp.float32),
        pltpu.VMEM((2, 2, WIN, LANES), jnp.float32),
    ]
    ends_shape = (GROUP, 2, ROWS, LANES)
    early_ends, sent = call(
        early_kernel, [ends_shape, (2, 2, 2, SENT, LANES)], scratch=scratch, scalars=1
    )(me, windows, rates_here)
    last = 2 * GROUP - 1
    received = lax.ppermute(sent, ("th", "tl"), [(t, last - t) for t in range(GROUP)])
    (ends,) = call(late_kernel, [ends_shape], scratch=scratch, scalars=1)(
        me, windows, rates_here, received, early_ends
    )
    ends = lax.all_to_all(ends, "tl", 0, 0)
    (out,) = call(merge_kernel, [(2, 4, ROWS, LANES)], scalars=1)(me, ends)
    return out[None]


def solution(mesh):
    shape = mesh.devices.shape
    split = Mesh(mesh.devices.reshape(shape[0] // GROUP, GROUP, *shape[1:]), ("th", "tl", "gy", "gz"))
    return jax.shard_map(
        per_device,
        mesh=split,
        in_specs=(P(("th", "tl"), None, None, "gy", "gz"), P(None, None, "gy", "gz")),
        out_specs=P(("th", "tl"), None, None, "gy", "gz"),
        check_vma=False,
    )
```

```python
import jax
import jax.numpy as jnp
from jax import lax
from jax.experimental import pallas as pl
from jax.experimental.pallas import tpu as pltpu
from jax.sharding import Mesh
from jax.sharding import PartitionSpec as P

FINE = 4
GROUP = 4
HALO = 16
SUB = 32
ROWS = 64
MARGIN = 12
WIN = ROWS + 2 * MARGIN
SENT = (80, 72)
LANES = 128
EXT = ROWS + 2 * HALO
TILES = EXT // 8
BLOCK = WIN // 8

spread_fast = 0.2
spread_slow = 0.1
fine_step = 0.125
coarse_step = 0.5

PAIRS = ((0, 3), (1, 2))


def lane_index():
    return lax.broadcasted_iota(jnp.int32, (8, LANES), 1)


def roll(block, shift, axis):
    shift = shift % block.shape[axis]
    return block if shift == 0 else pltpu.roll(block, shift, axis)


def pick(even, if_even, if_odd):
    return jnp.where(even, if_even, if_odd)


def ext_tile(one, two, own, even, index):
    if index < 2:
        rows = slice(8 * index, 8 * index + 8)
        return pick(even, two[rows, :], one[rows, :])
    if index < 10:
        return own[8 * (index - 2) : 8 * (index - 2) + 8, :]
    rows = slice(8 * (index - 10), 8 * (index - 10) + 8)
    return pick(even, one[rows, :], two[rows, :])


def strips_kernel(me, state, rates, y_two, y_one, two, one):
    lane = lane_index()
    even_y = me[1] % 2 == 0
    even_z = me[2] % 2 == 0
    for which, source in enumerate((state, rates)):
        for tile in range(TILES):
            first = jnp.zeros((8, LANES), jnp.float32)
            last = jnp.zeros((8, LANES), jnp.float32)
            for k in range(8):
                c, x = k // 4, k % 4
                rows = ext_tile(y_one.at[which, c, x], y_two.at[which, c, x], source.at[c, x], even_y, tile)
                here = (lane >= 16 * k) & (lane < 16 * k + 16)
                first = jnp.where(here, roll(rows, 16 * k, 1), first)
                last = jnp.where(here, roll(rows, 16 * k + 16, 1), last)
            one[which, 8 * tile : 8 * tile + 8, :] = pick(even_z, last, first)
            two[which, 8 * tile : 8 * tile + 8, :] = pick(even_z, first, last)


def lay_out(own, y_one, y_two, z_one, z_two, even_y, even_z, wide, lane):
    for tile in range(TILES):
        rows = slice(8 * tile, 8 * tile + 8)
        near, far = z_one[rows, :], z_two[rows, :]
        left = pick(even_z, far, near)
        right = pick(even_z, near, far)
        for k in range(8):
            c, x = k // 4, k % 4
            here = ext_tile(y_one.at[c, x], y_two.at[c, x], own.at[c, x], even_y, tile)
            wide[0, c, x, rows, :] = jnp.where(lane < 16, roll(left, -16 * k, 1), roll(here, 16, 1))
            wide[1, c, x, rows, :] = jnp.where(lane >= 112, roll(right, 112 - 16 * k, 1), roll(here, -16, 1))


def window_tile(wide, c, pair, sub, r, lane):
    block, moved = ((0, 0), (1, 0), (0, 1), (1, 1))[sub]
    begin = HALO - MARGIN + 8 * r
    parts = [wide[block, c, x, begin : begin + 8, :] for x in PAIRS[pair]]
    parts[1 - moved] = roll(parts[1 - moved], 64, 1)
    return jnp.where(lane < 64, parts[0], parts[1])


def tile_step(source, target, coefs_of, length):
    for x in range(4):
        for j in range(TILES):
            keep_a, gain, keep_b = coefs_of(x, j)
            here = [source[c, x, j] for c in range(2)]
            near = []
            for c in range(2):
                below = source[c, max(x - 1, 0), j]
                above = source[c, min(x + 1, 3), j]
                before = source[c, x, j - 1] if j > 0 else roll(source[c, x, TILES - 1], 1, 0)
                after = source[c, x, j + 1] if j < TILES - 1 else roll(source[c, x, 0], -1, 0)
                along_z = roll(here[c], 1, 1) + roll(here[c], -1, 1)
                near.append(((below + above) + (before + after)) + along_z)
            a, b = here
            product = length * (a * b * b)
            target[0, x, j] = a * keep_a + (length * spread_fast) * near[0] + (gain - product)
            target[1, x, j] = b * keep_b + (length * spread_slow) * near[1] + product


def coefs_from(feed, kill, length):
    gain = length * feed
    keep_a = (1.0 - 6.0 * spread_fast * length) - gain
    keep_b = (1.0 - 6.0 * spread_slow * length) - length * (feed + kill)
    return keep_a, gain, keep_b


def first_kernel(
    me, state, rates, y_two, y_one, z_two, z_one, windows, rates_here, wide, wide_rates, coefs, even, odd, slow
):
    lane = lane_index()
    even_y = me[1] % 2 == 0
    even_z = me[2] % 2 == 0
    for which, source, target in ((0, state, wide), (1, rates, wide_rates)):
        lay_out(
            source,
            y_one.at[which],
            y_two.at[which],
            z_one.at[which],
            z_two.at[which],
            even_y,
            even_z,
            target,
            lane,
        )

    def rows_of(j):
        return pl.ds(j, 8, stride=TILES)

    def block(w, carry):
        for x in range(4):
            for j in range(TILES):
                feed = wide_rates[w, 0, x, rows_of(j), :]
                kill = wide_rates[w, 1, x, rows_of(j), :]
                for i, value in enumerate(coefs_from(feed, kill, fine_step)):
                    coefs[i, x, j] = value
                for c in range(2):
                    even[c, x, j] = wide[w, c, x, rows_of(j), :]

        def coarse_coefs(x, j):
            feed = wide_rates[w, 0, x, rows_of(j), :]
            kill = wide_rates[w, 1, x, rows_of(j), :]
            return coefs_from(feed, kill, coarse_step)

        def fine_coefs(x, j):
            return [coefs[i, x, j] for i in range(3)]

        tile_step(even, slow, coarse_coefs, coarse_step)

        def two_steps(_, inner):
            tile_step(even, odd, fine_coefs, fine_step)
            tile_step(odd, even, fine_coefs, fine_step)
            return inner

        lax.fori_loop(0, FINE // 2, two_steps, 0)
        leading = me[0] == 0
        for c in range(2):
            for x in range(4):
                for j in range(TILES):
                    coarse_end = slow[c, x, j]
                    difference = even[c, x, j] - coarse_end
                    wide[w, c, x, rows_of(j), :] = jnp.where(leading, coarse_end + difference, difference)
        return carry

    lax.fori_loop(0, 2, block, 0)

    early = me[0] < GROUP
    for sub in range(GROUP):
        worker = jnp.where(early, sub, GROUP - 1 - sub)
        for c in range(2):
            for pair in range(2):
                for r in range(BLOCK):
                    windows[worker, c, pair, 8 * r : 8 * r + 8, :] = window_tile(wide, c, pair, sub, r, lane)

        @pl.when(worker == me[0] % GROUP)
        def _():
            for c in range(2):
                for pair in range(2):
                    for r in range(BLOCK):
                        rates_here[c, pair, 8 * r : 8 * r + 8, :] = window_tile(
                            wide_rates, c, pair, sub, r, lane
                        )


def load_state(ref):
    return [[[ref[c, p, j] for j in range(BLOCK)] for p in range(2)] for c in range(2)]


def save_state(ref, state):
    for c in range(2):
        for p in range(2):
            for j in range(BLOCK):
                ref[c, p, j] = state[c][p][j]


def neighbours(s, p, j, other):
    here = s[j]
    if p == 0:
        along_x = here + other[j]
    else:
        along_x = other[j] + roll(here, 64, 1)
    before = s[j - 1] if j > 0 else roll(s[BLOCK - 1], 1, 0)
    after = s[j + 1] if j < BLOCK - 1 else roll(s[0], -1, 0)
    along_z = roll(here, 1, 1) + roll(here, -1, 1)
    return (along_x + (before + after)) + along_z


def step(state, coefs, which, length):
    a, b = state
    new_a = [[None] * BLOCK, [None] * BLOCK]
    new_b = [[None] * BLOCK, [None] * BLOCK]
    for p in range(2):
        for j in range(BLOCK):
            here_a, here_b = a[p][j], b[p][j]
            product = length * (here_a * here_b * here_b)
            near_a = neighbours(a[p], p, j, a[1 - p])
            near_b = neighbours(b[p], p, j, b[1 - p])
            keep_a = coefs[which, 0, p, j]
            gain = coefs[which, 1, p, j]
            keep_b = coefs[which, 2, p, j]
            new_a[p][j] = here_a * keep_a + (length * spread_fast) * near_a + (gain - product)
            new_b[p][j] = here_b * keep_b + (length * spread_slow) * near_b + product
    return [new_a, new_b]


def combine(op, left, right):
    return [[[op(left[c][p][j], right[c][p][j]) for j in range(BLOCK)] for p in range(2)] for c in range(2)]


def add(left, right):
    return combine(lambda l, r: l + r, left, right)


def subtract(left, right):
    return combine(lambda l, r: l - r, left, right)


def rows_of(j):
    return pl.ds(j, 8, stride=BLOCK)


def load_window(ref):
    return [[[ref[c, p, rows_of(j), :] for j in range(BLOCK)] for p in range(2)] for c in range(2)]


def save_coefs(coefs, rates):
    for p in range(2):
        for j in range(BLOCK):
            feed = rates[0, p, rows_of(j), :]
            kill = rates[1, p, rows_of(j), :]
            for which, length in enumerate((fine_step, coarse_step)):
                for i, value in enumerate(coefs_from(feed, kill, length)):
                    coefs[which, i, p, j] = value


def fine(state, coefs):
    for _ in range(FINE):
        state = step(state, coefs, 0, fine_step)
    return state


def coarse(state, coefs):
    return step(state, coefs, 1, coarse_step)


def put(out, rows, m, state):
    lane = lane_index()
    for c in range(2):
        for j in range(BLOCK):
            outer, inner = state[c][0][j], state[c][1][j]
            low = jnp.where(lane < 32, roll(outer, -16, 1), roll(inner, 16, 1))
            high = jnp.where(lane < 96, roll(inner, -16, 1), roll(outer, 16, 1))
            rows[c, rows_of(j), :] = jnp.where(lane < 64, low, high)
        out[m, c] = rows[c, MARGIN : MARGIN + ROWS, :]


def sweep(first, windows, coefs, starts, coarse_ends):
    def turn(m, carry):
        end = coarse(load_state(starts.at[m]), coefs)
        save_state(coarse_ends.at[m], end)
        save_state(starts.at[m + 1], add(end, load_window(windows.at[m])))
        return carry

    lax.fori_loop(first, GROUP, turn, 0)


def second_terms(first, coefs, starts, coarse_ends):
    def turn(m, carry):
        end = fine(load_state(starts.at[m]), coefs)
        save_state(starts.at[m], subtract(end, load_state(coarse_ends.at[m])))
        return carry

    lax.fori_loop(first, GROUP, turn, 0)


def second_sweep(first, coefs, current, terms, rows, out):
    def turn(m, carry):
        state = add(coarse(load_state(current), coefs), load_state(terms.at[m]))
        put(out, rows, m, state)
        save_state(current, state)
        return carry

    lax.fori_loop(first, GROUP, turn, 0)


def pack(sent, which, kept, state):
    begin = MARGIN + (ROWS - SENT[which]) // 2
    for c in range(2):
        for p in range(2):
            for j in range(BLOCK):
                kept[c, p, rows_of(j), :] = state[c][p][j]
            sent[c, p] = kept[c, p, begin : begin + SENT[which], :]


def unpack(sent, which, kept, target):
    begin = MARGIN + (ROWS - SENT[which]) // 2
    for c in range(2):
        for p in range(2):
            kept[c, p, begin : begin + SENT[which], :] = sent[c, p]
    save_state(target, load_window(kept))


def early_kernel(
    me, windows, rates, ends, sent_one, sent_two, coefs, starts, coarse_ends, current, rows, kept
):
    @pl.when(me[0] < GROUP)
    def _():
        save_coefs(coefs, rates)
        save_state(starts.at[1], load_window(windows.at[0]))
        sweep(1, windows, coefs, starts, coarse_ends)
        put(ends, rows, 0, load_state(starts.at[1]))
        pack(sent_one, 0, kept, load_state(starts.at[GROUP]))
        second_terms(1, coefs, starts, coarse_ends)
        state = add(load_state(coarse_ends.at[1]), load_state(starts.at[1]))
        put(ends, rows, 1, state)
        save_state(current, state)
        second_sweep(2, coefs, current, starts, rows, ends)
        pack(sent_two, 1, kept, load_state(current))


def late_terms_kernel(me, windows, rates, received, after, terms, coefs, starts, coarse_ends, kept):
    del after

    @pl.when(me[0] >= GROUP)
    def _():
        save_coefs(coefs, rates)
        kept[...] = jnp.zeros_like(kept)
        unpack(received, 0, kept, starts.at[0])
        sweep(0, windows, coefs, starts, coarse_ends)
        second_terms(0, coefs, starts, coarse_ends)
        for m in range(GROUP):
            terms[m] = starts[m]


def late_ends_kernel(me, terms, rates, received, early_ends, ends, coefs, current, rows, kept):
    @pl.when(me[0] < GROUP)
    def _():
        for m in range(GROUP):
            ends[m] = early_ends[m]

    @pl.when(me[0] >= GROUP)
    def _():
        save_coefs(coefs, rates)
        kept[...] = jnp.zeros_like(kept)
        unpack(received, 1, kept, current)
        second_sweep(0, coefs, current, terms, rows, ends)


def merge_kernel(me, parts, out):
    lane = lane_index()
    early = me[0] < GROUP
    workers = [jnp.where(early, sub, GROUP - 1 - sub) for sub in range(GROUP)]
    for c in range(2):
        for r in range(ROWS // 8):
            rows = slice(8 * r, 8 * r + 8)
            strips = [parts[workers[sub], c, rows, :] for sub in range(GROUP)]
            for x in range(4):
                blocks = [roll(strips[sub], SUB * (sub - x), 1) for sub in range(GROUP)]
                low = jnp.where(lane < 32, blocks[0], blocks[1])
                high = jnp.where(lane < 96, blocks[2], blocks[3])
                out[c, x, rows, :] = jnp.where(lane < 64, low, high)


def call(kernel, shapes, scratch=(), scalars=0, unread=0):
    vmem = pl.BlockSpec(memory_space=pltpu.VMEM)
    smem = pl.BlockSpec(memory_space=pltpu.SMEM)
    anywhere = pl.BlockSpec(memory_space=pl.ANY)

    def run(*args):
        read = len(args) - scalars - unread
        return pl.pallas_call(
            kernel,
            out_shape=[jax.ShapeDtypeStruct(s, jnp.float32) for s in shapes],
            in_specs=[smem] * scalars + [vmem] * read + [anywhere] * unread,
            out_specs=[vmem] * len(shapes),
            scratch_shapes=list(scratch),
            compiler_params=pltpu.CompilerParams(vmem_limit_bytes=32 * 1024 * 1024),
        )(*args)

    return run


def swap(block, axis, begin):
    count = lax.axis_size(axis)
    route = []
    for i in range(begin, begin + count, 2):
        a, b = i % count, (i + 1) % count
        route += [(a, b), (b, a)]
    return lax.ppermute(block, axis, route)


def edge(blocks, begin):
    return jnp.stack([lax.dynamic_slice_in_dim(block, begin, HALO, 2) for block in blocks])


def per_device(iterate, rates):
    state = iterate[0]
    slice_index = GROUP * lax.axis_index("th") + lax.axis_index("tl")
    gy, gz = lax.axis_index("gy"), lax.axis_index("gz")
    me = jnp.stack([slice_index, gy, gz]).astype(jnp.int32)
    odd = gy % 2
    two = edge((state, rates), odd * (ROWS - HALO))
    one = edge((state, rates), (1 - odd) * (ROWS - HALO))
    y_two = swap(two, "gy", 1)
    y_one = swap(one, "gy", 0)
    strip = (2, EXT, LANES)
    two, one = call(strips_kernel, [strip, strip], scalars=1)(me, state, rates, y_two, y_one)
    z_two = swap(two, "gz", 1)
    z_one = swap(one, "gz", 0)
    tile_state = pltpu.VMEM((2, 4, TILES, 8, LANES), jnp.float32)
    windows, rates_here = call(
        first_kernel,
        [(GROUP, 2, 2, WIN, LANES), (2, 2, WIN, LANES)],
        scratch=[
            pltpu.VMEM((2, 2, 4, EXT, LANES), jnp.float32),
            pltpu.VMEM((2, 2, 4, EXT, LANES), jnp.float32),
            pltpu.VMEM((3, 4, TILES, 8, LANES), jnp.float32),
            tile_state,
            tile_state,
            tile_state,
        ],
        scalars=1,
    )(me, state, rates, y_two, y_one, z_two, z_one)
    windows = lax.all_to_all(windows, "tl", 0, 0)

    states = (2, 2, BLOCK, 8, LANES)
    coefs = pltpu.VMEM((2, 3, *states[1:]), jnp.float32)
    starts = pltpu.VMEM((GROUP + 1, *states), jnp.float32)
    coarse_ends = pltpu.VMEM((GROUP, *states), jnp.float32)
    current = pltpu.VMEM(states, jnp.float32)
    rows = pltpu.VMEM((2, WIN, LANES), jnp.float32)
    kept = pltpu.VMEM((2, 2, WIN, LANES), jnp.float32)
    ends_shape = (GROUP, 2, ROWS, LANES)
    early_ends, sent_one, sent_two = call(
        early_kernel,
        [ends_shape] + [(2, 2, count, LANES) for count in SENT],
        scratch=[coefs, starts, coarse_ends, current, rows, kept],
        scalars=1,
    )(me, windows, rates_here)
    last = 2 * GROUP - 1
    route = [(t, last - t) for t in range(GROUP)]
    received_one = lax.ppermute(sent_one, ("th", "tl"), route)
    received_two = lax.ppermute(sent_two, ("th", "tl"), route)

    def hand_back(ends):
        return lax.all_to_all(ends, "tl", 0, 0)

    def leave(ends):
        return ends

    early = slice_index < GROUP
    ends = lax.cond(early, hand_back, leave, early_ends)
    (terms,) = call(
        late_terms_kernel, [(GROUP, *states)], scratch=[coefs, starts, coarse_ends, kept], scalars=1, unread=1
    )(me, windows, rates_here, received_one, ends)
    (ends,) = call(late_ends_kernel, [ends_shape], scratch=[coefs, current, rows, kept], scalars=1)(
        me, terms, rates_here, received_two, ends
    )
    ends = lax.cond(early, leave, hand_back, ends)
    (out,) = call(merge_kernel, [(2, 4, ROWS, LANES)], scalars=1)(me, ends)
    return out[None]


def solution(mesh):
    shape = mesh.devices.shape
    split = Mesh(mesh.devices.reshape(shape[0] // GROUP, GROUP, *shape[1:]), ("th", "tl", "gy", "gz"))
    return jax.shard_map(
        per_device,
        mesh=split,
        in_specs=(P(("th", "tl"), None, None, "gy", "gz"), P(None, None, "gy", "gz")),
        out_specs=P(("th", "tl"), None, None, "gy", "gz"),
        check_vma=False,
    )
```

```python
import jax
import jax.numpy as jnp
from jax import lax
from jax.experimental import pallas as pl
from jax.experimental.pallas import tpu as pltpu
from jax.sharding import Mesh
from jax.sharding import PartitionSpec as P

FINE = 4
GROUP = 4
HALO = 16
SUB = 32
ROWS = 64
MARGIN = 12
WIN = ROWS + 2 * MARGIN
SENT = 80
LANES = 128
EXT = ROWS + 2 * HALO
TILES = EXT // 8
BLOCK = WIN // 8

spread_fast = 0.2
spread_slow = 0.1
fine_step = 0.125
coarse_step = 0.5

PAIRS = ((0, 3), (1, 2))


def lane_index():
    return lax.broadcasted_iota(jnp.int32, (8, LANES), 1)


def roll(block, shift, axis):
    shift = shift % block.shape[axis]
    return block if shift == 0 else pltpu.roll(block, shift, axis)


def pick(even, if_even, if_odd):
    return jnp.where(even, if_even, if_odd)


def ext_tile(one, two, own, even, index):
    if index < 2:
        rows = slice(8 * index, 8 * index + 8)
        return pick(even, two[rows, :], one[rows, :])
    if index < 10:
        return own[8 * (index - 2) : 8 * (index - 2) + 8, :]
    rows = slice(8 * (index - 10), 8 * (index - 10) + 8)
    return pick(even, one[rows, :], two[rows, :])


def strips_kernel(me, state, rates, y_two, y_one, two, one):
    lane = lane_index()
    even_y = me[1] % 2 == 0
    even_z = me[2] % 2 == 0
    for which, source in enumerate((state, rates)):
        for tile in range(TILES):
            first = jnp.zeros((8, LANES), jnp.float32)
            last = jnp.zeros((8, LANES), jnp.float32)
            for k in range(8):
                c, x = k // 4, k % 4
                rows = ext_tile(y_one.at[which, c, x], y_two.at[which, c, x], source.at[c, x], even_y, tile)
                here = (lane >= 16 * k) & (lane < 16 * k + 16)
                first = jnp.where(here, roll(rows, 16 * k, 1), first)
                last = jnp.where(here, roll(rows, 16 * k + 16, 1), last)
            one[which, 8 * tile : 8 * tile + 8, :] = pick(even_z, last, first)
            two[which, 8 * tile : 8 * tile + 8, :] = pick(even_z, first, last)


def lay_out(own, y_one, y_two, z_one, z_two, even_y, even_z, wide, lane):
    for tile in range(TILES):
        rows = slice(8 * tile, 8 * tile + 8)
        near, far = z_one[rows, :], z_two[rows, :]
        left = pick(even_z, far, near)
        right = pick(even_z, near, far)
        for k in range(8):
            c, x = k // 4, k % 4
            here = ext_tile(y_one.at[c, x], y_two.at[c, x], own.at[c, x], even_y, tile)
            wide[0, c, x, rows, :] = jnp.where(lane < 16, roll(left, -16 * k, 1), roll(here, 16, 1))
            wide[1, c, x, rows, :] = jnp.where(lane >= 112, roll(right, 112 - 16 * k, 1), roll(here, -16, 1))


def window_tile(wide, c, pair, sub, r, lane):
    block, moved = ((0, 0), (1, 0), (0, 1), (1, 1))[sub]
    begin = HALO - MARGIN + 8 * r
    parts = [wide[block, c, x, begin : begin + 8, :] for x in PAIRS[pair]]
    parts[1 - moved] = roll(parts[1 - moved], 64, 1)
    return jnp.where(lane < 64, parts[0], parts[1])


def tile_step(source, target, coefs_of, length):
    for x in range(4):
        for j in range(TILES):
            keep_a, gain, keep_b = coefs_of(x, j)
            here = [source[c, x, j] for c in range(2)]
            near = []
            for c in range(2):
                below = source[c, max(x - 1, 0), j]
                above = source[c, min(x + 1, 3), j]
                before = source[c, x, j - 1] if j > 0 else roll(source[c, x, TILES - 1], 1, 0)
                after = source[c, x, j + 1] if j < TILES - 1 else roll(source[c, x, 0], -1, 0)
                along_z = roll(here[c], 1, 1) + roll(here[c], -1, 1)
                near.append(((below + above) + (before + after)) + along_z)
            a, b = here
            product = length * (a * b * b)
            target[0, x, j] = a * keep_a + (length * spread_fast) * near[0] + (gain - product)
            target[1, x, j] = b * keep_b + (length * spread_slow) * near[1] + product


def coefs_from(feed, kill, length):
    gain = length * feed
    keep_a = (1.0 - 6.0 * spread_fast * length) - gain
    keep_b = (1.0 - 6.0 * spread_slow * length) - length * (feed + kill)
    return keep_a, gain, keep_b


def first_kernel(
    me, state, rates, y_two, y_one, z_two, z_one, windows, rates_here, wide, wide_rates, coefs, even, odd, slow
):
    lane = lane_index()
    even_y = me[1] % 2 == 0
    even_z = me[2] % 2 == 0
    for which, source, target in ((0, state, wide), (1, rates, wide_rates)):
        lay_out(
            source,
            y_one.at[which],
            y_two.at[which],
            z_one.at[which],
            z_two.at[which],
            even_y,
            even_z,
            target,
            lane,
        )

    def rows_of(j):
        return pl.ds(j, 8, stride=TILES)

    def block(w, carry):
        for x in range(4):
            for j in range(TILES):
                feed = wide_rates[w, 0, x, rows_of(j), :]
                kill = wide_rates[w, 1, x, rows_of(j), :]
                for i, value in enumerate(coefs_from(feed, kill, fine_step)):
                    coefs[i, x, j] = value
                for c in range(2):
                    even[c, x, j] = wide[w, c, x, rows_of(j), :]

        def coarse_coefs(x, j):
            feed = wide_rates[w, 0, x, rows_of(j), :]
            kill = wide_rates[w, 1, x, rows_of(j), :]
            return coefs_from(feed, kill, coarse_step)

        def fine_coefs(x, j):
            return [coefs[i, x, j] for i in range(3)]

        tile_step(even, slow, coarse_coefs, coarse_step)

        def two_steps(_, inner):
            tile_step(even, odd, fine_coefs, fine_step)
            tile_step(odd, even, fine_coefs, fine_step)
            return inner

        lax.fori_loop(0, FINE // 2, two_steps, 0)
        leading = me[0] == 0
        for c in range(2):
            for x in range(4):
                for j in range(TILES):
                    coarse_end = slow[c, x, j]
                    difference = even[c, x, j] - coarse_end
                    wide[w, c, x, rows_of(j), :] = jnp.where(leading, coarse_end + difference, difference)
        return carry

    lax.fori_loop(0, 2, block, 0)

    early = me[0] < GROUP
    for sub in range(GROUP):
        worker = jnp.where(early, sub, GROUP - 1 - sub)
        for c in range(2):
            for pair in range(2):
                for r in range(BLOCK):
                    windows[worker, c, pair, 8 * r : 8 * r + 8, :] = window_tile(wide, c, pair, sub, r, lane)

        @pl.when(worker == me[0] % GROUP)
        def _():
            for c in range(2):
                for pair in range(2):
                    for r in range(BLOCK):
                        rates_here[c, pair, 8 * r : 8 * r + 8, :] = window_tile(
                            wide_rates, c, pair, sub, r, lane
                        )


def load_state(ref):
    return [[[ref[c, p, j] for j in range(BLOCK)] for p in range(2)] for c in range(2)]


def save_state(ref, state):
    for c in range(2):
        for p in range(2):
            for j in range(BLOCK):
                ref[c, p, j] = state[c][p][j]


def neighbours(s, p, j, other):
    here = s[j]
    if p == 0:
        along_x = here + other[j]
    else:
        along_x = other[j] + roll(here, 64, 1)
    before = s[j - 1] if j > 0 else roll(s[BLOCK - 1], 1, 0)
    after = s[j + 1] if j < BLOCK - 1 else roll(s[0], -1, 0)
    along_z = roll(here, 1, 1) + roll(here, -1, 1)
    return (along_x + (before + after)) + along_z


def step(state, coefs, which, length):
    a, b = state
    new_a = [[None] * BLOCK, [None] * BLOCK]
    new_b = [[None] * BLOCK, [None] * BLOCK]
    for p in range(2):
        for j in range(BLOCK):
            here_a, here_b = a[p][j], b[p][j]
            product = length * (here_a * here_b * here_b)
            near_a = neighbours(a[p], p, j, a[1 - p])
            near_b = neighbours(b[p], p, j, b[1 - p])
            keep_a = coefs[which, 0, p, j]
            gain = coefs[which, 1, p, j]
            keep_b = coefs[which, 2, p, j]
            new_a[p][j] = here_a * keep_a + (length * spread_fast) * near_a + (gain - product)
            new_b[p][j] = here_b * keep_b + (length * spread_slow) * near_b + product
    return [new_a, new_b]


def combine(op, left, right):
    return [[[op(left[c][p][j], right[c][p][j]) for j in range(BLOCK)] for p in range(2)] for c in range(2)]


def add(left, right):
    return combine(lambda l, r: l + r, left, right)


def subtract(left, right):
    return combine(lambda l, r: l - r, left, right)


def rows_of(j):
    return pl.ds(j, 8, stride=BLOCK)


def load_window(ref):
    return [[[ref[c, p, rows_of(j), :] for j in range(BLOCK)] for p in range(2)] for c in range(2)]


def save_coefs(coefs, rates):
    for p in range(2):
        for j in range(BLOCK):
            feed = rates[0, p, rows_of(j), :]
            kill = rates[1, p, rows_of(j), :]
            for which, length in enumerate((fine_step, coarse_step)):
                for i, value in enumerate(coefs_from(feed, kill, length)):
                    coefs[which, i, p, j] = value


def fine(state, coefs):
    for _ in range(FINE):
        state = step(state, coefs, 0, fine_step)
    return state


def coarse(state, coefs):
    return step(state, coefs, 1, coarse_step)


def put(out, rows, m, state):
    lane = lane_index()
    for c in range(2):
        for j in range(BLOCK):
            outer, inner = state[c][0][j], state[c][1][j]
            low = jnp.where(lane < 32, roll(outer, -16, 1), roll(inner, 16, 1))
            high = jnp.where(lane < 96, roll(inner, -16, 1), roll(outer, 16, 1))
            rows[c, rows_of(j), :] = jnp.where(lane < 64, low, high)
        out[m, c] = rows[c, MARGIN : MARGIN + ROWS, :]


def sweep(first, windows, coefs, starts, coarse_ends):
    def turn(m, carry):
        end = coarse(load_state(starts.at[m]), coefs)
        save_state(coarse_ends.at[m], end)
        save_state(starts.at[m + 1], add(end, load_window(windows.at[m])))
        return carry

    lax.fori_loop(first, GROUP, turn, 0)


def second_terms(first, coefs, starts, coarse_ends):
    def turn(m, carry):
        end = fine(load_state(starts.at[m]), coefs)
        save_state(starts.at[m], subtract(end, load_state(coarse_ends.at[m])))
        return carry

    lax.fori_loop(first, GROUP, turn, 0)


def second_sweep(first, coefs, current, terms, rows, out):
    def turn(m, carry):
        state = add(coarse(load_state(current), coefs), load_state(terms.at[m]))
        put(out, rows, m, state)
        save_state(current, state)
        return carry

    lax.fori_loop(first, GROUP, turn, 0)


def between(lane, begin, end):
    return (lane >= begin) & (lane < end)


def pack(sent, one, two):
    lane = lane_index()
    begin = MARGIN + (ROWS - SENT) // 2
    for r in range(SENT // 8):
        rows = slice(8 * r, 8 * r + 8)
        there = slice(begin + 8 * r, begin + 8 * r + 8)
        for k in range(4):
            second = two[k // 2, k % 2, there, :]
            half = k % 2
            first = roll(one[0, k // 2, there, :], 93 - (64 * half + 9), 1)
            block = jnp.where(between(lane, 52, 92), roll(second, -24, 1), first)
            sent[k, rows, :] = jnp.where(between(lane, 12, 52), second, block)
        for p in range(2):
            sent[4 + p, rows, :] = one[1, p, there, :]


def unpack(sent, one, two):
    lane = lane_index()
    begin = MARGIN + (ROWS - SENT) // 2
    for r in range(SENT // 8):
        rows = slice(8 * r, 8 * r + 8)
        there = slice(begin + 8 * r, begin + 8 * r + 8)
        blocks = [sent[k, rows, :] for k in range(4)]
        for k in range(4):
            two[k // 2, k % 2, there, :] = jnp.where(lane < 64, blocks[k], roll(blocks[k], 24, 1))
        for p in range(2):
            low, high = roll(blocks[2 * p], 9 - 93, 1), roll(blocks[2 * p + 1], 64 + 9 - 93, 1)
            one[0, p, there, :] = jnp.where(lane < 64, low, high)
            one[1, p, there, :] = sent[4 + p, rows, :]


def save_window(ref, state):
    for c in range(2):
        for p in range(2):
            for j in range(BLOCK):
                ref[c, p, rows_of(j), :] = state[c][p][j]


def early_kernel(me, windows, rates, ends, sent, coefs, starts, coarse_ends, current, rows, one, two):
    @pl.when(me[0] < GROUP)
    def _():
        save_coefs(coefs, rates)
        save_state(starts.at[1], load_window(windows.at[0]))
        sweep(1, windows, coefs, starts, coarse_ends)
        put(ends, rows, 0, load_state(starts.at[1]))
        save_window(one, load_state(starts.at[GROUP]))
        second_terms(1, coefs, starts, coarse_ends)
        state = add(load_state(coarse_ends.at[1]), load_state(starts.at[1]))
        put(ends, rows, 1, state)
        save_state(current, state)
        second_sweep(2, coefs, current, starts, rows, ends)
        save_window(two, load_state(current))
        pack(sent, one, two)


def late_kernel(
    me, windows, rates, received, early_ends, ends, coefs, starts, coarse_ends, current, rows, one, two
):
    @pl.when(me[0] < GROUP)
    def _():
        for m in range(GROUP):
            ends[m] = early_ends[m]

    @pl.when(me[0] >= GROUP)
    def _():
        save_coefs(coefs, rates)
        one[...] = jnp.zeros_like(one)
        two[...] = jnp.zeros_like(two)
        unpack(received, one, two)
        save_state(starts.at[0], load_window(one))
        save_state(current, load_window(two))
        sweep(0, windows, coefs, starts, coarse_ends)
        second_terms(0, coefs, starts, coarse_ends)
        second_sweep(0, coefs, current, starts, rows, ends)


def merge_kernel(me, parts, out):
    lane = lane_index()
    early = me[0] < GROUP
    workers = [jnp.where(early, sub, GROUP - 1 - sub) for sub in range(GROUP)]
    for c in range(2):
        for r in range(ROWS // 8):
            rows = slice(8 * r, 8 * r + 8)
            strips = [parts[workers[sub], c, rows, :] for sub in range(GROUP)]
            for x in range(4):
                blocks = [roll(strips[sub], SUB * (sub - x), 1) for sub in range(GROUP)]
                low = jnp.where(lane < 32, blocks[0], blocks[1])
                high = jnp.where(lane < 96, blocks[2], blocks[3])
                out[c, x, rows, :] = jnp.where(lane < 64, low, high)


def call(kernel, shapes, scratch=(), scalars=0):
    vmem = pl.BlockSpec(memory_space=pltpu.VMEM)
    smem = pl.BlockSpec(memory_space=pltpu.SMEM)

    def run(*args):
        return pl.pallas_call(
            kernel,
            out_shape=[jax.ShapeDtypeStruct(s, jnp.float32) for s in shapes],
            in_specs=[smem] * scalars + [vmem] * (len(args) - scalars),
            out_specs=[vmem] * len(shapes),
            scratch_shapes=list(scratch),
            compiler_params=pltpu.CompilerParams(vmem_limit_bytes=32 * 1024 * 1024),
        )(*args)

    return run


def swap(block, axis, begin):
    count = lax.axis_size(axis)
    route = []
    for i in range(begin, begin + count, 2):
        a, b = i % count, (i + 1) % count
        route += [(a, b), (b, a)]
    return lax.ppermute(block, axis, route)


def edge(blocks, begin):
    return jnp.stack([lax.dynamic_slice_in_dim(block, begin, HALO, 2) for block in blocks])


def per_device(iterate, rates):
    state = iterate[0]
    slice_index = GROUP * lax.axis_index("th") + lax.axis_index("tl")
    gy, gz = lax.axis_index("gy"), lax.axis_index("gz")
    me = jnp.stack([slice_index, gy, gz]).astype(jnp.int32)
    odd = gy % 2
    two = edge((state, rates), odd * (ROWS - HALO))
    one = edge((state, rates), (1 - odd) * (ROWS - HALO))
    y_two = swap(two, "gy", 1)
    y_one = swap(one, "gy", 0)
    strip = (2, EXT, LANES)
    two, one = call(strips_kernel, [strip, strip], scalars=1)(me, state, rates, y_two, y_one)
    z_two = swap(two, "gz", 1)
    z_one = swap(one, "gz", 0)
    tile_state = pltpu.VMEM((2, 4, TILES, 8, LANES), jnp.float32)
    windows, rates_here = call(
        first_kernel,
        [(GROUP, 2, 2, WIN, LANES), (2, 2, WIN, LANES)],
        scratch=[
            pltpu.VMEM((2, 2, 4, EXT, LANES), jnp.float32),
            pltpu.VMEM((2, 2, 4, EXT, LANES), jnp.float32),
            pltpu.VMEM((3, 4, TILES, 8, LANES), jnp.float32),
            tile_state,
            tile_state,
            tile_state,
        ],
        scalars=1,
    )(me, state, rates, y_two, y_one, z_two, z_one)
    windows = lax.all_to_all(windows, "tl", 0, 0)

    states = (2, 2, BLOCK, 8, LANES)
    coefs = pltpu.VMEM((2, 3, *states[1:]), jnp.float32)
    starts = pltpu.VMEM((GROUP + 1, *states), jnp.float32)
    coarse_ends = pltpu.VMEM((GROUP, *states), jnp.float32)
    current = pltpu.VMEM(states, jnp.float32)
    rows = pltpu.VMEM((2, WIN, LANES), jnp.float32)
    window = pltpu.VMEM((2, 2, WIN, LANES), jnp.float32)
    scratch = [coefs, starts, coarse_ends, current, rows, window, window]
    ends_shape = (GROUP, 2, ROWS, LANES)
    early_ends, sent = call(early_kernel, [ends_shape, (6, SENT, LANES)], scratch=scratch, scalars=1)(
        me, windows, rates_here
    )
    last = 2 * GROUP - 1
    received = lax.ppermute(sent, ("th", "tl"), [(t, last - t) for t in range(GROUP)])

    def hand_back(ends):
        return lax.all_to_all(ends, "tl", 0, 0)

    def leave(ends):
        return ends

    early = slice_index < GROUP
    ends = lax.cond(early, hand_back, leave, early_ends)
    (ends,) = call(late_kernel, [ends_shape], scratch=scratch, scalars=1)(
        me, windows, rates_here, received, ends
    )
    ends = lax.cond(early, leave, hand_back, ends)
    (out,) = call(merge_kernel, [(2, 4, ROWS, LANES)], scalars=1)(me, ends)
    return out[None]


def solution(mesh):
    shape = mesh.devices.shape
    split = Mesh(mesh.devices.reshape(shape[0] // GROUP, GROUP, *shape[1:]), ("th", "tl", "gy", "gz"))
    return jax.shard_map(
        per_device,
        mesh=split,
        in_specs=(P(("th", "tl"), None, None, "gy", "gz"), P(None, None, "gy", "gz")),
        out_specs=P(("th", "tl"), None, None, "gy", "gz"),
        check_vma=False,
    )
```

```python
import jax
import jax.numpy as jnp
from jax import lax
from jax.experimental import pallas as pl
from jax.experimental.pallas import tpu as pltpu
from jax.sharding import Mesh
from jax.sharding import PartitionSpec as P

FINE = 4
GROUP = 4
HALO = 16
SUB = 32
ROWS = 64
WIN = ROWS + 2 * 12
LATE_WIN = ROWS + 2 * 8
SENT_TWO = ROWS + 2 * 4
LANES = 128
EXT = ROWS + 2 * HALO
TILES = EXT // 8

spread_fast = 0.2
spread_slow = 0.1
fine_step = 0.125
coarse_step = 0.5

PAIRS = ((0, 3), (1, 2))


def lane_index():
    return lax.broadcasted_iota(jnp.int32, (8, LANES), 1)


def roll(block, shift, axis):
    shift = shift % block.shape[axis]
    return block if shift == 0 else pltpu.roll(block, shift, axis)


def pick(even, if_even, if_odd):
    return jnp.where(even, if_even, if_odd)


def ext_tile(one, two, own, even, index):
    if index < 2:
        rows = slice(8 * index, 8 * index + 8)
        return pick(even, two[rows, :], one[rows, :])
    if index < 10:
        return own[8 * (index - 2) : 8 * (index - 2) + 8, :]
    rows = slice(8 * (index - 10), 8 * (index - 10) + 8)
    return pick(even, one[rows, :], two[rows, :])


def strips_kernel(me, state, rates, y_two, y_one, two, one):
    lane = lane_index()
    even_y = me[1] % 2 == 0
    even_z = me[2] % 2 == 0
    for which, source in enumerate((state, rates)):
        for tile in range(TILES):
            first = jnp.zeros((8, LANES), jnp.float32)
            last = jnp.zeros((8, LANES), jnp.float32)
            for k in range(8):
                c, x = k // 4, k % 4
                rows = ext_tile(y_one.at[which, c, x], y_two.at[which, c, x], source.at[c, x], even_y, tile)
                here = (lane >= 16 * k) & (lane < 16 * k + 16)
                first = jnp.where(here, roll(rows, 16 * k, 1), first)
                last = jnp.where(here, roll(rows, 16 * k + 16, 1), last)
            one[which, 8 * tile : 8 * tile + 8, :] = pick(even_z, last, first)
            two[which, 8 * tile : 8 * tile + 8, :] = pick(even_z, first, last)


def lay_out(own, y_one, y_two, z_one, z_two, even_y, even_z, wide, lane):
    for tile in range(TILES):
        rows = slice(8 * tile, 8 * tile + 8)
        near, far = z_one[rows, :], z_two[rows, :]
        left = pick(even_z, far, near)
        right = pick(even_z, near, far)
        for k in range(8):
            c, x = k // 4, k % 4
            here = ext_tile(y_one.at[c, x], y_two.at[c, x], own.at[c, x], even_y, tile)
            wide[0, c, x, rows, :] = jnp.where(lane < 16, roll(left, -16 * k, 1), roll(here, 16, 1))
            wide[1, c, x, rows, :] = jnp.where(lane >= 112, roll(right, 112 - 16 * k, 1), roll(here, -16, 1))


def window_tile(wide, c, pair, sub, begin, lane):
    block, moved = ((0, 0), (1, 0), (0, 1), (1, 1))[sub]
    parts = [wide[block, c, x, begin : begin + 8, :] for x in PAIRS[pair]]
    parts[1 - moved] = roll(parts[1 - moved], 64, 1)
    return jnp.where(lane < 64, parts[0], parts[1])


def tile_step(source, target, coefs_of, length):
    for x in range(4):
        for j in range(TILES):
            keep_a, gain, keep_b = coefs_of(x, j)
            here = [source[c, x, j] for c in range(2)]
            near = []
            for c in range(2):
                below = source[c, max(x - 1, 0), j]
                above = source[c, min(x + 1, 3), j]
                before = source[c, x, j - 1] if j > 0 else roll(source[c, x, TILES - 1], 1, 0)
                after = source[c, x, j + 1] if j < TILES - 1 else roll(source[c, x, 0], -1, 0)
                along_z = roll(here[c], 1, 1) + roll(here[c], -1, 1)
                near.append(((below + above) + (before + after)) + along_z)
            a, b = here
            product = length * (a * b * b)
            target[0, x, j] = a * keep_a + (length * spread_fast) * near[0] + (gain - product)
            target[1, x, j] = b * keep_b + (length * spread_slow) * near[1] + product


def coefs_from(feed, kill, length):
    gain = length * feed
    keep_a = (1.0 - 6.0 * spread_fast * length) - gain
    keep_b = (1.0 - 6.0 * spread_slow * length) - length * (feed + kill)
    return keep_a, gain, keep_b


def first_kernel(
    me,
    state,
    rates,
    y_two,
    y_one,
    z_two,
    z_one,
    early_windows,
    late_windows,
    rates_here,
    wide,
    wide_rates,
    coefs,
    even,
    odd,
    slow,
):
    lane = lane_index()
    even_y = me[1] % 2 == 0
    even_z = me[2] % 2 == 0
    for which, source, target in ((0, state, wide), (1, rates, wide_rates)):
        lay_out(
            source,
            y_one.at[which],
            y_two.at[which],
            z_one.at[which],
            z_two.at[which],
            even_y,
            even_z,
            target,
            lane,
        )

    def rows_of(j):
        return pl.ds(j, 8, stride=TILES)

    def block(w, carry):
        for x in range(4):
            for j in range(TILES):
                feed = wide_rates[w, 0, x, rows_of(j), :]
                kill = wide_rates[w, 1, x, rows_of(j), :]
                for i, value in enumerate(coefs_from(feed, kill, fine_step)):
                    coefs[i, x, j] = value
                for c in range(2):
                    even[c, x, j] = wide[w, c, x, rows_of(j), :]

        def coarse_coefs(x, j):
            feed = wide_rates[w, 0, x, rows_of(j), :]
            kill = wide_rates[w, 1, x, rows_of(j), :]
            return coefs_from(feed, kill, coarse_step)

        def fine_coefs(x, j):
            return [coefs[i, x, j] for i in range(3)]

        tile_step(even, slow, coarse_coefs, coarse_step)

        def two_steps(_, inner):
            tile_step(even, odd, fine_coefs, fine_step)
            tile_step(odd, even, fine_coefs, fine_step)
            return inner

        lax.fori_loop(0, FINE // 2, two_steps, 0)
        leading = me[0] == 0
        for c in range(2):
            for x in range(4):
                for j in range(TILES):
                    coarse_end = slow[c, x, j]
                    difference = even[c, x, j] - coarse_end
                    wide[w, c, x, rows_of(j), :] = jnp.where(leading, coarse_end + difference, difference)
        return carry

    lax.fori_loop(0, 2, block, 0)

    def cut(source, sub, target):
        rows = target.shape[2]
        for c in range(2):
            for pair in range(2):
                for at in range(0, rows, 8):
                    begin = (EXT - rows) // 2 + at
                    target[c, pair, at : at + 8, :] = window_tile(source, c, pair, sub, begin, lane)

    @pl.when(me[0] < GROUP)
    def _():
        for sub in range(GROUP):
            cut(wide, sub, early_windows.at[sub])

    @pl.when(me[0] >= GROUP)
    def _():
        for sub in range(GROUP):
            cut(wide, sub, late_windows.at[GROUP - 1 - sub])

    worker = me[0] % GROUP
    for sub in range(GROUP):

        @pl.when(jnp.where(me[0] < GROUP, worker, GROUP - 1 - worker) == sub)
        def _():
            cut(wide_rates, sub, rates_here)


def over(op, count):
    return [[[op(c, p, j) for j in range(count)] for p in range(2)] for c in range(2)]


def load_state(ref):
    return over(lambda c, p, j: ref[c, p, j], ref.shape[2])


def save_state(ref, state):
    for c in range(2):
        for p in range(2):
            for j, value in enumerate(state[c][p]):
                ref[c, p, j] = value


def load_window(ref):
    block = ref.shape[2] // 8
    return over(lambda c, p, j: ref[c, p, pl.ds(j, 8, stride=block), :], block)


def save_window(ref, state):
    block = ref.shape[2] // 8
    for c in range(2):
        for p in range(2):
            for j, value in enumerate(state[c][p]):
                ref[c, p, pl.ds(j, 8, stride=block), :] = value


def combine(op, left, right):
    return over(lambda c, p, j: op(left[c][p][j], right[c][p][j]), len(left[0][0]))


def add(left, right):
    return combine(lambda l, r: l + r, left, right)


def subtract(left, right):
    return combine(lambda l, r: l - r, left, right)


def neighbours(s, p, j, other):
    here = s[j]
    if p == 0:
        along_x = here + other[j]
    else:
        along_x = other[j] + roll(here, 64, 1)
    before = s[j - 1] if j > 0 else roll(s[-1], 1, 0)
    after = s[j + 1] if j < len(s) - 1 else roll(s[0], -1, 0)
    along_z = roll(here, 1, 1) + roll(here, -1, 1)
    return (along_x + (before + after)) + along_z


def step(state, coefs, which, length):
    a, b = state
    new = [[[], []], [[], []]]
    for p in range(2):
        for j in range(len(a[p])):
            here_a, here_b = a[p][j], b[p][j]
            product = length * (here_a * here_b * here_b)
            near_a = neighbours(a[p], p, j, a[1 - p])
            near_b = neighbours(b[p], p, j, b[1 - p])
            keep_a = coefs[which, 0, p, j]
            gain = coefs[which, 1, p, j]
            keep_b = coefs[which, 2, p, j]
            new[0][p].append(here_a * keep_a + (length * spread_fast) * near_a + (gain - product))
            new[1][p].append(here_b * keep_b + (length * spread_slow) * near_b + product)
    return new


def save_coefs(coefs, rates, steps):
    block = coefs.shape[3]
    begin = (rates.shape[2] - 8 * block) // 2
    for p in range(2):
        for j in range(block):
            feed = rates[0, p, pl.ds(begin + j, 8, stride=block), :]
            kill = rates[1, p, pl.ds(begin + j, 8, stride=block), :]
            for which in steps:
                length = (fine_step, coarse_step)[which]
                for i, value in enumerate(coefs_from(feed, kill, length)):
                    coefs[which, i, p, j] = value


def fine(state, coefs):
    for _ in range(FINE):
        state = step(state, coefs, 0, fine_step)
    return state


def coarse(state, coefs):
    return step(state, coefs, 1, coarse_step)


def put(out, rows, m, state):
    lane = lane_index()
    block = len(state[0][0])
    begin = (8 * block - ROWS) // 2
    for c in range(2):
        for j in range(block):
            outer, inner = state[c][0][j], state[c][1][j]
            low = jnp.where(lane < 32, roll(outer, -16, 1), roll(inner, 16, 1))
            high = jnp.where(lane < 96, roll(inner, -16, 1), roll(outer, 16, 1))
            rows[c, pl.ds(j, 8, stride=block), :] = jnp.where(lane < 64, low, high)
        out[m, c] = rows[c, begin : begin + ROWS, :]


def sweep(first, windows, coefs, starts, coarse_ends):
    def turn(m, carry):
        end = coarse(load_state(starts.at[m]), coefs)
        save_state(coarse_ends.at[m], end)
        save_state(starts.at[m + 1], add(end, load_window(windows.at[m])))
        return carry

    lax.fori_loop(first, GROUP, turn, 0)


def second_terms(first, coefs, starts, coarse_ends, terms):
    def turn(m, carry):
        end = fine(load_state(starts.at[m]), coefs)
        save_state(terms.at[m], subtract(end, load_state(coarse_ends.at[m])))
        return carry

    lax.fori_loop(first, GROUP, turn, 0)


def second_sweep(first, coefs, current, terms, rows, out):
    def turn(m, carry):
        state = add(coarse(load_state(current), coefs), load_state(terms.at[m]))
        put(out, rows, m, state)
        save_state(current, state)
        return carry

    lax.fori_loop(first, GROUP, turn, 0)


def pack_two(sent, window):
    lane = lane_index()
    begin = (window.shape[2] - SENT_TWO) // 2
    for r in range(0, SENT_TWO, 8):
        for k in range(3):
            block = jnp.zeros((8, LANES), jnp.float32)
            for i in range(3):
                b = 3 * k + i
                if b < 8:
                    c, p, half = b // 4, b // 2 % 2, b % 2
                    rows = window[c, p, begin + r : begin + r + 8, :]
                    here = (lane >= 40 * i) & (lane < 40 * i + 40)
                    block = jnp.where(here, roll(rows, 40 * i - 12 - 64 * half, 1), block)
            sent[k, r : r + 8, :] = block


def unpack_two(sent, window):
    lane = lane_index()
    begin = (window.shape[2] - SENT_TWO) // 2
    for r in range(0, SENT_TWO, 8):
        for c in range(2):
            for p in range(2):
                halves = []
                for half in range(2):
                    b = 4 * c + 2 * p + half
                    rows = sent[b // 3, r : r + 8, :]
                    halves.append(roll(rows, 12 + 64 * half - 40 * (b % 3), 1))
                window[c, p, begin + r : begin + r + 8, :] = jnp.where(lane < 64, halves[0], halves[1])


def early_first_kernel(me, windows, rates, starts, coarse_ends, sent, coefs, window):
    @pl.when(me[0] < GROUP)
    def _():
        save_coefs(coefs, rates, (1,))
        save_state(starts.at[1], load_window(windows.at[0]))
        sweep(1, windows, coefs, starts, coarse_ends)
        save_window(window, load_state(starts.at[GROUP]))
        begin = (WIN - LATE_WIN) // 2
        for c in range(2):
            for p in range(2):
                sent[c, p] = window[c, p, begin : begin + LATE_WIN, :]


def early_second_kernel(me, starts, coarse_ends, rates, ends, sent, coefs, terms, current, rows, window):
    @pl.when(me[0] < GROUP)
    def _():
        save_coefs(coefs, rates, (0, 1))
        put(ends, rows, 0, load_state(starts.at[1]))
        second_terms(1, coefs, starts, coarse_ends, terms)
        state = add(load_state(coarse_ends.at[1]), load_state(terms.at[1]))
        put(ends, rows, 1, state)
        save_state(current, state)
        second_sweep(2, coefs, current, terms, rows, ends)
        save_window(window, load_state(current))
        pack_two(sent, window)


def late_first_kernel(me, windows, rates, received, terms, coefs, starts, coarse_ends):
    @pl.when(me[0] >= GROUP)
    def _():
        save_coefs(coefs, rates, (0, 1))
        save_state(starts.at[0], load_window(received))
        sweep(0, windows, coefs, starts, coarse_ends)
        second_terms(0, coefs, starts, coarse_ends, terms)


def late_second_kernel(me, terms, rates, received, early_ends, ends, coefs, current, rows, window):
    @pl.when(me[0] < GROUP)
    def _():
        for m in range(GROUP):
            ends[m] = early_ends[m]

    @pl.when(me[0] >= GROUP)
    def _():
        save_coefs(coefs, rates, (1,))
        window[...] = jnp.zeros_like(window)
        unpack_two(received, window)
        save_state(current, load_window(window))
        second_sweep(0, coefs, current, terms, rows, ends)


def merge_kernel(me, parts, out):
    lane = lane_index()
    early = me[0] < GROUP
    workers = [jnp.where(early, sub, GROUP - 1 - sub) for sub in range(GROUP)]
    for c in range(2):
        for r in range(ROWS // 8):
            rows = slice(8 * r, 8 * r + 8)
            strips = [parts[workers[sub], c, rows, :] for sub in range(GROUP)]
            for x in range(4):
                blocks = [roll(strips[sub], SUB * (sub - x), 1) for sub in range(GROUP)]
                low = jnp.where(lane < 32, blocks[0], blocks[1])
                high = jnp.where(lane < 96, blocks[2], blocks[3])
                out[c, x, rows, :] = jnp.where(lane < 64, low, high)


def call(kernel, shapes, scratch=(), scalars=0):
    vmem = pl.BlockSpec(memory_space=pltpu.VMEM)
    smem = pl.BlockSpec(memory_space=pltpu.SMEM)

    def run(*args):
        return pl.pallas_call(
            kernel,
            out_shape=[jax.ShapeDtypeStruct(s, jnp.float32) for s in shapes],
            in_specs=[smem] * scalars + [vmem] * (len(args) - scalars),
            out_specs=[vmem] * len(shapes),
            scratch_shapes=list(scratch),
            compiler_params=pltpu.CompilerParams(vmem_limit_bytes=32 * 1024 * 1024),
        )(*args)

    return run


def swap(block, axis, begin):
    count = lax.axis_size(axis)
    route = []
    for i in range(begin, begin + count, 2):
        a, b = i % count, (i + 1) % count
        route += [(a, b), (b, a)]
    return lax.ppermute(block, axis, route)


def edge(blocks, begin):
    return jnp.stack([lax.dynamic_slice_in_dim(block, begin, HALO, 2) for block in blocks])


def per_device(iterate, rates):
    state = iterate[0]
    slice_index = GROUP * lax.axis_index("th") + lax.axis_index("tl")
    gy, gz = lax.axis_index("gy"), lax.axis_index("gz")
    me = jnp.stack([slice_index, gy, gz]).astype(jnp.int32)
    odd = gy % 2
    two = edge((state, rates), odd * (ROWS - HALO))
    one = edge((state, rates), (1 - odd) * (ROWS - HALO))
    y_two = swap(two, "gy", 1)
    y_one = swap(one, "gy", 0)
    strip = (2, EXT, LANES)
    two, one = call(strips_kernel, [strip, strip], scalars=1)(me, state, rates, y_two, y_one)
    z_two = swap(two, "gz", 1)
    z_one = swap(one, "gz", 0)
    tile_state = pltpu.VMEM((2, 4, TILES, 8, LANES), jnp.float32)
    early_windows, late_windows, rates_here = call(
        first_kernel,
        [(GROUP, 2, 2, WIN, LANES), (GROUP, 2, 2, LATE_WIN, LANES), (2, 2, WIN, LANES)],
        scratch=[
            pltpu.VMEM((2, 2, 4, EXT, LANES), jnp.float32),
            pltpu.VMEM((2, 2, 4, EXT, LANES), jnp.float32),
            pltpu.VMEM((3, 4, TILES, 8, LANES), jnp.float32),
            tile_state,
            tile_state,
            tile_state,
        ],
        scalars=1,
    )(me, state, rates, y_two, y_one, z_two, z_one)

    def exchange(block):
        return lax.all_to_all(block, "tl", 0, 0)

    def leave(block):
        return block

    early = slice_index < GROUP
    last = 2 * GROUP - 1
    route = [(t, last - t) for t in range(GROUP)]

    def hand_over(block):
        return lax.ppermute(block, ("th", "tl"), route)

    def states_of(rows):
        return (2, 2, rows // 8, 8, LANES)

    def scratch_of(rows):
        coefs = pltpu.VMEM((2, 3, *states_of(rows)[1:]), jnp.float32)
        current = pltpu.VMEM(states_of(rows), jnp.float32)
        flat = pltpu.VMEM((2, rows, LANES), jnp.float32)
        window = pltpu.VMEM((2, 2, rows, LANES), jnp.float32)
        return coefs, current, flat, window

    coefs, current, flat, window = scratch_of(WIN)
    starts_shape, slices_shape = (GROUP + 1, *states_of(WIN)), (GROUP, *states_of(WIN))
    ends_shape = (GROUP, 2, ROWS, LANES)
    windows = lax.cond(early, exchange, leave, early_windows)
    starts, coarse_ends, sent = call(
        early_first_kernel,
        [starts_shape, slices_shape, (2, 2, LATE_WIN, LANES)],
        scratch=[coefs, window],
        scalars=1,
    )(me, windows, rates_here)
    received_one = hand_over(sent)
    ends, sent = call(
        early_second_kernel,
        [ends_shape, (3, SENT_TWO, LANES)],
        scratch=[coefs, pltpu.VMEM(slices_shape, jnp.float32), current, flat, window],
        scalars=1,
    )(me, starts, coarse_ends, rates_here)
    received_two = hand_over(sent)

    ends, windows = lax.cond(
        early, lambda e, w: (exchange(e), w), lambda e, w: (e, exchange(w)), ends, late_windows
    )
    coefs, current, flat, window = scratch_of(LATE_WIN)
    starts_shape, slices_shape = (GROUP + 1, *states_of(LATE_WIN)), (GROUP, *states_of(LATE_WIN))
    (terms,) = call(
        late_first_kernel,
        [slices_shape],
        scratch=[coefs, pltpu.VMEM(starts_shape, jnp.float32), pltpu.VMEM(slices_shape, jnp.float32)],
        scalars=1,
    )(me, windows, rates_here, received_one)
    (ends,) = call(late_second_kernel, [ends_shape], scratch=[coefs, current, flat, window], scalars=1)(
        me, terms, rates_here, received_two, ends
    )
    ends = lax.cond(early, leave, exchange, ends)
    (out,) = call(merge_kernel, [(2, 4, ROWS, LANES)], scalars=1)(me, ends)
    return out[None]


def solution(mesh):
    shape = mesh.devices.shape
    split = Mesh(mesh.devices.reshape(shape[0] // GROUP, GROUP, *shape[1:]), ("th", "tl", "gy", "gz"))
    return jax.shard_map(
        per_device,
        mesh=split,
        in_specs=(P(("th", "tl"), None, None, "gy", "gz"), P(None, None, "gy", "gz")),
        out_specs=P(("th", "tl"), None, None, "gy", "gz"),
        check_vma=False,
    )
```

```python
import jax
import jax.numpy as jnp
from jax import lax
from jax.experimental import pallas as pl
from jax.experimental.pallas import tpu as pltpu
from jax.sharding import Mesh
from jax.sharding import PartitionSpec as P

FINE = 4
GROUP = 4
HALO = 16
SUB = 32
ROWS = 64
WIN = ROWS + 2 * 12
LATE_WIN = ROWS + 2 * 8
SENT = LATE_WIN
LANES = 128
EXT = ROWS + 2 * HALO
TILES = EXT // 8

spread_fast = 0.2
spread_slow = 0.1
fine_step = 0.125
coarse_step = 0.5

PAIRS = ((0, 3), (1, 2))


def lane_index():
    return lax.broadcasted_iota(jnp.int32, (8, LANES), 1)


def roll(block, shift, axis):
    shift = shift % block.shape[axis]
    return block if shift == 0 else pltpu.roll(block, shift, axis)


def pick(even, if_even, if_odd):
    return jnp.where(even, if_even, if_odd)


def ext_tile(one, two, own, even, index):
    if index < 2:
        rows = slice(8 * index, 8 * index + 8)
        return pick(even, two[rows, :], one[rows, :])
    if index < 10:
        return own[8 * (index - 2) : 8 * (index - 2) + 8, :]
    rows = slice(8 * (index - 10), 8 * (index - 10) + 8)
    return pick(even, one[rows, :], two[rows, :])


def strips_kernel(me, state, rates, y_two, y_one, two, one):
    lane = lane_index()
    even_y = me[1] % 2 == 0
    even_z = me[2] % 2 == 0
    for which, source in enumerate((state, rates)):
        for tile in range(TILES):
            first = jnp.zeros((8, LANES), jnp.float32)
            last = jnp.zeros((8, LANES), jnp.float32)
            for k in range(8):
                c, x = k // 4, k % 4
                rows = ext_tile(y_one.at[which, c, x], y_two.at[which, c, x], source.at[c, x], even_y, tile)
                here = (lane >= 16 * k) & (lane < 16 * k + 16)
                first = jnp.where(here, roll(rows, 16 * k, 1), first)
                last = jnp.where(here, roll(rows, 16 * k + 16, 1), last)
            one[which, 8 * tile : 8 * tile + 8, :] = pick(even_z, last, first)
            two[which, 8 * tile : 8 * tile + 8, :] = pick(even_z, first, last)


def lay_out(own, y_one, y_two, z_one, z_two, even_y, even_z, wide, lane):
    for tile in range(TILES):
        rows = slice(8 * tile, 8 * tile + 8)
        near, far = z_one[rows, :], z_two[rows, :]
        left = pick(even_z, far, near)
        right = pick(even_z, near, far)
        for k in range(8):
            c, x = k // 4, k % 4
            here = ext_tile(y_one.at[c, x], y_two.at[c, x], own.at[c, x], even_y, tile)
            wide[0, c, x, rows, :] = jnp.where(lane >= 112, roll(left, 112 - 16 * k, 1), here)
            wide[1, c, x, rows, :] = jnp.where(lane < 16, roll(right, -16 * k, 1), here)


def window_tile(wide, c, pair, sub, begin, lane):
    block = (0, 1, 0, 1)[sub]
    low, high = [
        roll(wide[block, c, x, begin : begin + 8, :], 64 * half + HALO - SUB * sub, 1)
        for half, x in enumerate(PAIRS[pair])
    ]
    return jnp.where(lane < 64, low, high)


def tile_step(source, target, coefs_of, length):
    def row(j):
        return [[source[c, x, j % TILES] for x in range(4)] for c in range(2)]

    first, final = row(0), row(TILES - 1)
    before, here = final, first
    for j in range(TILES):
        after = (row(j + 1) if j < TILES - 2 else final) if j < TILES - 1 else first
        for x in range(4):
            near = []
            for c in range(2):
                lower = roll(before[c][x], 1, 0) if j == 0 else before[c][x]
                upper = roll(after[c][x], -1, 0) if j == TILES - 1 else after[c][x]
                along_x = here[c][max(x - 1, 0)] + here[c][min(x + 1, 3)]
                along_z = roll(here[c][x], 1, 1) + roll(here[c][x], -1, 1)
                near.append((along_x + (lower + upper)) + along_z)
            a, b = here[0][x], here[1][x]
            keep_a, gain, keep_b = coefs_of(x, j)
            product = length * (a * b * b)
            target[0, x, j] = a * keep_a + (length * spread_fast) * near[0] + (gain - product)
            target[1, x, j] = b * keep_b + (length * spread_slow) * near[1] + product
        before, here = here, after


def coefs_from(feed, kill, length):
    gain = length * feed
    keep_a = (1.0 - 6.0 * spread_fast * length) - gain
    keep_b = (1.0 - 6.0 * spread_slow * length) - length * (feed + kill)
    return keep_a, gain, keep_b


def first_kernel(
    me,
    state,
    rates,
    y_two,
    y_one,
    z_two,
    z_one,
    early_windows,
    late_windows,
    rates_here,
    wide,
    wide_rates,
    coefs,
    even,
    odd,
    slow,
):
    lane = lane_index()
    even_y = me[1] % 2 == 0
    even_z = me[2] % 2 == 0
    for which, source, target in ((0, state, wide), (1, rates, wide_rates)):
        lay_out(
            source,
            y_one.at[which],
            y_two.at[which],
            z_one.at[which],
            z_two.at[which],
            even_y,
            even_z,
            target,
            lane,
        )

    def rows_of(j):
        return pl.ds(j, 8, stride=TILES)

    def block(w, carry):
        for x in range(4):
            for j in range(TILES):
                feed = wide_rates[w, 0, x, rows_of(j), :]
                kill = wide_rates[w, 1, x, rows_of(j), :]
                for i, value in enumerate(coefs_from(feed, kill, fine_step)):
                    coefs[i, x, j] = value
                for c in range(2):
                    even[c, x, j] = wide[w, c, x, rows_of(j), :]

        def coarse_coefs(x, j):
            feed = wide_rates[w, 0, x, rows_of(j), :]
            kill = wide_rates[w, 1, x, rows_of(j), :]
            return coefs_from(feed, kill, coarse_step)

        def fine_coefs(x, j):
            return [coefs[i, x, j] for i in range(3)]

        tile_step(even, slow, coarse_coefs, coarse_step)

        def two_steps(_, inner):
            tile_step(even, odd, fine_coefs, fine_step)
            tile_step(odd, even, fine_coefs, fine_step)
            return inner

        lax.fori_loop(0, FINE // 2, two_steps, 0)
        leading = me[0] == 0
        for c in range(2):
            for x in range(4):
                for j in range(TILES):
                    coarse_end = slow[c, x, j]
                    difference = even[c, x, j] - coarse_end
                    wide[w, c, x, rows_of(j), :] = jnp.where(leading, coarse_end + difference, difference)
        return carry

    lax.fori_loop(0, 2, block, 0)

    def cut(source, sub, target):
        rows = target.shape[2]
        for c in range(2):
            for pair in range(2):
                for at in range(0, rows, 8):
                    begin = (EXT - rows) // 2 + at
                    target[c, pair, at : at + 8, :] = window_tile(source, c, pair, sub, begin, lane)

    @pl.when(me[0] < GROUP)
    def _():
        for sub in range(GROUP):
            cut(wide, sub, early_windows.at[sub])

    @pl.when(me[0] >= GROUP)
    def _():
        for sub in range(GROUP):
            cut(wide, sub, late_windows.at[GROUP - 1 - sub])

    worker = me[0] % GROUP
    for sub in range(GROUP):

        @pl.when(jnp.where(me[0] < GROUP, worker, GROUP - 1 - worker) == sub)
        def _():
            cut(wide_rates, sub, rates_here)


def over(op, count):
    return [[[op(c, p, j) for j in range(count)] for p in range(2)] for c in range(2)]


def load_state(ref):
    return over(lambda c, p, j: ref[c, p, j], ref.shape[2])


def save_state(ref, state):
    for c in range(2):
        for p in range(2):
            for j, value in enumerate(state[c][p]):
                ref[c, p, j] = value


def load_window(ref):
    block = ref.shape[2] // 8
    return over(lambda c, p, j: ref[c, p, pl.ds(j, 8, stride=block), :], block)


def save_window(ref, state):
    block = ref.shape[2] // 8
    for c in range(2):
        for p in range(2):
            for j, value in enumerate(state[c][p]):
                ref[c, p, pl.ds(j, 8, stride=block), :] = value


def combine(op, left, right):
    return over(lambda c, p, j: op(left[c][p][j], right[c][p][j]), len(left[0][0]))


def add(left, right):
    return combine(lambda l, r: l + r, left, right)


def subtract(left, right):
    return combine(lambda l, r: l - r, left, right)


def neighbours(s, p, j, other):
    here = s[j]
    if p == 0:
        along_x = here + other[j]
    else:
        along_x = other[j] + roll(here, 64, 1)
    before = s[j - 1] if j > 0 else roll(s[-1], 1, 0)
    after = s[j + 1] if j < len(s) - 1 else roll(s[0], -1, 0)
    along_z = roll(here, 1, 1) + roll(here, -1, 1)
    return (along_x + (before + after)) + along_z


def step(state, coefs, which, length):
    a, b = state
    new = [[[], []], [[], []]]
    for p in range(2):
        for j in range(len(a[p])):
            here_a, here_b = a[p][j], b[p][j]
            product = length * (here_a * here_b * here_b)
            near_a = neighbours(a[p], p, j, a[1 - p])
            near_b = neighbours(b[p], p, j, b[1 - p])
            keep_a = coefs[which, 0, p, j]
            gain = coefs[which, 1, p, j]
            keep_b = coefs[which, 2, p, j]
            new[0][p].append(here_a * keep_a + (length * spread_fast) * near_a + (gain - product))
            new[1][p].append(here_b * keep_b + (length * spread_slow) * near_b + product)
    return new


def save_coefs(coefs, rates):
    block = coefs.shape[3]
    begin = (rates.shape[2] - 8 * block) // 2
    for p in range(2):
        for j in range(block):
            feed = rates[0, p, pl.ds(begin + j, 8, stride=block), :]
            kill = rates[1, p, pl.ds(begin + j, 8, stride=block), :]
            for which, length in enumerate((fine_step, coarse_step)):
                for i, value in enumerate(coefs_from(feed, kill, length)):
                    coefs[which, i, p, j] = value


def fine(state, coefs):
    for _ in range(FINE):
        state = step(state, coefs, 0, fine_step)
    return state


def coarse(state, coefs):
    return step(state, coefs, 1, coarse_step)


def put(out, rows, m, state):
    lane = lane_index()
    block = len(state[0][0])
    begin = (8 * block - ROWS) // 2
    for c in range(2):
        for j in range(block):
            outer, inner = state[c][0][j], state[c][1][j]
            low = jnp.where(lane < 32, roll(outer, -16, 1), roll(inner, 16, 1))
            high = jnp.where(lane < 96, roll(inner, -16, 1), roll(outer, 16, 1))
            rows[c, pl.ds(j, 8, stride=block), :] = jnp.where(lane < 64, low, high)
        out[m, c] = rows[c, begin : begin + ROWS, :]


def sweep(first, windows, coefs, starts, coarse_ends):
    def turn(m, carry):
        end = coarse(load_state(starts.at[m]), coefs)
        save_state(coarse_ends.at[m], end)
        save_state(starts.at[m + 1], add(end, load_window(windows.at[m])))
        return carry

    lax.fori_loop(first, GROUP, turn, 0)


def second_terms(first, coefs, starts, coarse_ends, terms):
    def turn(m, carry):
        end = fine(load_state(starts.at[m]), coefs)
        save_state(terms.at[m], subtract(end, load_state(coarse_ends.at[m])))
        return carry

    lax.fori_loop(first, GROUP, turn, 0)


def second_sweep(first, coefs, current, terms, rows, out):
    def turn(m, carry):
        state = add(coarse(load_state(current), coefs), load_state(terms.at[m]))
        put(out, rows, m, state)
        save_state(current, state)
        return carry

    lax.fori_loop(first, GROUP, turn, 0)


def between(lane, begin, end):
    return (lane >= begin) & (lane < end)


def pack(sent, one, two):
    lane = lane_index()
    begin = (one.shape[2] - SENT) // 2
    for r in range(0, SENT, 8):
        rows, there = slice(r, r + 8), slice(begin + r, begin + r + 8)
        for k in range(4):
            second = two[k // 2, k % 2, there, :]
            half = k % 2
            first = roll(one[0, k // 2, there, :], 93 - (64 * half + 9), 1)
            block = jnp.where(between(lane, 52, 92), roll(second, -24, 1), first)
            sent[k, rows, :] = jnp.where(between(lane, 12, 52), second, block)
        for p in range(2):
            sent[4 + p, rows, :] = one[1, p, there, :]


def unpack(sent, one, two):
    lane = lane_index()
    begin = (one.shape[2] - SENT) // 2
    for r in range(0, SENT, 8):
        rows, there = slice(r, r + 8), slice(begin + r, begin + r + 8)
        blocks = [sent[k, rows, :] for k in range(4)]
        for k in range(4):
            two[k // 2, k % 2, there, :] = jnp.where(lane < 64, blocks[k], roll(blocks[k], 24, 1))
        for p in range(2):
            low, high = roll(blocks[2 * p], 9 - 93, 1), roll(blocks[2 * p + 1], 64 + 9 - 93, 1)
            one[0, p, there, :] = jnp.where(lane < 64, low, high)
            one[1, p, there, :] = sent[4 + p, rows, :]


def early_kernel(
    me, windows, rates, ends, sent, coefs, starts, coarse_ends, terms, current, rows, one, two
):
    @pl.when(me[0] < GROUP)
    def _():
        save_coefs(coefs, rates)
        save_state(starts.at[1], load_window(windows.at[0]))
        sweep(1, windows, coefs, starts, coarse_ends)
        put(ends, rows, 0, load_state(starts.at[1]))
        save_window(one, load_state(starts.at[GROUP]))
        second_terms(1, coefs, starts, coarse_ends, terms)
        state = add(load_state(coarse_ends.at[1]), load_state(terms.at[1]))
        put(ends, rows, 1, state)
        save_state(current, state)
        second_sweep(2, coefs, current, terms, rows, ends)
        save_window(two, load_state(current))
        pack(sent, one, two)


def late_kernel(
    windows, rates, received, ends, coefs, starts, coarse_ends, terms, current, rows, one, two
):
    save_coefs(coefs, rates)
    unpack(received, one, two)
    save_state(starts.at[0], load_window(one))
    save_state(current, load_window(two))
    sweep(0, windows, coefs, starts, coarse_ends)
    second_terms(0, coefs, starts, coarse_ends, terms)
    second_sweep(0, coefs, current, terms, rows, ends)


def merge_kernel(me, parts, out):
    lane = lane_index()
    early = me[0] < GROUP
    workers = [jnp.where(early, sub, GROUP - 1 - sub) for sub in range(GROUP)]
    for c in range(2):
        for r in range(ROWS // 8):
            rows = slice(8 * r, 8 * r + 8)
            strips = [parts[workers[sub], c, rows, :] for sub in range(GROUP)]
            for x in range(4):
                blocks = [roll(strips[sub], SUB * (sub - x), 1) for sub in range(GROUP)]
                low = jnp.where(lane < 32, blocks[0], blocks[1])
                high = jnp.where(lane < 96, blocks[2], blocks[3])
                out[c, x, rows, :] = jnp.where(lane < 64, low, high)


def call(kernel, shapes, scratch=(), scalars=0):
    vmem = pl.BlockSpec(memory_space=pltpu.VMEM)
    smem = pl.BlockSpec(memory_space=pltpu.SMEM)

    def run(*args):
        return pl.pallas_call(
            kernel,
            out_shape=[jax.ShapeDtypeStruct(s, jnp.float32) for s in shapes],
            in_specs=[smem] * scalars + [vmem] * (len(args) - scalars),
            out_specs=[vmem] * len(shapes),
            scratch_shapes=list(scratch),
            compiler_params=pltpu.CompilerParams(vmem_limit_bytes=32 * 1024 * 1024),
        )(*args)

    return run


def swap(block, axis, begin):
    count = lax.axis_size(axis)
    route = []
    for i in range(begin, begin + count, 2):
        a, b = i % count, (i + 1) % count
        route += [(a, b), (b, a)]
    return lax.ppermute(block, axis, route)


def edge(blocks, begin):
    return jnp.stack([lax.dynamic_slice_in_dim(block, begin, HALO, 2) for block in blocks])


def per_device(iterate, rates):
    state = iterate[0]
    slice_index = GROUP * lax.axis_index("th") + lax.axis_index("tl")
    gy, gz = lax.axis_index("gy"), lax.axis_index("gz")
    me = jnp.stack([slice_index, gy, gz]).astype(jnp.int32)
    odd = gy % 2
    two = edge((state, rates), odd * (ROWS - HALO))
    one = edge((state, rates), (1 - odd) * (ROWS - HALO))
    y_two = swap(two, "gy", 1)
    y_one = swap(one, "gy", 0)
    strip = (2, EXT, LANES)
    two, one = call(strips_kernel, [strip, strip], scalars=1)(me, state, rates, y_two, y_one)
    z_two = swap(two, "gz", 1)
    z_one = swap(one, "gz", 0)
    tile_state = pltpu.VMEM((2, 4, TILES, 8, LANES), jnp.float32)
    early_windows, late_windows, rates_here = call(
        first_kernel,
        [(GROUP, 2, 2, WIN, LANES), (GROUP, 2, 2, LATE_WIN, LANES), (2, 2, WIN, LANES)],
        scratch=[
            pltpu.VMEM((2, 2, 4, EXT, LANES), jnp.float32),
            pltpu.VMEM((2, 2, 4, EXT, LANES), jnp.float32),
            pltpu.VMEM((3, 4, TILES, 8, LANES), jnp.float32),
            tile_state,
            tile_state,
            tile_state,
        ],
        scalars=1,
    )(me, state, rates, y_two, y_one, z_two, z_one)

    def exchange(block):
        return lax.all_to_all(block, "tl", 0, 0)

    def leave(block):
        return block

    early = slice_index < GROUP
    last = 2 * GROUP - 1
    route = [(t, last - t) for t in range(GROUP)]

    def hand_over(block):
        return lax.ppermute(block, ("th", "tl"), route)

    def scratch_of(rows):
        states = (2, 2, rows // 8, 8, LANES)
        coefs = pltpu.VMEM((2, 3, *states[1:]), jnp.float32)
        starts = pltpu.VMEM((GROUP + 1, *states), jnp.float32)
        slices = pltpu.VMEM((GROUP, *states), jnp.float32)
        current = pltpu.VMEM(states, jnp.float32)
        flat = pltpu.VMEM((2, rows, LANES), jnp.float32)
        window = pltpu.VMEM((2, 2, rows, LANES), jnp.float32)
        return [coefs, starts, slices, slices, current, flat, window, window]

    ends_shape = (GROUP, 2, ROWS, LANES)
    windows = lax.cond(early, exchange, leave, early_windows)
    ends, sent = call(early_kernel, [ends_shape, (6, SENT, LANES)], scratch=scratch_of(WIN), scalars=1)(
        me, windows, rates_here
    )
    received = hand_over(sent)
    parts, windows = lax.cond(
        early, lambda e, w: (exchange(e), w), lambda e, w: (e, exchange(w)), ends, late_windows
    )

    def merge(parts):
        return call(merge_kernel, [(2, 4, ROWS, LANES)], scalars=1)(me, parts)[0]

    def end_early(parts, windows, received):
        return merge(parts)

    def end_late(parts, windows, received):
        (ends,) = call(late_kernel, [ends_shape], scratch=scratch_of(LATE_WIN))(windows, rates_here, received)
        return merge(exchange(ends))

    return lax.cond(early, end_early, end_late, parts, windows, received)[None]


def solution(mesh):
    shape = mesh.devices.shape
    split = Mesh(mesh.devices.reshape(shape[0] // GROUP, GROUP, *shape[1:]), ("th", "tl", "gy", "gz"))
    return jax.shard_map(
        per_device,
        mesh=split,
        in_specs=(P(("th", "tl"), None, None, "gy", "gz"), P(None, None, "gy", "gz")),
        out_specs=P(("th", "tl"), None, None, "gy", "gz"),
        check_vma=False,
    )
```

```python
import jax
import jax.numpy as jnp
from jax import lax
from jax.experimental import pallas as pl
from jax.experimental.pallas import tpu as pltpu
from jax.sharding import Mesh
from jax.sharding import PartitionSpec as P

FINE = 4
GROUP = 4
HALO = 16
SUB = 32
ROWS = 64
WIN = ROWS + 2 * 12
LATE_WIN = ROWS + 2 * 8
SENT_TWO = ROWS + 2 * 4
LANES = 128
EXT = ROWS + 2 * HALO
TILES = EXT // 8

spread_fast = 0.2
spread_slow = 0.1
fine_step = 0.125
coarse_step = 0.5

PAIRS = ((0, 3), (1, 2))


def lane_index():
    return lax.broadcasted_iota(jnp.int32, (8, LANES), 1)


def roll(block, shift, axis):
    shift = shift % block.shape[axis]
    return block if shift == 0 else pltpu.roll(block, shift, axis)


def pick(even, if_even, if_odd):
    return jnp.where(even, if_even, if_odd)


def ext_tile(one, two, own, even, index):
    if index < 2:
        rows = slice(8 * index, 8 * index + 8)
        return pick(even, two[rows, :], one[rows, :])
    if index < 10:
        return own[8 * (index - 2) : 8 * (index - 2) + 8, :]
    rows = slice(8 * (index - 10), 8 * (index - 10) + 8)
    return pick(even, one[rows, :], two[rows, :])


def strips_kernel(me, state, rates, y_two, y_one, two, one):
    lane = lane_index()
    even_y = me[1] % 2 == 0
    even_z = me[2] % 2 == 0
    for which, source in enumerate((state, rates)):
        for tile in range(TILES):
            first = jnp.zeros((8, LANES), jnp.float32)
            last = jnp.zeros((8, LANES), jnp.float32)
            for k in range(8):
                c, x = k // 4, k % 4
                rows = ext_tile(y_one.at[which, c, x], y_two.at[which, c, x], source.at[c, x], even_y, tile)
                here = (lane >= 16 * k) & (lane < 16 * k + 16)
                first = jnp.where(here, roll(rows, 16 * k, 1), first)
                last = jnp.where(here, roll(rows, 16 * k + 16, 1), last)
            one[which, 8 * tile : 8 * tile + 8, :] = pick(even_z, last, first)
            two[which, 8 * tile : 8 * tile + 8, :] = pick(even_z, first, last)


def lay_out(own, y_one, y_two, z_one, z_two, even_y, even_z, wide, lane):
    for tile in range(TILES):
        rows = slice(8 * tile, 8 * tile + 8)
        near, far = z_one[rows, :], z_two[rows, :]
        left = pick(even_z, far, near)
        right = pick(even_z, near, far)
        for k in range(8):
            c, x = k // 4, k % 4
            here = ext_tile(y_one.at[c, x], y_two.at[c, x], own.at[c, x], even_y, tile)
            wide[0, c, x, rows, :] = jnp.where(lane < 16, roll(left, -16 * k, 1), roll(here, 16, 1))
            wide[1, c, x, rows, :] = jnp.where(lane >= 112, roll(right, 112 - 16 * k, 1), roll(here, -16, 1))


def window_tile(wide, c, pair, sub, begin, lane):
    block, moved = ((0, 0), (1, 0), (0, 1), (1, 1))[sub]
    parts = [wide[block, c, x, begin : begin + 8, :] for x in PAIRS[pair]]
    parts[1 - moved] = roll(parts[1 - moved], 64, 1)
    return jnp.where(lane < 64, parts[0], parts[1])


def tile_step(source, target, coefs_of, length):
    for x in range(4):
        for j in range(TILES):
            keep_a, gain, keep_b = coefs_of(x, j)
            here = [source[c, x, j] for c in range(2)]
            near = []
            for c in range(2):
                below = source[c, max(x - 1, 0), j]
                above = source[c, min(x + 1, 3), j]
                before = source[c, x, j - 1] if j > 0 else roll(source[c, x, TILES - 1], 1, 0)
                after = source[c, x, j + 1] if j < TILES - 1 else roll(source[c, x, 0], -1, 0)
                along_z = roll(here[c], 1, 1) + roll(here[c], -1, 1)
                near.append(((below + above) + (before + after)) + along_z)
            a, b = here
            product = length * (a * b * b)
            target[0, x, j] = a * keep_a + (length * spread_fast) * near[0] + (gain - product)
            target[1, x, j] = b * keep_b + (length * spread_slow) * near[1] + product


def coefs_from(feed, kill, length):
    gain = length * feed
    keep_a = (1.0 - 6.0 * spread_fast * length) - gain
    keep_b = (1.0 - 6.0 * spread_slow * length) - length * (feed + kill)
    return keep_a, gain, keep_b


def first_kernel(
    me,
    state,
    rates,
    y_two,
    y_one,
    z_two,
    z_one,
    early_windows,
    late_windows,
    rates_here,
    wide,
    wide_rates,
    coefs,
    even,
    odd,
    slow,
):
    lane = lane_index()
    even_y = me[1] % 2 == 0
    even_z = me[2] % 2 == 0
    for which, source, target in ((0, state, wide), (1, rates, wide_rates)):
        lay_out(
            source,
            y_one.at[which],
            y_two.at[which],
            z_one.at[which],
            z_two.at[which],
            even_y,
            even_z,
            target,
            lane,
        )

    def rows_of(j):
        return pl.ds(j, 8, stride=TILES)

    def block(w, carry):
        for x in range(4):
            for j in range(TILES):
                feed = wide_rates[w, 0, x, rows_of(j), :]
                kill = wide_rates[w, 1, x, rows_of(j), :]
                for i, value in enumerate(coefs_from(feed, kill, fine_step)):
                    coefs[i, x, j] = value
                for c in range(2):
                    even[c, x, j] = wide[w, c, x, rows_of(j), :]

        def coarse_coefs(x, j):
            feed = wide_rates[w, 0, x, rows_of(j), :]
            kill = wide_rates[w, 1, x, rows_of(j), :]
            return coefs_from(feed, kill, coarse_step)

        def fine_coefs(x, j):
            return [coefs[i, x, j] for i in range(3)]

        tile_step(even, slow, coarse_coefs, coarse_step)

        def two_steps(_, inner):
            tile_step(even, odd, fine_coefs, fine_step)
            tile_step(odd, even, fine_coefs, fine_step)
            return inner

        lax.fori_loop(0, FINE // 2, two_steps, 0)
        leading = me[0] == 0
        for c in range(2):
            for x in range(4):
                for j in range(TILES):
                    coarse_end = slow[c, x, j]
                    difference = even[c, x, j] - coarse_end
                    wide[w, c, x, rows_of(j), :] = jnp.where(leading, coarse_end + difference, difference)
        return carry

    lax.fori_loop(0, 2, block, 0)

    def cut(source, sub, target):
        rows = target.shape[2]
        for c in range(2):
            for pair in range(2):
                for at in range(0, rows, 8):
                    begin = (EXT - rows) // 2 + at
                    target[c, pair, at : at + 8, :] = window_tile(source, c, pair, sub, begin, lane)

    @pl.when(me[0] < GROUP)
    def _():
        for sub in range(GROUP):
            cut(wide, sub, early_windows.at[sub])

    @pl.when(me[0] >= GROUP)
    def _():
        for sub in range(GROUP):
            cut(wide, sub, late_windows.at[GROUP - 1 - sub])

    worker = me[0] % GROUP
    for sub in range(GROUP):

        @pl.when(jnp.where(me[0] < GROUP, worker, GROUP - 1 - worker) == sub)
        def _():
            cut(wide_rates, sub, rates_here)


def over(op, count):
    return [[[op(c, p, j) for j in range(count)] for p in range(2)] for c in range(2)]


def load_state(ref):
    return over(lambda c, p, j: ref[c, p, j], ref.shape[2])


def save_state(ref, state):
    for c in range(2):
        for p in range(2):
            for j, value in enumerate(state[c][p]):
                ref[c, p, j] = value


def load_window(ref):
    block = ref.shape[2] // 8
    return over(lambda c, p, j: ref[c, p, pl.ds(j, 8, stride=block), :], block)


def save_window(ref, state):
    block = ref.shape[2] // 8
    for c in range(2):
        for p in range(2):
            for j, value in enumerate(state[c][p]):
                ref[c, p, pl.ds(j, 8, stride=block), :] = value


def combine(op, left, right):
    return over(lambda c, p, j: op(left[c][p][j], right[c][p][j]), len(left[0][0]))


def add(left, right):
    return combine(lambda l, r: l + r, left, right)


def subtract(left, right):
    return combine(lambda l, r: l - r, left, right)


def neighbours(s, p, j, other):
    here = s[j]
    if p == 0:
        along_x = here + other[j]
    else:
        along_x = other[j] + roll(here, 64, 1)
    before = s[j - 1] if j > 0 else roll(s[-1], 1, 0)
    after = s[j + 1] if j < len(s) - 1 else roll(s[0], -1, 0)
    along_z = roll(here, 1, 1) + roll(here, -1, 1)
    return (along_x + (before + after)) + along_z


def step(state, coefs, which, length):
    a, b = state
    new = [[[], []], [[], []]]
    for p in range(2):
        for j in range(len(a[p])):
            here_a, here_b = a[p][j], b[p][j]
            product = length * (here_a * here_b * here_b)
            near_a = neighbours(a[p], p, j, a[1 - p])
            near_b = neighbours(b[p], p, j, b[1 - p])
            keep_a = coefs[which, 0, p, j]
            gain = coefs[which, 1, p, j]
            keep_b = coefs[which, 2, p, j]
            new[0][p].append(here_a * keep_a + (length * spread_fast) * near_a + (gain - product))
            new[1][p].append(here_b * keep_b + (length * spread_slow) * near_b + product)
    return new


def save_coefs(coefs, rates, steps):
    block = coefs.shape[3]
    begin = (rates.shape[2] - 8 * block) // 2
    for p in range(2):
        for j in range(block):
            feed = rates[0, p, pl.ds(begin + j, 8, stride=block), :]
            kill = rates[1, p, pl.ds(begin + j, 8, stride=block), :]
            for which in steps:
                length = (fine_step, coarse_step)[which]
                for i, value in enumerate(coefs_from(feed, kill, length)):
                    coefs[which, i, p, j] = value


def fine(state, coefs):
    for _ in range(FINE):
        state = step(state, coefs, 0, fine_step)
    return state


def coarse(state, coefs):
    return step(state, coefs, 1, coarse_step)


def put(out, rows, m, state):
    lane = lane_index()
    block = len(state[0][0])
    begin = (8 * block - ROWS) // 2
    for c in range(2):
        for j in range(block):
            outer, inner = state[c][0][j], state[c][1][j]
            low = jnp.where(lane < 32, roll(outer, -16, 1), roll(inner, 16, 1))
            high = jnp.where(lane < 96, roll(inner, -16, 1), roll(outer, 16, 1))
            rows[c, pl.ds(j, 8, stride=block), :] = jnp.where(lane < 64, low, high)
        out[m, c] = rows[c, begin : begin + ROWS, :]


def sweep(first, windows, coefs, starts, coarse_ends):
    def turn(m, carry):
        end = coarse(load_state(starts.at[m]), coefs)
        save_state(coarse_ends.at[m], end)
        save_state(starts.at[m + 1], add(end, load_window(windows.at[m])))
        return carry

    lax.fori_loop(first, GROUP, turn, 0)


def second_terms(first, coefs, starts, coarse_ends, terms):
    def turn(m, carry):
        end = fine(load_state(starts.at[m]), coefs)
        save_state(terms.at[m], subtract(end, load_state(coarse_ends.at[m])))
        return carry

    lax.fori_loop(first, GROUP, turn, 0)


def second_sweep(first, coefs, current, terms, rows, out):
    def turn(m, carry):
        state = add(coarse(load_state(current), coefs), load_state(terms.at[m]))
        put(out, rows, m, state)
        save_state(current, state)
        return carry

    lax.fori_loop(first, GROUP, turn, 0)


def pack_two(sent, window):
    lane = lane_index()
    begin = (window.shape[2] - SENT_TWO) // 2
    for r in range(0, SENT_TWO, 8):
        for k in range(3):
            block = jnp.zeros((8, LANES), jnp.float32)
            for i in range(3):
                b = 3 * k + i
                if b < 8:
                    c, p, half = b // 4, b // 2 % 2, b % 2
                    rows = window[c, p, begin + r : begin + r + 8, :]
                    here = (lane >= 40 * i) & (lane < 40 * i + 40)
                    block = jnp.where(here, roll(rows, 40 * i - 12 - 64 * half, 1), block)
            sent[k, r : r + 8, :] = block


def unpack_two(sent, window):
    lane = lane_index()
    begin = (window.shape[2] - SENT_TWO) // 2
    for r in range(0, SENT_TWO, 8):
        for c in range(2):
            for p in range(2):
                halves = []
                for half in range(2):
                    b = 4 * c + 2 * p + half
                    rows = sent[b // 3, r : r + 8, :]
                    halves.append(roll(rows, 12 + 64 * half - 40 * (b % 3), 1))
                window[c, p, begin + r : begin + r + 8, :] = jnp.where(lane < 64, halves[0], halves[1])


def early_first_kernel(me, windows, rates, starts, coarse_ends, sent, coefs, window):
    @pl.when(me[0] < GROUP)
    def _():
        save_coefs(coefs, rates, (1,))
        save_state(starts.at[1], load_window(windows.at[0]))
        sweep(1, windows, coefs, starts, coarse_ends)
        save_window(window, load_state(starts.at[GROUP]))
        begin = (WIN - LATE_WIN) // 2
        for c in range(2):
            for p in range(2):
                sent[c, p] = window[c, p, begin : begin + LATE_WIN, :]


def early_second_kernel(me, starts, coarse_ends, rates, ends, sent, coefs, terms, current, rows, window):
    @pl.when(me[0] < GROUP)
    def _():
        save_coefs(coefs, rates, (0, 1))
        put(ends, rows, 0, load_state(starts.at[1]))
        second_terms(1, coefs, starts, coarse_ends, terms)
        state = add(load_state(coarse_ends.at[1]), load_state(terms.at[1]))
        put(ends, rows, 1, state)
        save_state(current, state)
        second_sweep(2, coefs, current, terms, rows, ends)
        save_window(window, load_state(current))
        pack_two(sent, window)


def late_first_kernel(me, windows, rates, received, terms, coefs, starts, coarse_ends):
    @pl.when(me[0] >= GROUP)
    def _():
        save_coefs(coefs, rates, (0, 1))
        save_state(starts.at[0], load_window(received))
        sweep(0, windows, coefs, starts, coarse_ends)
        second_terms(0, coefs, starts, coarse_ends, terms)


def late_second_kernel(terms, rates, received, ends, coefs, current, rows, window):
    save_coefs(coefs, rates, (1,))
    window[...] = jnp.zeros_like(window)
    unpack_two(received, window)
    save_state(current, load_window(window))
    second_sweep(0, coefs, current, terms, rows, ends)


def merge_kernel(me, parts, out):
    lane = lane_index()
    early = me[0] < GROUP
    workers = [jnp.where(early, sub, GROUP - 1 - sub) for sub in range(GROUP)]
    for c in range(2):
        for r in range(ROWS // 8):
            rows = slice(8 * r, 8 * r + 8)
            strips = [parts[workers[sub], c, rows, :] for sub in range(GROUP)]
            for x in range(4):
                blocks = [roll(strips[sub], SUB * (sub - x), 1) for sub in range(GROUP)]
                low = jnp.where(lane < 32, blocks[0], blocks[1])
                high = jnp.where(lane < 96, blocks[2], blocks[3])
                out[c, x, rows, :] = jnp.where(lane < 64, low, high)


def call(kernel, shapes, scratch=(), scalars=0):
    vmem = pl.BlockSpec(memory_space=pltpu.VMEM)
    smem = pl.BlockSpec(memory_space=pltpu.SMEM)

    def run(*args):
        return pl.pallas_call(
            kernel,
            out_shape=[jax.ShapeDtypeStruct(s, jnp.float32) for s in shapes],
            in_specs=[smem] * scalars + [vmem] * (len(args) - scalars),
            out_specs=[vmem] * len(shapes),
            scratch_shapes=list(scratch),
            compiler_params=pltpu.CompilerParams(vmem_limit_bytes=32 * 1024 * 1024),
        )(*args)

    return run


def swap(block, axis, begin):
    count = lax.axis_size(axis)
    route = []
    for i in range(begin, begin + count, 2):
        a, b = i % count, (i + 1) % count
        route += [(a, b), (b, a)]
    return lax.ppermute(block, axis, route)


def edge(blocks, begin):
    return jnp.stack([lax.dynamic_slice_in_dim(block, begin, HALO, 2) for block in blocks])


def per_device(iterate, rates):
    state = iterate[0]
    slice_index = GROUP * lax.axis_index("th") + lax.axis_index("tl")
    gy, gz = lax.axis_index("gy"), lax.axis_index("gz")
    me = jnp.stack([slice_index, gy, gz]).astype(jnp.int32)
    odd = gy % 2
    two = edge((state, rates), odd * (ROWS - HALO))
    one = edge((state, rates), (1 - odd) * (ROWS - HALO))
    y_two = swap(two, "gy", 1)
    y_one = swap(one, "gy", 0)
    strip = (2, EXT, LANES)
    two, one = call(strips_kernel, [strip, strip], scalars=1)(me, state, rates, y_two, y_one)
    z_two = swap(two, "gz", 1)
    z_one = swap(one, "gz", 0)
    tile_state = pltpu.VMEM((2, 4, TILES, 8, LANES), jnp.float32)
    early_windows, late_windows, rates_here = call(
        first_kernel,
        [(GROUP, 2, 2, WIN, LANES), (GROUP, 2, 2, LATE_WIN, LANES), (2, 2, WIN, LANES)],
        scratch=[
            pltpu.VMEM((2, 2, 4, EXT, LANES), jnp.float32),
            pltpu.VMEM((2, 2, 4, EXT, LANES), jnp.float32),
            pltpu.VMEM((3, 4, TILES, 8, LANES), jnp.float32),
            tile_state,
            tile_state,
            tile_state,
        ],
        scalars=1,
    )(me, state, rates, y_two, y_one, z_two, z_one)

    def exchange(block):
        return lax.all_to_all(block, "tl", 0, 0)

    def leave(block):
        return block

    early = slice_index < GROUP
    last = 2 * GROUP - 1
    route = [(t, last - t) for t in range(GROUP)]

    def hand_over(block):
        return lax.ppermute(block, ("th", "tl"), route)

    def states_of(rows):
        return (2, 2, rows // 8, 8, LANES)

    def scratch_of(rows):
        coefs = pltpu.VMEM((2, 3, *states_of(rows)[1:]), jnp.float32)
        current = pltpu.VMEM(states_of(rows), jnp.float32)
        flat = pltpu.VMEM((2, rows, LANES), jnp.float32)
        window = pltpu.VMEM((2, 2, rows, LANES), jnp.float32)
        return coefs, current, flat, window

    coefs, current, flat, window = scratch_of(WIN)
    starts_shape, slices_shape = (GROUP + 1, *states_of(WIN)), (GROUP, *states_of(WIN))
    ends_shape = (GROUP, 2, ROWS, LANES)
    windows = lax.cond(early, exchange, leave, early_windows)
    starts, coarse_ends, sent = call(
        early_first_kernel,
        [starts_shape, slices_shape, (2, 2, LATE_WIN, LANES)],
        scratch=[coefs, window],
        scalars=1,
    )(me, windows, rates_here)
    received_one = hand_over(sent)
    ends, sent = call(
        early_second_kernel,
        [ends_shape, (3, SENT_TWO, LANES)],
        scratch=[coefs, pltpu.VMEM(slices_shape, jnp.float32), current, flat, window],
        scalars=1,
    )(me, starts, coarse_ends, rates_here)
    received_two = hand_over(sent)

    ends, late_windows = lax.optimization_barrier((ends, late_windows))
    ends = lax.cond(early, exchange, leave, ends)
    windows = lax.cond(early, leave, exchange, late_windows)
    coefs, current, flat, window = scratch_of(LATE_WIN)
    starts_shape, slices_shape = (GROUP + 1, *states_of(LATE_WIN)), (GROUP, *states_of(LATE_WIN))
    (terms,) = call(
        late_first_kernel,
        [slices_shape],
        scratch=[coefs, pltpu.VMEM(starts_shape, jnp.float32), pltpu.VMEM(slices_shape, jnp.float32)],
        scalars=1,
    )(me, windows, rates_here, received_one)

    def end_late(parts, terms, received):
        scratch = [coefs, current, flat, window]
        (ends,) = call(late_second_kernel, [ends_shape], scratch=scratch)(terms, rates_here, received)
        return exchange(ends)

    ends = lax.cond(early, lambda parts, terms, received: parts, end_late, ends, terms, received_two)
    (out,) = call(merge_kernel, [(2, 4, ROWS, LANES)], scalars=1)(me, ends)
    return out[None]


def solution(mesh):
    shape = mesh.devices.shape
    split = Mesh(mesh.devices.reshape(shape[0] // GROUP, GROUP, *shape[1:]), ("th", "tl", "gy", "gz"))
    return jax.shard_map(
        per_device,
        mesh=split,
        in_specs=(P(("th", "tl"), None, None, "gy", "gz"), P(None, None, "gy", "gz")),
        out_specs=P(("th", "tl"), None, None, "gy", "gz"),
        check_vma=False,
    )
```

```python
import jax
import jax.numpy as jnp
from jax import lax
from jax.experimental import pallas as pl
from jax.experimental.pallas import tpu as pltpu
from jax.sharding import Mesh
from jax.sharding import PartitionSpec as P

FINE = 4
GROUP = 4
HALO = 16
SUB = 32
ROWS = 64
WIN = ROWS + 2 * 12
LATE_WIN = ROWS + 2 * 8
SENT_TWO = ROWS + 2 * 4
COLUMNS_ONE = SUB + 2 * 7
COLUMNS_TWO = SUB + 2 * 4
LANES = 128
EXT = ROWS + 2 * HALO
TILES = EXT // 8

spread_fast = 0.2
spread_slow = 0.1
fine_step = 0.125
coarse_step = 0.5

PAIRS = ((0, 3), (1, 2))


def lane_index():
    return lax.broadcasted_iota(jnp.int32, (8, LANES), 1)


def roll(block, shift, axis):
    shift = shift % block.shape[axis]
    return block if shift == 0 else pltpu.roll(block, shift, axis)


def pick(even, if_even, if_odd):
    return jnp.where(even, if_even, if_odd)


def ext_tile(one, two, own, even, index):
    if index < 2:
        rows = slice(8 * index, 8 * index + 8)
        return pick(even, two[rows, :], one[rows, :])
    if index < 10:
        return own[8 * (index - 2) : 8 * (index - 2) + 8, :]
    rows = slice(8 * (index - 10), 8 * (index - 10) + 8)
    return pick(even, one[rows, :], two[rows, :])


def strips_kernel(me, state, rates, y_two, y_one, two, one):
    lane = lane_index()
    even_y = me[1] % 2 == 0
    even_z = me[2] % 2 == 0
    for which, source in enumerate((state, rates)):
        for tile in range(TILES):
            first = jnp.zeros((8, LANES), jnp.float32)
            last = jnp.zeros((8, LANES), jnp.float32)
            for k in range(8):
                c, x = k // 4, k % 4
                rows = ext_tile(y_one.at[which, c, x], y_two.at[which, c, x], source.at[c, x], even_y, tile)
                here = (lane >= 16 * k) & (lane < 16 * k + 16)
                first = jnp.where(here, roll(rows, 16 * k, 1), first)
                last = jnp.where(here, roll(rows, 16 * k + 16, 1), last)
            one[which, 8 * tile : 8 * tile + 8, :] = pick(even_z, last, first)
            two[which, 8 * tile : 8 * tile + 8, :] = pick(even_z, first, last)


def lay_out(own, y_one, y_two, z_one, z_two, even_y, even_z, wide, lane):
    for tile in range(TILES):
        rows = slice(8 * tile, 8 * tile + 8)
        near, far = z_one[rows, :], z_two[rows, :]
        left = pick(even_z, far, near)
        right = pick(even_z, near, far)
        for k in range(8):
            c, x = k // 4, k % 4
            here = ext_tile(y_one.at[c, x], y_two.at[c, x], own.at[c, x], even_y, tile)
            wide[0, c, x, rows, :] = jnp.where(lane < 16, roll(left, -16 * k, 1), roll(here, 16, 1))
            wide[1, c, x, rows, :] = jnp.where(lane >= 112, roll(right, 112 - 16 * k, 1), roll(here, -16, 1))


def window_tile(wide, c, pair, sub, begin, lane):
    block, moved = ((0, 0), (1, 0), (0, 1), (1, 1))[sub]
    parts = [wide[block, c, x, begin : begin + 8, :] for x in PAIRS[pair]]
    parts[1 - moved] = roll(parts[1 - moved], 64, 1)
    return jnp.where(lane < 64, parts[0], parts[1])


def tile_step(source, target, coefs_of, length):
    for x in range(4):
        for j in range(TILES):
            keep_a, gain, keep_b = coefs_of(x, j)
            here = [source[c, x, j] for c in range(2)]
            near = []
            for c in range(2):
                below = source[c, max(x - 1, 0), j]
                above = source[c, min(x + 1, 3), j]
                before = source[c, x, j - 1] if j > 0 else roll(source[c, x, TILES - 1], 1, 0)
                after = source[c, x, j + 1] if j < TILES - 1 else roll(source[c, x, 0], -1, 0)
                along_z = roll(here[c], 1, 1) + roll(here[c], -1, 1)
                near.append(((below + above) + (before + after)) + along_z)
            a, b = here
            product = length * (a * b * b)
            target[0, x, j] = a * keep_a + (length * spread_fast) * near[0] + (gain - product)
            target[1, x, j] = b * keep_b + (length * spread_slow) * near[1] + product


def coefs_from(feed, kill, length):
    gain = length * feed
    keep_a = (1.0 - 6.0 * spread_fast * length) - gain
    keep_b = (1.0 - 6.0 * spread_slow * length) - length * (feed + kill)
    return keep_a, gain, keep_b


def first_kernel(
    me,
    state,
    rates,
    y_two,
    y_one,
    z_two,
    z_one,
    early_windows,
    late_windows,
    rates_here,
    wide,
    wide_rates,
    coefs,
    even,
    odd,
    slow,
):
    lane = lane_index()
    even_y = me[1] % 2 == 0
    even_z = me[2] % 2 == 0
    for which, source, target in ((0, state, wide), (1, rates, wide_rates)):
        lay_out(
            source,
            y_one.at[which],
            y_two.at[which],
            z_one.at[which],
            z_two.at[which],
            even_y,
            even_z,
            target,
            lane,
        )

    def rows_of(j):
        return pl.ds(j, 8, stride=TILES)

    def block(w, carry):
        for x in range(4):
            for j in range(TILES):
                feed = wide_rates[w, 0, x, rows_of(j), :]
                kill = wide_rates[w, 1, x, rows_of(j), :]
                for i, value in enumerate(coefs_from(feed, kill, fine_step)):
                    coefs[i, x, j] = value
                for c in range(2):
                    even[c, x, j] = wide[w, c, x, rows_of(j), :]

        def coarse_coefs(x, j):
            feed = wide_rates[w, 0, x, rows_of(j), :]
            kill = wide_rates[w, 1, x, rows_of(j), :]
            return coefs_from(feed, kill, coarse_step)

        def fine_coefs(x, j):
            return [coefs[i, x, j] for i in range(3)]

        tile_step(even, slow, coarse_coefs, coarse_step)

        def two_steps(_, inner):
            tile_step(even, odd, fine_coefs, fine_step)
            tile_step(odd, even, fine_coefs, fine_step)
            return inner

        lax.fori_loop(0, FINE // 2, two_steps, 0)
        leading = me[0] == 0
        for c in range(2):
            for x in range(4):
                for j in range(TILES):
                    coarse_end = slow[c, x, j]
                    difference = even[c, x, j] - coarse_end
                    wide[w, c, x, rows_of(j), :] = jnp.where(leading, coarse_end + difference, difference)
        return carry

    lax.fori_loop(0, 2, block, 0)

    def cut(source, sub, target):
        rows = target.shape[2]
        for c in range(2):
            for pair in range(2):
                for at in range(0, rows, 8):
                    begin = (EXT - rows) // 2 + at
                    target[c, pair, at : at + 8, :] = window_tile(source, c, pair, sub, begin, lane)

    @pl.when(me[0] < GROUP)
    def _():
        for sub in range(GROUP):
            cut(wide, sub, early_windows.at[sub])

    @pl.when(me[0] >= GROUP)
    def _():
        for sub in range(GROUP):
            cut(wide, sub, late_windows.at[GROUP - 1 - sub])

    worker = me[0] % GROUP
    for sub in range(GROUP):

        @pl.when(jnp.where(me[0] < GROUP, worker, GROUP - 1 - worker) == sub)
        def _():
            cut(wide_rates, sub, rates_here)


def over(op, count):
    return [[[op(c, p, j) for j in range(count)] for p in range(2)] for c in range(2)]


def load_state(ref):
    return over(lambda c, p, j: ref[c, p, j], ref.shape[2])


def save_state(ref, state):
    for c in range(2):
        for p in range(2):
            for j, value in enumerate(state[c][p]):
                ref[c, p, j] = value


def load_window(ref):
    block = ref.shape[2] // 8
    return over(lambda c, p, j: ref[c, p, pl.ds(j, 8, stride=block), :], block)


def save_window(ref, state):
    block = ref.shape[2] // 8
    for c in range(2):
        for p in range(2):
            for j, value in enumerate(state[c][p]):
                ref[c, p, pl.ds(j, 8, stride=block), :] = value


def combine(op, left, right):
    return over(lambda c, p, j: op(left[c][p][j], right[c][p][j]), len(left[0][0]))


def add(left, right):
    return combine(lambda l, r: l + r, left, right)


def subtract(left, right):
    return combine(lambda l, r: l - r, left, right)


def neighbours(s, p, j, other):
    here = s[j]
    if p == 0:
        along_x = here + other[j]
    else:
        along_x = other[j] + roll(here, 64, 1)
    before = s[j - 1] if j > 0 else roll(s[-1], 1, 0)
    after = s[j + 1] if j < len(s) - 1 else roll(s[0], -1, 0)
    along_z = roll(here, 1, 1) + roll(here, -1, 1)
    return (along_x + (before + after)) + along_z


def step(state, coefs, which, length):
    a, b = state
    new = [[[], []], [[], []]]
    for p in range(2):
        for j in range(len(a[p])):
            here_a, here_b = a[p][j], b[p][j]
            product = length * (here_a * here_b * here_b)
            near_a = neighbours(a[p], p, j, a[1 - p])
            near_b = neighbours(b[p], p, j, b[1 - p])
            keep_a = coefs[which, 0, p, j]
            gain = coefs[which, 1, p, j]
            keep_b = coefs[which, 2, p, j]
            new[0][p].append(here_a * keep_a + (length * spread_fast) * near_a + (gain - product))
            new[1][p].append(here_b * keep_b + (length * spread_slow) * near_b + product)
    return new


def save_coefs(coefs, rates, steps):
    block = coefs.shape[3]
    begin = (rates.shape[2] - 8 * block) // 2
    for p in range(2):
        for j in range(block):
            feed = rates[0, p, pl.ds(begin + j, 8, stride=block), :]
            kill = rates[1, p, pl.ds(begin + j, 8, stride=block), :]
            for which in steps:
                length = (fine_step, coarse_step)[which]
                for i, value in enumerate(coefs_from(feed, kill, length)):
                    coefs[which, i, p, j] = value


def fine(state, coefs):
    for _ in range(FINE):
        state = step(state, coefs, 0, fine_step)
    return state


def coarse(state, coefs):
    return step(state, coefs, 1, coarse_step)


def put(out, rows, m, state):
    lane = lane_index()
    block = len(state[0][0])
    begin = (8 * block - ROWS) // 2
    for c in range(2):
        for j in range(block):
            outer, inner = state[c][0][j], state[c][1][j]
            low = jnp.where(lane < 32, roll(outer, -16, 1), roll(inner, 16, 1))
            high = jnp.where(lane < 96, roll(inner, -16, 1), roll(outer, 16, 1))
            rows[c, pl.ds(j, 8, stride=block), :] = jnp.where(lane < 64, low, high)
        out[m, c] = rows[c, begin : begin + ROWS, :]


def sweep(first, windows, coefs, starts, coarse_ends):
    def turn(m, carry):
        end = coarse(load_state(starts.at[m]), coefs)
        save_state(coarse_ends.at[m], end)
        save_state(starts.at[m + 1], add(end, load_window(windows.at[m])))
        return carry

    lax.fori_loop(first, GROUP, turn, 0)


def second_terms(first, coefs, starts, coarse_ends, terms):
    def turn(m, carry):
        end = fine(load_state(starts.at[m]), coefs)
        save_state(terms.at[m], subtract(end, load_state(coarse_ends.at[m])))
        return carry

    lax.fori_loop(first, GROUP, turn, 0)


def second_sweep(first, coefs, current, terms, rows, out):
    def turn(m, carry):
        state = add(coarse(load_state(current), coefs), load_state(terms.at[m]))
        put(out, rows, m, state)
        save_state(current, state)
        return carry

    lax.fori_loop(first, GROUP, turn, 0)


def between(lane, begin, end):
    return (lane >= begin) & (lane < end)


def strip_start(b, k, width):
    start = width * b - LANES * k
    return start if -width < start < LANES else None


def pack_columns(sent, window, width):
    lane = lane_index()
    begin = (window.shape[2] - sent.shape[1]) // 2
    for r in range(0, sent.shape[1], 8):
        for k in range(sent.shape[0]):
            block = jnp.zeros((8, LANES), jnp.float32)
            for b in range(8):
                start = strip_start(b, k, width)
                if start is not None:
                    c, p, half = b // 4, b // 2 % 2, b % 2
                    rows = window[c, p, begin + r : begin + r + 8, :]
                    own = 64 * half + (64 - width) // 2
                    block = jnp.where(between(lane, start, start + width), roll(rows, start - own, 1), block)
            sent[k, r : r + 8, :] = block


def unpack_columns(sent, window, width):
    lane = lane_index()
    begin = (window.shape[2] - sent.shape[1]) // 2
    for r in range(0, sent.shape[1], 8):
        for c in range(2):
            for p in range(2):
                halves = []
                for half in range(2):
                    own = 64 * half + (64 - width) // 2
                    value = None
                    for k in range(sent.shape[0]):
                        start = strip_start(4 * c + 2 * p + half, k, width)
                        if start is not None:
                            part = roll(sent[k, r : r + 8, :], own - start, 1)
                            value = part if value is None else jnp.where(lane < own - start, value, part)
                    halves.append(value)
                window[c, p, begin + r : begin + r + 8, :] = jnp.where(lane < 64, halves[0], halves[1])


def early_first_kernel(me, windows, rates, starts, coarse_ends, sent, coefs, window):
    @pl.when(me[0] < GROUP)
    def _():
        save_coefs(coefs, rates, (1,))
        save_state(starts.at[1], load_window(windows.at[0]))
        sweep(1, windows, coefs, starts, coarse_ends)
        save_window(window, load_state(starts.at[GROUP]))
        pack_columns(sent, window, COLUMNS_ONE)


def early_second_kernel(me, starts, coarse_ends, rates, ends, sent, coefs, terms, current, rows, window):
    @pl.when(me[0] < GROUP)
    def _():
        save_coefs(coefs, rates, (0, 1))
        put(ends, rows, 0, load_state(starts.at[1]))
        second_terms(1, coefs, starts, coarse_ends, terms)
        state = add(load_state(coarse_ends.at[1]), load_state(terms.at[1]))
        put(ends, rows, 1, state)
        save_state(current, state)
        second_sweep(2, coefs, current, terms, rows, ends)
        save_window(window, load_state(current))
        pack_columns(sent, window, COLUMNS_TWO)


def late_first_kernel(me, windows, rates, received, terms, coefs, starts, coarse_ends, window):
    @pl.when(me[0] >= GROUP)
    def _():
        save_coefs(coefs, rates, (0, 1))
        unpack_columns(received, window, COLUMNS_ONE)
        save_state(starts.at[0], load_window(window))
        sweep(0, windows, coefs, starts, coarse_ends)
        second_terms(0, coefs, starts, coarse_ends, terms)


def late_second_kernel(terms, rates, received, ends, coefs, current, rows, window):
    save_coefs(coefs, rates, (1,))
    window[...] = jnp.zeros_like(window)
    unpack_columns(received, window, COLUMNS_TWO)
    save_state(current, load_window(window))
    second_sweep(0, coefs, current, terms, rows, ends)


def merge_kernel(me, parts, out):
    lane = lane_index()
    early = me[0] < GROUP
    workers = [jnp.where(early, sub, GROUP - 1 - sub) for sub in range(GROUP)]
    for c in range(2):
        for r in range(ROWS // 8):
            rows = slice(8 * r, 8 * r + 8)
            strips = [parts[workers[sub], c, rows, :] for sub in range(GROUP)]
            for x in range(4):
                blocks = [roll(strips[sub], SUB * (sub - x), 1) for sub in range(GROUP)]
                low = jnp.where(lane < 32, blocks[0], blocks[1])
                high = jnp.where(lane < 96, blocks[2], blocks[3])
                out[c, x, rows, :] = jnp.where(lane < 64, low, high)


def call(kernel, shapes, scratch=(), scalars=0):
    vmem = pl.BlockSpec(memory_space=pltpu.VMEM)
    smem = pl.BlockSpec(memory_space=pltpu.SMEM)

    def run(*args):
        return pl.pallas_call(
            kernel,
            out_shape=[jax.ShapeDtypeStruct(s, jnp.float32) for s in shapes],
            in_specs=[smem] * scalars + [vmem] * (len(args) - scalars),
            out_specs=[vmem] * len(shapes),
            scratch_shapes=list(scratch),
            compiler_params=pltpu.CompilerParams(vmem_limit_bytes=32 * 1024 * 1024),
        )(*args)

    return run


def swap(block, axis, begin):
    count = lax.axis_size(axis)
    route = []
    for i in range(begin, begin + count, 2):
        a, b = i % count, (i + 1) % count
        route += [(a, b), (b, a)]
    return lax.ppermute(block, axis, route)


def edge(blocks, begin):
    return jnp.stack([lax.dynamic_slice_in_dim(block, begin, HALO, 2) for block in blocks])


def per_device(iterate, rates):
    state = iterate[0]
    slice_index = GROUP * lax.axis_index("th") + lax.axis_index("tl")
    gy, gz = lax.axis_index("gy"), lax.axis_index("gz")
    me = jnp.stack([slice_index, gy, gz]).astype(jnp.int32)
    odd = gy % 2
    two = edge((state, rates), odd * (ROWS - HALO))
    one = edge((state, rates), (1 - odd) * (ROWS - HALO))
    y_two = swap(two, "gy", 1)
    y_one = swap(one, "gy", 0)
    strip = (2, EXT, LANES)
    two, one = call(strips_kernel, [strip, strip], scalars=1)(me, state, rates, y_two, y_one)
    z_two = swap(two, "gz", 1)
    z_one = swap(one, "gz", 0)
    tile_state = pltpu.VMEM((2, 4, TILES, 8, LANES), jnp.float32)
    early_windows, late_windows, rates_here = call(
        first_kernel,
        [(GROUP, 2, 2, WIN, LANES), (GROUP, 2, 2, LATE_WIN, LANES), (2, 2, WIN, LANES)],
        scratch=[
            pltpu.VMEM((2, 2, 4, EXT, LANES), jnp.float32),
            pltpu.VMEM((2, 2, 4, EXT, LANES), jnp.float32),
            pltpu.VMEM((3, 4, TILES, 8, LANES), jnp.float32),
            tile_state,
            tile_state,
            tile_state,
        ],
        scalars=1,
    )(me, state, rates, y_two, y_one, z_two, z_one)

    def exchange(block):
        return lax.all_to_all(block, "tl", 0, 0)

    def leave(block):
        return block

    early = slice_index < GROUP
    last = 2 * GROUP - 1
    route = [(t, last - t) for t in range(GROUP)]

    def hand_over(block):
        return lax.ppermute(block, ("th", "tl"), route)

    def states_of(rows):
        return (2, 2, rows // 8, 8, LANES)

    def scratch_of(rows):
        coefs = pltpu.VMEM((2, 3, *states_of(rows)[1:]), jnp.float32)
        current = pltpu.VMEM(states_of(rows), jnp.float32)
        flat = pltpu.VMEM((2, rows, LANES), jnp.float32)
        window = pltpu.VMEM((2, 2, rows, LANES), jnp.float32)
        return coefs, current, flat, window

    coefs, current, flat, window = scratch_of(WIN)
    starts_shape, slices_shape = (GROUP + 1, *states_of(WIN)), (GROUP, *states_of(WIN))
    ends_shape = (GROUP, 2, ROWS, LANES)
    windows = lax.cond(early, exchange, leave, early_windows)
    starts, coarse_ends, sent = call(
        early_first_kernel,
        [starts_shape, slices_shape, (3, LATE_WIN, LANES)],
        scratch=[coefs, window],
        scalars=1,
    )(me, windows, rates_here)
    received_one = hand_over(sent)
    ends, sent = call(
        early_second_kernel,
        [ends_shape, (3, SENT_TWO, LANES)],
        scratch=[coefs, pltpu.VMEM(slices_shape, jnp.float32), current, flat, window],
        scalars=1,
    )(me, starts, coarse_ends, rates_here)
    received_two = hand_over(sent)

    ends, late_windows = lax.optimization_barrier((ends, late_windows))
    ends = lax.cond(early, exchange, leave, ends)
    windows = lax.cond(early, leave, exchange, late_windows)
    coefs, current, flat, window = scratch_of(LATE_WIN)
    starts_shape, slices_shape = (GROUP + 1, *states_of(LATE_WIN)), (GROUP, *states_of(LATE_WIN))
    (terms,) = call(
        late_first_kernel,
        [slices_shape],
        scratch=[coefs, pltpu.VMEM(starts_shape, jnp.float32), pltpu.VMEM(slices_shape, jnp.float32), window],
        scalars=1,
    )(me, windows, rates_here, received_one)

    def end_late(parts, terms, received):
        scratch = [coefs, current, flat, window]
        (ends,) = call(late_second_kernel, [ends_shape], scratch=scratch)(terms, rates_here, received)
        return exchange(ends)

    ends = lax.cond(early, lambda parts, terms, received: parts, end_late, ends, terms, received_two)
    (out,) = call(merge_kernel, [(2, 4, ROWS, LANES)], scalars=1)(me, ends)
    return out[None]


def solution(mesh):
    shape = mesh.devices.shape
    split = Mesh(mesh.devices.reshape(shape[0] // GROUP, GROUP, *shape[1:]), ("th", "tl", "gy", "gz"))
    return jax.shard_map(
        per_device,
        mesh=split,
        in_specs=(P(("th", "tl"), None, None, "gy", "gz"), P(None, None, "gy", "gz")),
        out_specs=P(("th", "tl"), None, None, "gy", "gz"),
        check_vma=False,
    )
```

```python
import jax
import jax.numpy as jnp
from jax import lax
from jax.experimental import pallas as pl
from jax.experimental.pallas import tpu as pltpu
from jax.sharding import Mesh
from jax.sharding import PartitionSpec as P

FINE = 4
GROUP = 4
HALO = 16
SUB = 32
ROWS = 64
WIN = ROWS + 2 * 12
LATE_WIN = ROWS + 2 * 8
SENT_TWO = ROWS + 2 * 4
COLUMNS_ONE = SUB + 2 * 7
COLUMNS_TWO = SUB + 2 * 4
LANES = 128
EXT = ROWS + 2 * HALO
TILES = EXT // 8

spread_fast = 0.2
spread_slow = 0.1
fine_step = 0.125
coarse_step = 0.5

PAIRS = ((0, 3), (1, 2))


def lane_index():
    return lax.broadcasted_iota(jnp.int32, (8, LANES), 1)


def roll(block, shift, axis):
    shift = shift % block.shape[axis]
    return block if shift == 0 else pltpu.roll(block, shift, axis)


def pick(even, if_even, if_odd):
    return jnp.where(even, if_even, if_odd)


def ext_tile(one, two, own, even, index):
    if index < 2:
        rows = slice(8 * index, 8 * index + 8)
        return pick(even, two[rows, :], one[rows, :])
    if index < 10:
        return own[8 * (index - 2) : 8 * (index - 2) + 8, :]
    rows = slice(8 * (index - 10), 8 * (index - 10) + 8)
    return pick(even, one[rows, :], two[rows, :])


def strips_kernel(me, state, rates, y_two, y_one, two, one):
    lane = lane_index()
    even_y = me[1] % 2 == 0
    even_z = me[2] % 2 == 0
    for which, source in enumerate((state, rates)):
        for tile in range(TILES):
            first = jnp.zeros((8, LANES), jnp.float32)
            last = jnp.zeros((8, LANES), jnp.float32)
            for k in range(8):
                c, x = k // 4, k % 4
                rows = ext_tile(y_one.at[which, c, x], y_two.at[which, c, x], source.at[c, x], even_y, tile)
                here = (lane >= 16 * k) & (lane < 16 * k + 16)
                first = jnp.where(here, roll(rows, 16 * k, 1), first)
                last = jnp.where(here, roll(rows, 16 * k + 16, 1), last)
            one[which, 8 * tile : 8 * tile + 8, :] = pick(even_z, last, first)
            two[which, 8 * tile : 8 * tile + 8, :] = pick(even_z, first, last)


def lay_out(own, y_one, y_two, z_one, z_two, even_y, even_z, wide, lane):
    for tile in range(TILES):
        rows = slice(8 * tile, 8 * tile + 8)
        near, far = z_one[rows, :], z_two[rows, :]
        left = pick(even_z, far, near)
        right = pick(even_z, near, far)
        for k in range(8):
            c, x = k // 4, k % 4
            here = ext_tile(y_one.at[c, x], y_two.at[c, x], own.at[c, x], even_y, tile)
            wide[0, c, x, rows, :] = jnp.where(lane < 16, roll(left, -16 * k, 1), roll(here, 16, 1))
            wide[1, c, x, rows, :] = jnp.where(lane >= 112, roll(right, 112 - 16 * k, 1), roll(here, -16, 1))


def window_tile(wide, c, pair, sub, begin, lane):
    block, moved = ((0, 0), (1, 0), (0, 1), (1, 1))[sub]
    parts = [wide[block, c, x, begin : begin + 8, :] for x in PAIRS[pair]]
    parts[1 - moved] = roll(parts[1 - moved], 64, 1)
    return jnp.where(lane < 64, parts[0], parts[1])


def tile_step(source, target, coefs_of, length):
    for x in range(4):
        for j in range(TILES):
            keep_a, gain, keep_b = coefs_of(x, j)
            here = [source[c, x, j] for c in range(2)]
            near = []
            for c in range(2):
                below = source[c, max(x - 1, 0), j]
                above = source[c, min(x + 1, 3), j]
                before = source[c, x, j - 1] if j > 0 else roll(source[c, x, TILES - 1], 1, 0)
                after = source[c, x, j + 1] if j < TILES - 1 else roll(source[c, x, 0], -1, 0)
                along_z = roll(here[c], 1, 1) + roll(here[c], -1, 1)
                near.append(((below + above) + (before + after)) + along_z)
            a, b = here
            product = length * (a * b * b)
            target[0, x, j] = a * keep_a + (length * spread_fast) * near[0] + (gain - product)
            target[1, x, j] = b * keep_b + (length * spread_slow) * near[1] + product


def coefs_from(feed, kill, length):
    gain = length * feed
    keep_a = (1.0 - 6.0 * spread_fast * length) - gain
    keep_b = (1.0 - 6.0 * spread_slow * length) - length * (feed + kill)
    return keep_a, gain, keep_b


def first_kernel(
    me,
    state,
    rates,
    y_two,
    y_one,
    z_one,
    z_two,
    early_windows,
    late_windows,
    rates_here,
    wide,
    wide_rates,
    coefs,
    even,
    odd,
    slow,
):
    lane = lane_index()
    even_y = me[1] % 2 == 0
    even_z = me[2] % 2 == 0
    for which, source, target in ((0, state, wide), (1, rates, wide_rates)):
        lay_out(
            source,
            y_one.at[which],
            y_two.at[which],
            z_one.at[which],
            z_two.at[which],
            even_y,
            even_z,
            target,
            lane,
        )

    def rows_of(j):
        return pl.ds(j, 8, stride=TILES)

    def block(w, carry):
        for x in range(4):
            for j in range(TILES):
                feed = wide_rates[w, 0, x, rows_of(j), :]
                kill = wide_rates[w, 1, x, rows_of(j), :]
                for i, value in enumerate(coefs_from(feed, kill, fine_step)):
                    coefs[i, x, j] = value
                for c in range(2):
                    even[c, x, j] = wide[w, c, x, rows_of(j), :]

        def coarse_coefs(x, j):
            feed = wide_rates[w, 0, x, rows_of(j), :]
            kill = wide_rates[w, 1, x, rows_of(j), :]
            return coefs_from(feed, kill, coarse_step)

        def fine_coefs(x, j):
            return [coefs[i, x, j] for i in range(3)]

        tile_step(even, slow, coarse_coefs, coarse_step)

        def two_steps(_, inner):
            tile_step(even, odd, fine_coefs, fine_step)
            tile_step(odd, even, fine_coefs, fine_step)
            return inner

        lax.fori_loop(0, FINE // 2, two_steps, 0)
        leading = me[0] == 0
        for c in range(2):
            for x in range(4):
                for j in range(TILES):
                    coarse_end = slow[c, x, j]
                    difference = even[c, x, j] - coarse_end
                    wide[w, c, x, rows_of(j), :] = jnp.where(leading, coarse_end + difference, difference)
        return carry

    lax.fori_loop(0, 2, block, 0)

    def cut(source, sub, target):
        rows = target.shape[2]
        for c in range(2):
            for pair in range(2):
                for at in range(0, rows, 8):
                    begin = (EXT - rows) // 2 + at
                    target[c, pair, at : at + 8, :] = window_tile(source, c, pair, sub, begin, lane)

    @pl.when(me[0] < GROUP)
    def _():
        for sub in range(GROUP):
            cut(wide, sub, early_windows.at[sub])

    @pl.when(me[0] >= GROUP)
    def _():
        for sub in range(GROUP):
            cut(wide, sub, late_windows.at[GROUP - 1 - sub])

    worker = me[0] % GROUP
    for sub in range(GROUP):

        @pl.when(jnp.where(me[0] < GROUP, worker, GROUP - 1 - worker) == sub)
        def _():
            cut(wide_rates, sub, rates_here)


def over(op, count):
    return [[[op(c, p, j) for j in range(count)] for p in range(2)] for c in range(2)]


def load_state(ref):
    return over(lambda c, p, j: ref[c, p, j], ref.shape[2])


def save_state(ref, state):
    for c in range(2):
        for p in range(2):
            for j, value in enumerate(state[c][p]):
                ref[c, p, j] = value


def load_window(ref):
    block = ref.shape[2] // 8
    return over(lambda c, p, j: ref[c, p, pl.ds(j, 8, stride=block), :], block)


def save_window(ref, state):
    block = ref.shape[2] // 8
    for c in range(2):
        for p in range(2):
            for j, value in enumerate(state[c][p]):
                ref[c, p, pl.ds(j, 8, stride=block), :] = value


def combine(op, left, right):
    return over(lambda c, p, j: op(left[c][p][j], right[c][p][j]), len(left[0][0]))


def add(left, right):
    return combine(lambda l, r: l + r, left, right)


def subtract(left, right):
    return combine(lambda l, r: l - r, left, right)


def neighbours(s, p, j, other):
    here = s[j]
    if p == 0:
        along_x = here + other[j]
    else:
        along_x = other[j] + roll(here, 64, 1)
    before = s[j - 1] if j > 0 else roll(s[-1], 1, 0)
    after = s[j + 1] if j < len(s) - 1 else roll(s[0], -1, 0)
    along_z = roll(here, 1, 1) + roll(here, -1, 1)
    return (along_x + (before + after)) + along_z


def step(state, coefs, which, length):
    a, b = state
    new = [[[], []], [[], []]]
    for p in range(2):
        for j in range(len(a[p])):
            here_a, here_b = a[p][j], b[p][j]
            product = length * (here_a * here_b * here_b)
            near_a = neighbours(a[p], p, j, a[1 - p])
            near_b = neighbours(b[p], p, j, b[1 - p])
            keep_a = coefs[which, 0, p, j]
            gain = coefs[which, 1, p, j]
            keep_b = coefs[which, 2, p, j]
            new[0][p].append(here_a * keep_a + (length * spread_fast) * near_a + (gain - product))
            new[1][p].append(here_b * keep_b + (length * spread_slow) * near_b + product)
    return new


def save_coefs(coefs, rates, steps):
    block = coefs.shape[3]
    begin = (rates.shape[2] - 8 * block) // 2
    for p in range(2):
        for j in range(block):
            feed = rates[0, p, pl.ds(begin + j, 8, stride=block), :]
            kill = rates[1, p, pl.ds(begin + j, 8, stride=block), :]
            for which in steps:
                length = (fine_step, coarse_step)[which]
                for i, value in enumerate(coefs_from(feed, kill, length)):
                    coefs[which, i, p, j] = value


def fine(state, coefs):
    for _ in range(FINE):
        state = step(state, coefs, 0, fine_step)
    return state


def coarse(state, coefs):
    return step(state, coefs, 1, coarse_step)


def put(out, rows, m, state):
    lane = lane_index()
    block = len(state[0][0])
    begin = (8 * block - ROWS) // 2
    for c in range(2):
        for j in range(block):
            outer, inner = state[c][0][j], state[c][1][j]
            low = jnp.where(lane < 32, roll(outer, -16, 1), roll(inner, 16, 1))
            high = jnp.where(lane < 96, roll(inner, -16, 1), roll(outer, 16, 1))
            rows[c, pl.ds(j, 8, stride=block), :] = jnp.where(lane < 64, low, high)
        out[m, c] = rows[c, begin : begin + ROWS, :]


def sweep(first, windows, coefs, starts, coarse_ends):
    def turn(m, carry):
        end = coarse(load_state(starts.at[m]), coefs)
        save_state(coarse_ends.at[m], end)
        save_state(starts.at[m + 1], add(end, load_window(windows.at[m])))
        return carry

    lax.fori_loop(first, GROUP, turn, 0)


def second_terms(first, coefs, starts, coarse_ends, terms):
    def turn(m, carry):
        end = fine(load_state(starts.at[m]), coefs)
        save_state(terms.at[m], subtract(end, load_state(coarse_ends.at[m])))
        return carry

    lax.fori_loop(first, GROUP, turn, 0)


def second_sweep(first, coefs, current, terms, rows, out):
    def turn(m, carry):
        state = add(coarse(load_state(current), coefs), load_state(terms.at[m]))
        put(out, rows, m, state)
        save_state(current, state)
        return carry

    lax.fori_loop(first, GROUP, turn, 0)


def between(lane, begin, end):
    return (lane >= begin) & (lane < end)


def strip_start(b, k, width):
    start = width * b - LANES * k
    return start if -width < start < LANES else None


def pack_columns(sent, window, width):
    lane = lane_index()
    begin = (window.shape[2] - sent.shape[1]) // 2
    for r in range(0, sent.shape[1], 8):
        for k in range(sent.shape[0]):
            block = jnp.zeros((8, LANES), jnp.float32)
            for b in range(8):
                start = strip_start(b, k, width)
                if start is not None:
                    c, p, half = b // 4, b // 2 % 2, b % 2
                    rows = window[c, p, begin + r : begin + r + 8, :]
                    own = 64 * half + (64 - width) // 2
                    block = jnp.where(between(lane, start, start + width), roll(rows, start - own, 1), block)
            sent[k, r : r + 8, :] = block


def unpack_columns(sent, window, width):
    lane = lane_index()
    begin = (window.shape[2] - sent.shape[1]) // 2
    for r in range(0, sent.shape[1], 8):
        for c in range(2):
            for p in range(2):
                halves = []
                for half in range(2):
                    own = 64 * half + (64 - width) // 2
                    value = None
                    for k in range(sent.shape[0]):
                        start = strip_start(4 * c + 2 * p + half, k, width)
                        if start is not None:
                            part = roll(sent[k, r : r + 8, :], own - start, 1)
                            value = part if value is None else jnp.where(lane < own - start, value, part)
                    halves.append(value)
                window[c, p, begin + r : begin + r + 8, :] = jnp.where(lane < 64, halves[0], halves[1])


def early_first_kernel(me, windows, rates, starts, coarse_ends, sent, coefs, window):
    @pl.when(me[0] < GROUP)
    def _():
        save_coefs(coefs, rates, (1,))
        save_state(starts.at[1], load_window(windows.at[0]))
        sweep(1, windows, coefs, starts, coarse_ends)
        save_window(window, load_state(starts.at[GROUP]))
        pack_columns(sent, window, COLUMNS_ONE)


def early_second_kernel(me, starts, coarse_ends, rates, ends, sent, coefs, terms, current, rows, window):
    @pl.when(me[0] < GROUP)
    def _():
        save_coefs(coefs, rates, (0, 1))
        put(ends, rows, 0, load_state(starts.at[1]))
        second_terms(1, coefs, starts, coarse_ends, terms)
        state = add(load_state(coarse_ends.at[1]), load_state(terms.at[1]))
        put(ends, rows, 1, state)
        save_state(current, state)
        second_sweep(2, coefs, current, terms, rows, ends)
        save_window(window, load_state(current))
        pack_columns(sent, window, COLUMNS_TWO)


def late_first_kernel(me, windows, rates, received, terms, coefs, starts, coarse_ends, window):
    @pl.when(me[0] >= GROUP)
    def _():
        save_coefs(coefs, rates, (0, 1))
        unpack_columns(received, window, COLUMNS_ONE)
        save_state(starts.at[0], load_window(window))
        sweep(0, windows, coefs, starts, coarse_ends)
        second_terms(0, coefs, starts, coarse_ends, terms)


def late_second_kernel(terms, rates, received, ends, coefs, current, rows, window):
    save_coefs(coefs, rates, (1,))
    window[...] = jnp.zeros_like(window)
    unpack_columns(received, window, COLUMNS_TWO)
    save_state(current, load_window(window))
    second_sweep(0, coefs, current, terms, rows, ends)


def merge_kernel(me, parts, out):
    lane = lane_index()
    early = me[0] < GROUP
    workers = [jnp.where(early, sub, GROUP - 1 - sub) for sub in range(GROUP)]
    for c in range(2):
        for r in range(ROWS // 8):
            rows = slice(8 * r, 8 * r + 8)
            strips = [parts[workers[sub], c, rows, :] for sub in range(GROUP)]
            for x in range(4):
                blocks = [roll(strips[sub], SUB * (sub - x), 1) for sub in range(GROUP)]
                low = jnp.where(lane < 32, blocks[0], blocks[1])
                high = jnp.where(lane < 96, blocks[2], blocks[3])
                out[c, x, rows, :] = jnp.where(lane < 64, low, high)


def call(kernel, shapes, scratch=(), scalars=0):
    vmem = pl.BlockSpec(memory_space=pltpu.VMEM)
    smem = pl.BlockSpec(memory_space=pltpu.SMEM)

    def run(*args):
        return pl.pallas_call(
            kernel,
            out_shape=[jax.ShapeDtypeStruct(s, jnp.float32) for s in shapes],
            in_specs=[smem] * scalars + [vmem] * (len(args) - scalars),
            out_specs=[vmem] * len(shapes),
            scratch_shapes=list(scratch),
            compiler_params=pltpu.CompilerParams(vmem_limit_bytes=32 * 1024 * 1024),
        )(*args)

    return run


def swap(block, axis, begin):
    count = lax.axis_size(axis)
    route = []
    for i in range(begin, begin + count, 2):
        a, b = i % count, (i + 1) % count
        route += [(a, b), (b, a)]
    return lax.ppermute(block, axis, route)


def edge(blocks, begin):
    return jnp.stack([lax.dynamic_slice_in_dim(block, begin, HALO, 2) for block in blocks])


def per_device(iterate, rates):
    state = iterate[0]
    slice_index = GROUP * lax.axis_index("th") + lax.axis_index("tl")
    gy, gz = lax.axis_index("gy"), lax.axis_index("gz")
    me = jnp.stack([slice_index, gy, gz]).astype(jnp.int32)
    odd = gy % 2
    two = edge((state, rates), odd * (ROWS - HALO))
    one = edge((state, rates), (1 - odd) * (ROWS - HALO))
    y_two = swap(two, "gy", 1)
    y_one = swap(one, "gy", 0)
    strip = (2, EXT, LANES)
    two, one = call(strips_kernel, [strip, strip], scalars=1)(me, state, rates, y_two, y_one)
    z_two = swap(two, "gz", 1)
    z_one = swap(one, "gz", 0)
    tile_state = pltpu.VMEM((2, 4, TILES, 8, LANES), jnp.float32)
    early_windows, late_windows, rates_here = call(
        first_kernel,
        [(GROUP, 2, 2, WIN, LANES), (GROUP, 2, 2, LATE_WIN, LANES), (2, 2, WIN, LANES)],
        scratch=[
            pltpu.VMEM((2, 2, 4, EXT, LANES), jnp.float32),
            pltpu.VMEM((2, 2, 4, EXT, LANES), jnp.float32),
            pltpu.VMEM((3, 4, TILES, 8, LANES), jnp.float32),
            tile_state,
            tile_state,
            tile_state,
        ],
        scalars=1,
    )(me, state, rates, y_two, y_one, z_one, z_two)

    def exchange(block):
        return lax.all_to_all(block, "tl", 0, 0)

    def leave(block):
        return block

    early = slice_index < GROUP
    last = 2 * GROUP - 1
    route = [(t, last - t) for t in range(GROUP)]

    def hand_over(block):
        return lax.ppermute(block, ("th", "tl"), route)

    def states_of(rows):
        return (2, 2, rows // 8, 8, LANES)

    def scratch_of(rows):
        coefs = pltpu.VMEM((2, 3, *states_of(rows)[1:]), jnp.float32)
        current = pltpu.VMEM(states_of(rows), jnp.float32)
        flat = pltpu.VMEM((2, rows, LANES), jnp.float32)
        window = pltpu.VMEM((2, 2, rows, LANES), jnp.float32)
        return coefs, current, flat, window

    coefs, current, flat, window = scratch_of(WIN)
    starts_shape, slices_shape = (GROUP + 1, *states_of(WIN)), (GROUP, *states_of(WIN))
    ends_shape = (GROUP, 2, ROWS, LANES)
    windows = lax.cond(early, exchange, leave, early_windows)
    starts, coarse_ends, sent = call(
        early_first_kernel,
        [starts_shape, slices_shape, (3, LATE_WIN, LANES)],
        scratch=[coefs, window],
        scalars=1,
    )(me, windows, rates_here)
    received_one = hand_over(sent)
    ends, sent = call(
        early_second_kernel,
        [ends_shape, (3, SENT_TWO, LANES)],
        scratch=[coefs, pltpu.VMEM(slices_shape, jnp.float32), current, flat, window],
        scalars=1,
    )(me, starts, coarse_ends, rates_here)
    received_two = hand_over(sent)

    ends, late_windows = lax.optimization_barrier((ends, late_windows))
    ends = lax.cond(early, exchange, leave, ends)
    windows = lax.cond(early, leave, exchange, late_windows)
    coefs, current, flat, window = scratch_of(LATE_WIN)
    starts_shape, slices_shape = (GROUP + 1, *states_of(LATE_WIN)), (GROUP, *states_of(LATE_WIN))
    (terms,) = call(
        late_first_kernel,
        [slices_shape],
        scratch=[coefs, pltpu.VMEM(starts_shape, jnp.float32), pltpu.VMEM(slices_shape, jnp.float32), window],
        scalars=1,
    )(me, windows, rates_here, received_one)

    def end_late(parts, terms, received):
        scratch = [coefs, current, flat, window]
        (ends,) = call(late_second_kernel, [ends_shape], scratch=scratch)(terms, rates_here, received)
        return exchange(ends)

    ends = lax.cond(early, lambda parts, terms, received: parts, end_late, ends, terms, received_two)
    (out,) = call(merge_kernel, [(2, 4, ROWS, LANES)], scalars=1)(me, ends)
    return out[None]


def solution(mesh):
    shape = mesh.devices.shape
    split = Mesh(mesh.devices.reshape(shape[0] // GROUP, GROUP, *shape[1:]), ("th", "tl", "gy", "gz"))
    return jax.shard_map(
        per_device,
        mesh=split,
        in_specs=(P(("th", "tl"), None, None, "gy", "gz"), P(None, None, "gy", "gz")),
        out_specs=P(("th", "tl"), None, None, "gy", "gz"),
        check_vma=False,
    )
```

```python
import jax
import jax.numpy as jnp
from jax import lax
from jax.experimental import pallas as pl
from jax.experimental.pallas import tpu as pltpu
from jax.sharding import Mesh
from jax.sharding import PartitionSpec as P

FINE = 4
GROUP = 4
HALO = 16
SUB = 32
ROWS = 64
WIN = ROWS + 2 * 12
LATE_WIN = ROWS + 2 * 8
SENT_TWO = ROWS + 2 * 4
COLUMNS_ONE = SUB + 2 * 7
COLUMNS_TWO = SUB + 2 * 4
LANES = 128
EXT = ROWS + 2 * HALO
TILES = EXT // 8

spread_fast = 0.2
spread_slow = 0.1
fine_step = 0.125
coarse_step = 0.5

PAIRS = ((0, 3), (1, 2))


def lane_index():
    return lax.broadcasted_iota(jnp.int32, (8, LANES), 1)


def roll(block, shift, axis):
    shift = shift % block.shape[axis]
    return block if shift == 0 else pltpu.roll(block, shift, axis)


def pick(even, if_even, if_odd):
    return jnp.where(even, if_even, if_odd)


def ext_tile(one, two, own, even, index):
    if index < 2:
        rows = slice(8 * index, 8 * index + 8)
        return pick(even, two[rows, :], one[rows, :])
    if index < 10:
        return own[8 * (index - 2) : 8 * (index - 2) + 8, :]
    rows = slice(8 * (index - 10), 8 * (index - 10) + 8)
    return pick(even, one[rows, :], two[rows, :])


def pack_edges(blocks, lane):
    first = jnp.zeros((8, LANES), jnp.float32)
    last = jnp.zeros((8, LANES), jnp.float32)
    for k, rows in enumerate(blocks):
        here = (lane >= 16 * k) & (lane < 16 * k + 16)
        first = jnp.where(here, roll(rows, 16 * k, 1), first)
        last = jnp.where(here, roll(rows, 16 * k + 16, 1), last)
    return first, last


def own_strips_kernel(me, state, rates, two, one):
    lane = lane_index()
    even_z = me[2] % 2 == 0
    for which, source in enumerate((state, rates)):
        for at in range(0, ROWS, 8):
            rows = slice(at, at + 8)
            first, last = pack_edges([source[k // 4, k % 4, rows, :] for k in range(8)], lane)
            one[which, rows, :] = pick(even_z, last, first)
            two[which, rows, :] = pick(even_z, first, last)


def strips_kernel(me, own_two, own_one, y_two, y_one, two, one):
    lane = lane_index()
    even_y = me[1] % 2 == 0
    even_z = me[2] % 2 == 0
    one[:, HALO : HALO + ROWS, :] = own_one[...]
    two[:, HALO : HALO + ROWS, :] = own_two[...]
    for which in range(2):
        for tile in (0, 1, TILES - 2, TILES - 1):
            blocks = [
                ext_tile(y_one.at[which, k // 4, k % 4], y_two.at[which, k // 4, k % 4], None, even_y, tile)
                for k in range(8)
            ]
            first, last = pack_edges(blocks, lane)
            one[which, 8 * tile : 8 * tile + 8, :] = pick(even_z, last, first)
            two[which, 8 * tile : 8 * tile + 8, :] = pick(even_z, first, last)


def lay_out(own, y_one, y_two, z_one, z_two, even_y, even_z, wide, lane):
    for tile in range(TILES):
        rows = slice(8 * tile, 8 * tile + 8)
        near, far = z_one[rows, :], z_two[rows, :]
        left = pick(even_z, far, near)
        right = pick(even_z, near, far)
        for k in range(8):
            c, x = k // 4, k % 4
            here = ext_tile(y_one.at[c, x], y_two.at[c, x], own.at[c, x], even_y, tile)
            wide[0, c, x, rows, :] = jnp.where(lane < 16, roll(left, -16 * k, 1), roll(here, 16, 1))
            wide[1, c, x, rows, :] = jnp.where(lane >= 112, roll(right, 112 - 16 * k, 1), roll(here, -16, 1))


def window_tile(wide, c, pair, sub, begin, lane):
    block, moved = ((0, 0), (1, 0), (0, 1), (1, 1))[sub]
    parts = [wide[block, c, x, begin : begin + 8, :] for x in PAIRS[pair]]
    parts[1 - moved] = roll(parts[1 - moved], 64, 1)
    return jnp.where(lane < 64, parts[0], parts[1])


def tile_step(source, target, coefs_of, length):
    for x in range(4):
        for j in range(TILES):
            keep_a, gain, keep_b = coefs_of(x, j)
            here = [source[c, x, j] for c in range(2)]
            near = []
            for c in range(2):
                below = source[c, max(x - 1, 0), j]
                above = source[c, min(x + 1, 3), j]
                before = source[c, x, j - 1] if j > 0 else roll(source[c, x, TILES - 1], 1, 0)
                after = source[c, x, j + 1] if j < TILES - 1 else roll(source[c, x, 0], -1, 0)
                along_z = roll(here[c], 1, 1) + roll(here[c], -1, 1)
                near.append(((below + above) + (before + after)) + along_z)
            a, b = here
            product = length * (a * b * b)
            target[0, x, j] = a * keep_a + (length * spread_fast) * near[0] + (gain - product)
            target[1, x, j] = b * keep_b + (length * spread_slow) * near[1] + product


def coefs_from(feed, kill, length):
    gain = length * feed
    keep_a = (1.0 - 6.0 * spread_fast * length) - gain
    keep_b = (1.0 - 6.0 * spread_slow * length) - length * (feed + kill)
    return keep_a, gain, keep_b


def first_kernel(
    me,
    state,
    rates,
    y_two,
    y_one,
    z_two,
    z_one,
    early_windows,
    late_windows,
    rates_here,
    wide,
    wide_rates,
    coefs,
    even,
    odd,
    slow,
):
    lane = lane_index()
    even_y = me[1] % 2 == 0
    even_z = me[2] % 2 == 0
    for which, source, target in ((0, state, wide), (1, rates, wide_rates)):
        lay_out(
            source,
            y_one.at[which],
            y_two.at[which],
            z_one.at[which],
            z_two.at[which],
            even_y,
            even_z,
            target,
            lane,
        )

    def rows_of(j):
        return pl.ds(j, 8, stride=TILES)

    def block(w, carry):
        for x in range(4):
            for j in range(TILES):
                feed = wide_rates[w, 0, x, rows_of(j), :]
                kill = wide_rates[w, 1, x, rows_of(j), :]
                for i, value in enumerate(coefs_from(feed, kill, fine_step)):
                    coefs[i, x, j] = value
                for c in range(2):
                    even[c, x, j] = wide[w, c, x, rows_of(j), :]

        def coarse_coefs(x, j):
            feed = wide_rates[w, 0, x, rows_of(j), :]
            kill = wide_rates[w, 1, x, rows_of(j), :]
            return coefs_from(feed, kill, coarse_step)

        def fine_coefs(x, j):
            return [coefs[i, x, j] for i in range(3)]

        tile_step(even, slow, coarse_coefs, coarse_step)

        def two_steps(_, inner):
            tile_step(even, odd, fine_coefs, fine_step)
            tile_step(odd, even, fine_coefs, fine_step)
            return inner

        lax.fori_loop(0, FINE // 2, two_steps, 0)
        leading = me[0] == 0
        for c in range(2):
            for x in range(4):
                for j in range(TILES):
                    coarse_end = slow[c, x, j]
                    difference = even[c, x, j] - coarse_end
                    wide[w, c, x, rows_of(j), :] = jnp.where(leading, coarse_end + difference, difference)
        return carry

    lax.fori_loop(0, 2, block, 0)

    def cut(source, sub, target):
        rows = target.shape[2]
        for c in range(2):
            for pair in range(2):
                for at in range(0, rows, 8):
                    begin = (EXT - rows) // 2 + at
                    target[c, pair, at : at + 8, :] = window_tile(source, c, pair, sub, begin, lane)

    @pl.when(me[0] < GROUP)
    def _():
        for sub in range(GROUP):
            cut(wide, sub, early_windows.at[sub])

    @pl.when(me[0] >= GROUP)
    def _():
        for sub in range(GROUP):
            cut(wide, sub, late_windows.at[GROUP - 1 - sub])

    worker = me[0] % GROUP
    for sub in range(GROUP):

        @pl.when(jnp.where(me[0] < GROUP, worker, GROUP - 1 - worker) == sub)
        def _():
            cut(wide_rates, sub, rates_here)


def over(op, count):
    return [[[op(c, p, j) for j in range(count)] for p in range(2)] for c in range(2)]


def load_state(ref):
    return over(lambda c, p, j: ref[c, p, j], ref.shape[2])


def save_state(ref, state):
    for c in range(2):
        for p in range(2):
            for j, value in enumerate(state[c][p]):
                ref[c, p, j] = value


def load_window(ref):
    block = ref.shape[2] // 8
    return over(lambda c, p, j: ref[c, p, pl.ds(j, 8, stride=block), :], block)


def save_window(ref, state):
    block = ref.shape[2] // 8
    for c in range(2):
        for p in range(2):
            for j, value in enumerate(state[c][p]):
                ref[c, p, pl.ds(j, 8, stride=block), :] = value


def combine(op, left, right):
    return over(lambda c, p, j: op(left[c][p][j], right[c][p][j]), len(left[0][0]))


def add(left, right):
    return combine(lambda l, r: l + r, left, right)


def subtract(left, right):
    return combine(lambda l, r: l - r, left, right)


def neighbours(s, p, j, other):
    here = s[j]
    if p == 0:
        along_x = here + other[j]
    else:
        along_x = other[j] + roll(here, 64, 1)
    before = s[j - 1] if j > 0 else roll(s[-1], 1, 0)
    after = s[j + 1] if j < len(s) - 1 else roll(s[0], -1, 0)
    along_z = roll(here, 1, 1) + roll(here, -1, 1)
    return (along_x + (before + after)) + along_z


def step(state, coefs, which, length):
    a, b = state
    new = [[[], []], [[], []]]
    for p in range(2):
        for j in range(len(a[p])):
            here_a, here_b = a[p][j], b[p][j]
            product = length * (here_a * here_b * here_b)
            near_a = neighbours(a[p], p, j, a[1 - p])
            near_b = neighbours(b[p], p, j, b[1 - p])
            keep_a = coefs[which, 0, p, j]
            gain = coefs[which, 1, p, j]
            keep_b = coefs[which, 2, p, j]
            new[0][p].append(here_a * keep_a + (length * spread_fast) * near_a + (gain - product))
            new[1][p].append(here_b * keep_b + (length * spread_slow) * near_b + product)
    return new


def save_coefs(coefs, rates, steps):
    block = coefs.shape[3]
    begin = (rates.shape[2] - 8 * block) // 2
    for p in range(2):
        for j in range(block):
            feed = rates[0, p, pl.ds(begin + j, 8, stride=block), :]
            kill = rates[1, p, pl.ds(begin + j, 8, stride=block), :]
            for which in steps:
                length = (fine_step, coarse_step)[which]
                for i, value in enumerate(coefs_from(feed, kill, length)):
                    coefs[which, i, p, j] = value


def fine(state, coefs):
    for _ in range(FINE):
        state = step(state, coefs, 0, fine_step)
    return state


def coarse(state, coefs):
    return step(state, coefs, 1, coarse_step)


def put(out, rows, m, state):
    lane = lane_index()
    block = len(state[0][0])
    begin = (8 * block - ROWS) // 2
    for c in range(2):
        for j in range(block):
            outer, inner = state[c][0][j], state[c][1][j]
            low = jnp.where(lane < 32, roll(outer, -16, 1), roll(inner, 16, 1))
            high = jnp.where(lane < 96, roll(inner, -16, 1), roll(outer, 16, 1))
            rows[c, pl.ds(j, 8, stride=block), :] = jnp.where(lane < 64, low, high)
        out[m, c] = rows[c, begin : begin + ROWS, :]


def sweep(first, windows, coefs, starts, coarse_ends):
    def turn(m, carry):
        end = coarse(load_state(starts.at[m]), coefs)
        save_state(coarse_ends.at[m], end)
        save_state(starts.at[m + 1], add(end, load_window(windows.at[m])))
        return carry

    lax.fori_loop(first, GROUP, turn, 0)


def second_terms(first, coefs, starts, coarse_ends, terms):
    def turn(m, carry):
        end = fine(load_state(starts.at[m]), coefs)
        save_state(terms.at[m], subtract(end, load_state(coarse_ends.at[m])))
        return carry

    lax.fori_loop(first, GROUP, turn, 0)


def second_sweep(first, coefs, current, terms, rows, out):
    def turn(m, carry):
        state = add(coarse(load_state(current), coefs), load_state(terms.at[m]))
        put(out, rows, m, state)
        save_state(current, state)
        return carry

    lax.fori_loop(first, GROUP, turn, 0)


def between(lane, begin, end):
    return (lane >= begin) & (lane < end)


def strip_start(b, k, width):
    start = width * b - LANES * k
    return start if -width < start < LANES else None


def pack_columns(sent, window, width):
    lane = lane_index()
    begin = (window.shape[2] - sent.shape[1]) // 2
    for r in range(0, sent.shape[1], 8):
        for k in range(sent.shape[0]):
            block = jnp.zeros((8, LANES), jnp.float32)
            for b in range(8):
                start = strip_start(b, k, width)
                if start is not None:
                    c, p, half = b // 4, b // 2 % 2, b % 2
                    rows = window[c, p, begin + r : begin + r + 8, :]
                    own = 64 * half + (64 - width) // 2
                    block = jnp.where(between(lane, start, start + width), roll(rows, start - own, 1), block)
            sent[k, r : r + 8, :] = block


def unpack_columns(sent, window, width):
    lane = lane_index()
    begin = (window.shape[2] - sent.shape[1]) // 2
    for r in range(0, sent.shape[1], 8):
        for c in range(2):
            for p in range(2):
                halves = []
                for half in range(2):
                    own = 64 * half + (64 - width) // 2
                    value = None
                    for k in range(sent.shape[0]):
                        start = strip_start(4 * c + 2 * p + half, k, width)
                        if start is not None:
                            part = roll(sent[k, r : r + 8, :], own - start, 1)
                            value = part if value is None else jnp.where(lane < own - start, value, part)
                    halves.append(value)
                window[c, p, begin + r : begin + r + 8, :] = jnp.where(lane < 64, halves[0], halves[1])


def early_first_kernel(me, windows, rates, starts, coarse_ends, sent, coefs, window):
    @pl.when(me[0] < GROUP)
    def _():
        save_coefs(coefs, rates, (1,))
        save_state(starts.at[1], load_window(windows.at[0]))
        sweep(1, windows, coefs, starts, coarse_ends)
        save_window(window, load_state(starts.at[GROUP]))
        pack_columns(sent, window, COLUMNS_ONE)


def early_second_kernel(me, starts, coarse_ends, rates, ends, sent, coefs, terms, current, rows, window):
    @pl.when(me[0] < GROUP)
    def _():
        save_coefs(coefs, rates, (0, 1))
        put(ends, rows, 0, load_state(starts.at[1]))
        second_terms(1, coefs, starts, coarse_ends, terms)
        state = add(load_state(coarse_ends.at[1]), load_state(terms.at[1]))
        put(ends, rows, 1, state)
        save_state(current, state)
        second_sweep(2, coefs, current, terms, rows, ends)
        save_window(window, load_state(current))
        pack_columns(sent, window, COLUMNS_TWO)


def late_first_kernel(me, windows, rates, received, terms, coefs, starts, coarse_ends, window):
    @pl.when(me[0] >= GROUP)
    def _():
        save_coefs(coefs, rates, (0, 1))
        unpack_columns(received, window, COLUMNS_ONE)
        save_state(starts.at[0], load_window(window))
        sweep(0, windows, coefs, starts, coarse_ends)
        second_terms(0, coefs, starts, coarse_ends, terms)


def late_second_kernel(terms, rates, received, ends, coefs, current, rows, window):
    save_coefs(coefs, rates, (1,))
    window[...] = jnp.zeros_like(window)
    unpack_columns(received, window, COLUMNS_TWO)
    save_state(current, load_window(window))
    second_sweep(0, coefs, current, terms, rows, ends)


def merge_kernel(me, parts, out):
    lane = lane_index()
    early = me[0] < GROUP
    workers = [jnp.where(early, sub, GROUP - 1 - sub) for sub in range(GROUP)]
    for c in range(2):
        for r in range(ROWS // 8):
            rows = slice(8 * r, 8 * r + 8)
            strips = [parts[workers[sub], c, rows, :] for sub in range(GROUP)]
            for x in range(4):
                blocks = [roll(strips[sub], SUB * (sub - x), 1) for sub in range(GROUP)]
                low = jnp.where(lane < 32, blocks[0], blocks[1])
                high = jnp.where(lane < 96, blocks[2], blocks[3])
                out[c, x, rows, :] = jnp.where(lane < 64, low, high)


def call(kernel, shapes, scratch=(), scalars=0):
    vmem = pl.BlockSpec(memory_space=pltpu.VMEM)
    smem = pl.BlockSpec(memory_space=pltpu.SMEM)

    def run(*args):
        return pl.pallas_call(
            kernel,
            out_shape=[jax.ShapeDtypeStruct(s, jnp.float32) for s in shapes],
            in_specs=[smem] * scalars + [vmem] * (len(args) - scalars),
            out_specs=[vmem] * len(shapes),
            scratch_shapes=list(scratch),
            compiler_params=pltpu.CompilerParams(vmem_limit_bytes=32 * 1024 * 1024),
        )(*args)

    return run


def swap(block, axis, begin):
    count = lax.axis_size(axis)
    route = []
    for i in range(begin, begin + count, 2):
        a, b = i % count, (i + 1) % count
        route += [(a, b), (b, a)]
    return lax.ppermute(block, axis, route)


def edge(blocks, begin):
    return jnp.stack([lax.dynamic_slice_in_dim(block, begin, HALO, 2) for block in blocks])


def per_device(iterate, rates):
    state = iterate[0]
    slice_index = GROUP * lax.axis_index("th") + lax.axis_index("tl")
    gy, gz = lax.axis_index("gy"), lax.axis_index("gz")
    me = jnp.stack([slice_index, gy, gz]).astype(jnp.int32)
    odd = gy % 2
    two = edge((state, rates), odd * (ROWS - HALO))
    one = edge((state, rates), (1 - odd) * (ROWS - HALO))
    y_two = swap(two, "gy", 1)
    y_one = swap(one, "gy", 0)
    strip = (2, EXT, LANES)
    own = (2, ROWS, LANES)
    own_two, own_one = call(own_strips_kernel, [own, own], scalars=1)(me, state, rates)
    two, one = call(strips_kernel, [strip, strip], scalars=1)(me, own_two, own_one, y_two, y_one)
    z_two = swap(two, "gz", 1)
    z_one = swap(one, "gz", 0)
    tile_state = pltpu.VMEM((2, 4, TILES, 8, LANES), jnp.float32)
    early_windows, late_windows, rates_here = call(
        first_kernel,
        [(GROUP, 2, 2, WIN, LANES), (GROUP, 2, 2, LATE_WIN, LANES), (2, 2, WIN, LANES)],
        scratch=[
            pltpu.VMEM((2, 2, 4, EXT, LANES), jnp.float32),
            pltpu.VMEM((2, 2, 4, EXT, LANES), jnp.float32),
            pltpu.VMEM((3, 4, TILES, 8, LANES), jnp.float32),
            tile_state,
            tile_state,
            tile_state,
        ],
        scalars=1,
    )(me, state, rates, y_two, y_one, z_two, z_one)

    def exchange(block):
        return lax.all_to_all(block, "tl", 0, 0)

    def leave(block):
        return block

    early = slice_index < GROUP
    last = 2 * GROUP - 1
    route = [(t, last - t) for t in range(GROUP)]

    def hand_over(block):
        return lax.ppermute(block, ("th", "tl"), route)

    def states_of(rows):
        return (2, 2, rows // 8, 8, LANES)

    def scratch_of(rows):
        coefs = pltpu.VMEM((2, 3, *states_of(rows)[1:]), jnp.float32)
        current = pltpu.VMEM(states_of(rows), jnp.float32)
        flat = pltpu.VMEM((2, rows, LANES), jnp.float32)
        window = pltpu.VMEM((2, 2, rows, LANES), jnp.float32)
        return coefs, current, flat, window

    coefs, current, flat, window = scratch_of(WIN)
    starts_shape, slices_shape = (GROUP + 1, *states_of(WIN)), (GROUP, *states_of(WIN))
    ends_shape = (GROUP, 2, ROWS, LANES)
    windows = lax.cond(early, exchange, leave, early_windows)
    starts, coarse_ends, sent = call(
        early_first_kernel,
        [starts_shape, slices_shape, (3, LATE_WIN, LANES)],
        scratch=[coefs, window],
        scalars=1,
    )(me, windows, rates_here)
    received_one = hand_over(sent)
    ends, sent = call(
        early_second_kernel,
        [ends_shape, (3, SENT_TWO, LANES)],
        scratch=[coefs, pltpu.VMEM(slices_shape, jnp.float32), current, flat, window],
        scalars=1,
    )(me, starts, coarse_ends, rates_here)
    received_two = hand_over(sent)

    ends, late_windows = lax.optimization_barrier((ends, late_windows))
    ends = lax.cond(early, exchange, leave, ends)
    windows = lax.cond(early, leave, exchange, late_windows)
    coefs, current, flat, window = scratch_of(LATE_WIN)
    starts_shape, slices_shape = (GROUP + 1, *states_of(LATE_WIN)), (GROUP, *states_of(LATE_WIN))
    (terms,) = call(
        late_first_kernel,
        [slices_shape],
        scratch=[coefs, pltpu.VMEM(starts_shape, jnp.float32), pltpu.VMEM(slices_shape, jnp.float32), window],
        scalars=1,
    )(me, windows, rates_here, received_one)

    def end_late(parts, terms, received):
        scratch = [coefs, current, flat, window]
        (ends,) = call(late_second_kernel, [ends_shape], scratch=scratch)(terms, rates_here, received)
        return exchange(ends)

    ends = lax.cond(early, lambda parts, terms, received: parts, end_late, ends, terms, received_two)
    (out,) = call(merge_kernel, [(2, 4, ROWS, LANES)], scalars=1)(me, ends)
    return out[None]


def solution(mesh):
    shape = mesh.devices.shape
    split = Mesh(mesh.devices.reshape(shape[0] // GROUP, GROUP, *shape[1:]), ("th", "tl", "gy", "gz"))
    return jax.shard_map(
        per_device,
        mesh=split,
        in_specs=(P(("th", "tl"), None, None, "gy", "gz"), P(None, None, "gy", "gz")),
        out_specs=P(("th", "tl"), None, None, "gy", "gz"),
        check_vma=False,
    )
```
